32 devices in a mesh: rows: 16 (over z, y, core), ch: 2 (over x).
Axes of the slice: x: 2, y: 2, z: 4, core: 2. Of those that a mesh axis runs over, the one named last changes fastest.
Arguments:
- inputs: bfloat16 [32, 1024, 2048], P('rows', None, 'ch'), may hold values from -6 to 6
- doc_lengths: int32 [32, 8], P('rows'), may hold values from 1 to 512, 1024 in all within a row
- layer_norm_gain: float32 [2048], P('ch'), may hold values from 0.5 to 1.5
- layer_norm_bias: float32 [2048], P('ch'), may hold values from -3 to 3
- weight: bfloat16 [2048, 3, 2048], P(None, None, 'ch'), may hold values from -0.125 to 0.125
- forget_weight: float32 [2048], P('ch'), may hold values from -1 to 1
- reset_weight: float32 [2048], P('ch'), may hold values from -1 to 1
- forget_bias: float32 [2048], P('ch'), may hold values from 0 to 4
- reset_bias: float32 [2048], P('ch'), may hold values from -1 to 1
- out_grad: bfloat16 [32, 1024, 2048], P('rows', None, 'ch'), may hold values from -6 to 6
Outputs:
- mixed: bfloat16 [32, 1024, 2048], P('rows', None, 'ch')
- input_grad: bfloat16 [32, 1024, 2048], P('rows', None, 'ch')
- final_state: float32 [32, 2048], P('rows', 'ch')
- weight_grad: float32 [2048, 3, 2048], P(None, None, 'ch')
- gain_grad: float32 [2048], P('ch')
- shift_grad: float32 [2048], P('ch')
- forget_weight_grad: float32 [2048], P('ch')
- reset_weight_grad: float32 [2048], P('ch')
- forget_bias_grad: float32 [2048], P('ch')
- reset_bias_grad: float32 [2048], P('ch')
The draws below stay inside these ranges and needn't reach their ends.
Inputs may be any that keep to these rules, and one draw needn't show every extreme that they name: `doc_lengths`: each row's 8 lengths sum to 1024, and the longest document of every row has exactly 512 tokens.
All inputs are finite; a program needn't handle non-finite values.
Results may differ from the reference program's by a relative error of at most 0.0091.
Values may be sent and summed in bfloat16 or wider, within the bound.
A program may use at most 320 MiB of HBM per device.

```python
import math
import jax
import jax.numpy as jnp
import numpy as np
from jax import lax

H = 2048
ROW_LEN = 1024
DOCS = 8
ROWS_DEV = 2
MOST_DOC = 512
ROWS = 32


def shard_levels(key, shape, split, least, top_value):
    def one(axis_at, shards_of):
        heights = jax.random.uniform(jax.random.fold_in(jax.random.fold_in(key, 6), axis_at), (shards_of,), jnp.float32, least / len(split), top_value / len(split))
        return jnp.repeat(jnp.exp(heights), shape[axis_at] // shards_of).reshape((-1,) + (1,) * (len(shape) - axis_at - 1))

    level = one(*split[0])
    for cut in split[1:]:
        level = level * one(*cut)
    return level


def split_up(count, total, bound, skew):
    loads = [(1 << 20) // math.isqrt(rank ** skew) + 1 for rank in range(2, count + 1)]
    rest, holding = total - bound - (count - 1), [1] * (count - 1)
    while rest > 0:
        free = [i for i in range(count - 1) if holding[i] < bound]
        pool, remaining = sum([loads[i] for i in free]), rest
        for i in free:
            extra = min(bound - holding[i], max(1, remaining * loads[i] // pool), rest)
            holding[i] = holding[i] + extra
            rest = rest - extra
    return np.array([bound] + holding)


def uneven_parts(key, amount, total, reach, lean):
    if amount == 2:
        one = jax.random.randint(key, (), max(1, total - reach), min(reach, total - 1) + 1)
        return jnp.stack([one, total - one])
    sizes = jnp.asarray(split_up(amount, total, reach, lean), jnp.int32)
    twos = (amount - 1) // 2
    giver, sink = sizes[1:1 + 2 * twos:2], sizes[2:2 + 2 * twos:2]
    margin = jnp.minimum(giver - 1, reach - sink)
    moved = jax.random.randint(jax.random.fold_in(key, 1), (twos,), 0, 1 << 20) % (margin + 1)
    sizes = sizes.at[1:1 + 2 * twos:2].set(giver - moved).at[2:2 + 2 * twos:2].set(sink + moved)
    return sizes[jax.random.permutation(jax.random.fold_in(key, 2), amount)]


def noise(stream_key, shape, width, bound, split=(), kind=jnp.bfloat16):
    loudness = shard_levels(stream_key, shape, split, -0.22, 0.18) if split else 1.0
    drawn = jax.random.normal(stream_key, shape, jnp.float32) * width * loudness
    return jnp.minimum(jnp.maximum(drawn, -bound), bound).astype(kind)


def setup_inputs(seed: int = 0) -> dict:
    streams_of = jax.random.split(jax.random.key(seed), 11)
    inputs = noise(streams_of[0], (ROWS, ROW_LEN, H), 1.0, 6.0, ((0, 16), (2, 2)))
    doc_lengths = jax.vmap(lambda own: uneven_parts(own, DOCS, ROW_LEN, MOST_DOC, 2))(jax.random.split(streams_of[1], ROWS)).reshape((ROWS, DOCS)).astype(jnp.int32)
    layer_norm_gain = jnp.clip(1.0 + 0.1 * jax.random.normal(streams_of[2], (H,), jnp.float32), 0.5, 1.5)
    layer_norm_bias = noise(streams_of[3], (H,), 0.5, 3.0, ((0, 2),), jnp.float32)
    weight = noise(streams_of[4], (H, 3, H), H ** -0.5, 0.125, ((2, 2),))
    forget_weight = jnp.clip(jax.random.uniform(streams_of[5], (H,), jnp.float32, -1.0, 1.0) * shard_levels(streams_of[5], (H,), ((0, 2),), -0.4, 0.0), -1.0, 1.0)
    reset_weight = jnp.clip(jax.random.uniform(streams_of[6], (H,), jnp.float32, -1.0, 1.0) * shard_levels(streams_of[6], (H,), ((0, 2),), -0.4, 0.0), -1.0, 1.0)
    forget_bias = jnp.clip(4.0 * jax.random.uniform(streams_of[7], (H,), jnp.float32) ** shard_levels(streams_of[7], (H,), ((0, 2),), -0.2, 0.2), 0.0, 4.0)
    reset_bias = jnp.clip(jax.random.uniform(streams_of[8], (H,), jnp.float32, -1.0, 1.0) * shard_levels(streams_of[8], (H,), ((0, 2),), -0.4, 0.0), -1.0, 1.0)
    out_grad = noise(streams_of[9], (ROWS, ROW_LEN, H), 1.0, 6.0, ((0, 16), (2, 2)))
    return dict(inputs=inputs, doc_lengths=doc_lengths, layer_norm_gain=layer_norm_gain, layer_norm_bias=layer_norm_bias, weight=weight, forget_weight=forget_weight, reset_weight=reset_weight, forget_bias=forget_bias, reset_bias=reset_bias, out_grad=out_grad)


@jax.custom_vjp
def low(v):
    return lax.optimization_barrier(v.astype(jnp.bfloat16)).astype(jnp.float32)

@jax.custom_vjp
def low_back(v):
    return v

def low_keep(v):
    return (low(v), None)

def low_pass(kept, grad):
    return (grad,)

def back_keep(v):
    return (v, None)

def back_low(kept, grad):
    return (low(grad),)
low.defvjp(low_keep, low_pass)
low_back.defvjp(back_keep, back_low)
epsilon = 1e-05
highest = lax.Precision.HIGHEST

def keep_masks(doc_lengths, length):
    starts = jnp.cumsum(doc_lengths, axis=-1).astype(jnp.int32) - doc_lengths
    places = jnp.arange(length, dtype=jnp.int32)
    hits = (places[None, :, None] == starts[:, None, :]).astype(jnp.float32)
    return 1.0 - lax.optimization_barrier(jnp.sum(hits, axis=-1))

def group_forward(source_rows_input, keep_mask, layer_norm_gain, layer_norm_bias, weight, forget_weight, reset_weight, forget_bias, reset_bias):
    row_average_value = lax.optimization_barrier(jnp.mean(source_rows_input, axis=-1, keepdims=True))
    centered = source_rows_input - row_average_value
    row_var = lax.optimization_barrier(jnp.mean(centered * centered, axis=-1, keepdims=True))
    normed = low(centered * lax.rsqrt(row_var + epsilon) * layer_norm_gain + layer_norm_bias)
    projected = low_back(jnp.einsum('glh,hak->lgak', normed, weight, precision=highest))
    keep_time = jnp.transpose(keep_mask, (1, 0))

    def advance(state_now, inputs):
        up_x, up_f, keep_now = inputs
        previous = state_now * keep_now[:, None]
        forget = jax.nn.sigmoid(up_f + forget_weight * previous + forget_bias)
        state_new = forget * previous + (1.0 - forget) * up_x
        return (state_new, (state_new, previous))
    start_state = jnp.zeros((source_rows_input.shape[0], source_rows_input.shape[2]), jnp.float32)
    last_state, (states, previous) = lax.scan(jax.checkpoint(advance), start_state, (projected[:, :, 0], projected[:, :, 1], keep_time))
    reset_gate = jax.nn.sigmoid(projected[:, :, 2] + reset_weight * previous + reset_bias)
    source_time = jnp.transpose(source_rows_input, (1, 0, 2))
    highway = reset_gate * states + (1.0 - reset_gate) * source_time
    return (jnp.transpose(highway, (1, 0, 2)), last_state)

def reference(inputs, doc_lengths, layer_norm_gain, layer_norm_bias, weight, forget_weight, reset_weight, forget_bias, reset_bias, out_grad):
    groups = ROWS // ROWS_DEV
    keep_all = keep_masks(doc_lengths, ROW_LEN).reshape(groups, ROWS_DEV, ROW_LEN)
    source_rows_input = inputs.astype(jnp.float32).reshape(groups, ROWS_DEV, ROW_LEN, H)

    def whole(source_rows_input, gain_in, shift_in, weight_in, forget_w, reset_w, forget_b, reset_b):

        def one_group(paired):
            return jax.checkpoint(group_forward)(paired[0], paired[1], gain_in, shift_in, weight_in, forget_w, reset_w, forget_b, reset_b)
        highway, finals = lax.map(one_group, (source_rows_input, keep_all))
        return (highway, finals)
    highway, pullback, finals = jax.vjp(whole, source_rows_input, layer_norm_gain, layer_norm_bias, weight.astype(jnp.float32), forget_weight, reset_weight, forget_bias, reset_bias, has_aux=True)
    grads = pullback(out_grad.astype(jnp.float32).reshape(groups, ROWS_DEV, ROW_LEN, H))
    mixed = highway.reshape(ROWS, ROW_LEN, H).astype(jnp.bfloat16)
    input_grad = grads[0].reshape(ROWS, ROW_LEN, H).astype(jnp.bfloat16)
    return (mixed, input_grad, finals.reshape(ROWS, H), grads[3], grads[1], grads[2], grads[4], grads[5], grads[6], grads[7])
```

```python
import functools

import jax
import jax.numpy as jnp
from jax import lax
from jax.experimental import pallas as pl
from jax.experimental.pallas import tpu as pltpu
from jax.sharding import PartitionSpec as P

MESH = pl.DeviceIdType.MESH
F32 = jnp.float32
BF16 = jnp.bfloat16
EPSILON = 1e-05
LANES = 128
SUBLANES = 8
PROJECT_TOKENS = 128
RECUR_TOKENS = 64
GROUP = 16
ANY = pl.BlockSpec(memory_space=pl.ANY)
VMEM_LIMIT = 60 * 1024 * 1024


def project_kernel(
    x_ref, params_ref, weight_ref,
    u_ref, normed_t_ref, mean_ref, scale_ref,
    both, weights, params, normed, normed_t, mean_out, scale_out, u_out,
    send_sem, recv_sem, own_sem, param_sem, weight_sem, u_sem, t_sem, stat_sem,
):
    ch = lax.axis_index("ch")
    other = 1 - ch
    tokens, width = x_ref.shape
    full = 2 * width
    size = PROJECT_TOKENS
    chunks = tokens // size
    own_columns = pl.ds(pl.multiple_of(ch * width, width), width)

    load_weight = pltpu.make_async_copy(weight_ref, weights, weight_sem)
    load_weight.start()
    own_params = pltpu.make_async_copy(params_ref, params.at[ch], param_sem.at[0])
    own_params.start()

    barrier = pltpu.get_barrier_semaphore()
    pl.semaphore_signal(barrier, inc=1, device_id={"ch": other}, device_id_type=MESH)
    pl.semaphore_wait(barrier, 1)

    send_params = pltpu.make_async_remote_copy(
        src_ref=params_ref, dst_ref=params.at[ch], send_sem=param_sem.at[1], recv_sem=param_sem.at[2],
        device_id={"ch": other}, device_id_type=MESH,
    )
    send_params.start()

    def exchange(chunk):
        rows = pl.ds(pl.multiple_of(chunk * size, size), size)
        return pltpu.make_async_remote_copy(
            src_ref=x_ref.at[rows], dst_ref=both.at[rows, own_columns],
            send_sem=send_sem.at[chunk], recv_sem=recv_sem.at[chunk],
            device_id={"ch": other}, device_id_type=MESH,
        )

    def keep_own(chunk):
        rows = pl.ds(pl.multiple_of(chunk * size, size), size)
        return pltpu.make_async_copy(x_ref.at[rows], both.at[rows, own_columns], own_sem.at[chunk])

    def outputs(chunk, slot):
        rows = pl.ds(pl.multiple_of(chunk * size, size), size)
        return (
            pltpu.make_async_copy(u_out.at[slot], u_ref.at[:, rows], u_sem.at[slot]),
            pltpu.make_async_copy(normed_t.at[slot], normed_t_ref.at[:, rows], t_sem.at[slot]),
            pltpu.make_async_copy(mean_out.at[slot], mean_ref.at[rows], stat_sem.at[0, slot]),
            pltpu.make_async_copy(scale_out.at[slot], scale_ref.at[rows], stat_sem.at[1, slot]),
        )

    def begin(chunk, carry):
        exchange(chunk).start()
        keep_own(chunk).start()
        return carry

    lax.fori_loop(0, chunks, begin, 0)
    own_params.wait()
    send_params.wait()
    load_weight.wait()
    gain = jnp.concatenate([params[0, 0:1], params[1, 0:1]], axis=1)
    shift = jnp.concatenate([params[0, 1:2], params[1, 1:2]], axis=1)

    def work(chunk, carry):
        slot = lax.rem(chunk, 2)
        keep_own(chunk).wait()
        exchange(chunk).wait()

        @pl.when(chunk >= 2)
        def _():
            for copy in outputs(chunk - 2, slot):
                copy.wait()

        @pl.loop(0, size // GROUP)
        def _(part):
            rows = pl.ds(pl.multiple_of(chunk * size + part * GROUP, GROUP), GROUP)
            here = pl.ds(pl.multiple_of(part * GROUP, GROUP), GROUP)
            x = both[rows, :].astype(F32)
            mean = jnp.sum(x, axis=1, keepdims=True) * (1.0 / full)
            centered = x - mean
            variance = jnp.sum(centered * centered, axis=1, keepdims=True) * (1.0 / full)
            scale = lax.rsqrt(variance + EPSILON)
            normed[here, :] = (centered * scale * gain + shift).astype(BF16)
            mean_out[slot, here, :] = jnp.broadcast_to(mean, (GROUP, LANES))
            scale_out[slot, here, :] = jnp.broadcast_to(scale, (GROUP, LANES))

        for gate in range(3):
            u_out[slot, gate] = jnp.dot(normed[...], weights[gate], preferred_element_type=F32)

        @pl.loop(0, full // LANES)
        def _(part):
            columns = pl.ds(pl.multiple_of(part * LANES, LANES), LANES)
            normed_t[slot, columns, :] = normed[:, columns].T

        for copy in outputs(chunk, slot):
            copy.start()
        return carry

    lax.fori_loop(0, chunks, work, 0)
    for chunk in (chunks - 2, chunks - 1):
        for copy in outputs(chunk, chunk % 2):
            copy.wait()


def project(x, params, weight):
    tokens, width = x.shape
    full = 2 * width
    size = PROJECT_TOKENS
    chunks = tokens // size
    dma = pltpu.SemaphoreType.DMA
    return pl.pallas_call(
        project_kernel,
        out_shape=(
            jax.ShapeDtypeStruct((3, tokens, width), F32),
            jax.ShapeDtypeStruct((full, tokens), BF16),
            jax.ShapeDtypeStruct((tokens, LANES), F32),
            jax.ShapeDtypeStruct((tokens, LANES), F32),
        ),
        in_specs=[ANY] * 3,
        out_specs=[ANY] * 4,
        scratch_shapes=[
            pltpu.VMEM((tokens, full), BF16),
            pltpu.VMEM((3, full, width), BF16),
            pltpu.VMEM((2, SUBLANES, width), F32),
            pltpu.VMEM((size, full), BF16),
            pltpu.VMEM((2, full, size), BF16),
            pltpu.VMEM((2, size, LANES), F32),
            pltpu.VMEM((2, size, LANES), F32),
            pltpu.VMEM((2, 3, size, width), F32),
            dma((chunks,)), dma((chunks,)), dma((chunks,)), dma((3,)), dma, dma((2,)), dma((2,)), dma((2, 2)),
        ],
        compiler_params=pltpu.CompilerParams(
            collective_id=0, has_side_effects=True, vmem_limit_bytes=VMEM_LIMIT
        ),
        name="project",
    )(x, params, weight)


def recur_kernel(
    keep_ref, u_ref, x_ref, grad_ref, params_ref,
    mixed_ref, pass_ref, reset_ref, gates_ref, final_ref, sums_ref,
    direct_s, extra_s, forget_s, slope_s, before_s, state_s, sums_s,
):
    step = pl.program_id(0)
    rows_here, size = x_ref.shape[0], x_ref.shape[1]
    blocks = pl.num_programs(0) // 2
    width = x_ref.shape[2]
    block_forward = step
    block_back = 2 * blocks - 1 - step
    forget_weight = params_ref[0]
    reset_weight = params_ref[1]
    forget_bias = params_ref[2]
    reset_bias = params_ref[3]
    half_forget_weight = 0.5 * forget_weight
    half_reset_weight = 0.5 * reset_weight
    half_forget_bias = 0.5 * forget_bias
    half_reset_bias = 0.5 * reset_bias

    def spread(value):
        return value.astype(F32).reshape(GROUP, SUBLANES, LANES)

    def flat(parts):
        return jnp.stack(parts).reshape(GROUP, width).astype(BF16)

    @pl.when(step == 0)
    def _():
        state_s[...] = jnp.zeros_like(state_s)
        sums_s[...] = jnp.zeros_like(sums_s)

    @pl.when(step < blocks)
    def _():
        def group(index, carry):
            here = pl.ds(pl.multiple_of(index * GROUP, GROUP), GROUP)
            state = list(carry[:rows_here])
            weight_sum, bias_sum = carry[rows_here:]
            loaded = []
            for row in range(rows_here):
                loaded.append((
                    u_ref[0, row, here].reshape(GROUP, SUBLANES, LANES),
                    u_ref[1, row, here].reshape(GROUP, SUBLANES, LANES),
                    u_ref[2, row, here].reshape(GROUP, SUBLANES, LANES),
                    spread(x_ref[row, here]),
                    spread(grad_ref[row, here]),
                ))
            out = [([], [], []) for _ in range(rows_here)]
            for k in range(GROUP):
                time = block_forward * size + index * GROUP + k
                for row in range(rows_here):
                    up_x, up_f, up_r, x, grad = (part[k] for part in loaded[row])
                    before = state[row] * keep_ref[row, time]
                    bent = jnp.tanh(0.5 * up_f + half_forget_bias + half_forget_weight * before)
                    gap = before - up_x
                    after = 0.5 * (before + up_x) + bent * (0.5 * gap)
                    state[row] = after
                    forget = 0.5 * bent + 0.5
                    reset = 0.5 * jnp.tanh(0.5 * up_r + half_reset_bias + half_reset_weight * before) + 0.5
                    over = after - x
                    direct = grad * reset
                    reset_grad = direct * over * (1.0 - reset)
                    direct_s[row, time] = direct
                    extra_s[row, time] = reset_grad * reset_weight
                    forget_s[row, time] = forget
                    slope_s[row, time] = gap * forget * (1.0 - forget)
                    before_s[row, time] = before
                    weight_sum = weight_sum + reset_grad * before
                    bias_sum = bias_sum + reset_grad
                    out[row][0].append(x + reset * over)
                    out[row][1].append(grad - direct)
                    out[row][2].append(reset_grad)
            for row in range(rows_here):
                mixed_ref[row, here] = flat(out[row][0])
                pass_ref[row, here] = flat(out[row][1])
                reset_ref[row, here] = flat(out[row][2])
            return (*state, weight_sum, bias_sum)

        carry = lax.fori_loop(
            0, size // GROUP, group, (*[state_s[row] for row in range(rows_here)], sums_s[1], sums_s[3])
        )
        for row in range(rows_here):
            state_s[row] = carry[row]
        sums_s[1] = carry[rows_here]
        sums_s[3] = carry[rows_here + 1]

    @pl.when(step == blocks - 1)
    def _():
        final_ref[...] = state_s[...]
        state_s[...] = jnp.zeros_like(state_s)

    @pl.when(step >= blocks)
    def _():
        def group(turn, carry):
            index = size // GROUP - 1 - turn
            here = pl.ds(pl.multiple_of(index * GROUP, GROUP), GROUP)
            running = list(carry[:rows_here])
            weight_sum, bias_sum = carry[rows_here:]
            out = [([None] * GROUP, [None] * GROUP) for _ in range(rows_here)]
            for k in range(GROUP - 1, -1, -1):
                time = block_back * size + index * GROUP + k
                for row in range(rows_here):
                    forget = forget_s[row, time]
                    slope = slope_s[row, time]
                    keep = keep_ref[row, time]
                    state_grad = direct_s[row, time] + running[row]
                    through = (forget + slope * forget_weight) * keep
                    running[row] = through * state_grad + extra_s[row, time] * keep
                    forget_grad = state_grad * slope
                    weight_sum = weight_sum + forget_grad * before_s[row, time]
                    bias_sum = bias_sum + forget_grad
                    out[row][0][k] = state_grad - state_grad * forget
                    out[row][1][k] = forget_grad
            for row in range(rows_here):
                gates_ref[0, row, here] = flat(out[row][0])
                gates_ref[1, row, here] = flat(out[row][1])
            return (*running, weight_sum, bias_sum)

        carry = lax.fori_loop(
            0, size // GROUP, group, (*[state_s[row] for row in range(rows_here)], sums_s[0], sums_s[2])
        )
        for row in range(rows_here):
            state_s[row] = carry[row]
        sums_s[0] = carry[rows_here]
        sums_s[2] = carry[rows_here + 1]

    @pl.when(step == 2 * blocks - 1)
    def _():
        sums_ref[...] = sums_s[...]


def recur(keep, u, x, grad, params):
    rows_here, length, width = x.shape
    size = RECUR_TOKENS
    blocks = length // size
    ahead = lambda i: jnp.minimum(i, blocks - 1)
    back = lambda i: jnp.minimum(2 * blocks - 1 - i, blocks - 1)
    row_block = lambda place: pl.BlockSpec((rows_here, size, width), lambda i: (0, place(i), 0))
    whole = lambda *shape: pl.BlockSpec(shape, lambda i: (0,) * len(shape))
    tile = (SUBLANES, LANES)
    kept = pltpu.VMEM((rows_here, length) + tile, F32)
    return pl.pallas_call(
        recur_kernel,
        grid=(2 * blocks,),
        out_shape=(
            jax.ShapeDtypeStruct((rows_here, length, width), BF16),
            jax.ShapeDtypeStruct((rows_here, length, width), BF16),
            jax.ShapeDtypeStruct((rows_here, length, width), BF16),
            jax.ShapeDtypeStruct((2, rows_here, length, width), BF16),
            jax.ShapeDtypeStruct((rows_here,) + tile, F32),
            jax.ShapeDtypeStruct((4,) + tile, F32),
        ),
        in_specs=[
            pl.BlockSpec(memory_space=pltpu.SMEM),
            pl.BlockSpec((3, rows_here, size, width), lambda i: (0, 0, ahead(i), 0)),
            row_block(ahead), row_block(ahead), whole(4, *tile),
        ],
        out_specs=(
            row_block(ahead), row_block(ahead), row_block(ahead),
            pl.BlockSpec((2, rows_here, size, width), lambda i: (0, 0, back(i), 0)),
            whole(rows_here, *tile), whole(4, *tile),
        ),
        scratch_shapes=[kept] * 5 + [pltpu.VMEM((rows_here,) + tile, F32), pltpu.VMEM((4,) + tile, F32)],
        compiler_params=pltpu.CompilerParams(vmem_limit_bytes=VMEM_LIMIT),
        name="recur",
    )(keep, u, x, grad, params)


def on_device(
    inputs, doc_lengths, layer_norm_gain, layer_norm_bias, weight, forget_weight, reset_weight, forget_bias,
    reset_bias, out_grad,
):
    rows_here, length, width = inputs.shape
    full = width * lax.axis_size("ch")
    tokens = rows_here * length
    tile = (SUBLANES, LANES)
    weights = jnp.transpose(weight, (1, 0, 2))
    norm_params = jnp.zeros((SUBLANES, width), F32).at[0].set(layer_norm_gain).at[1].set(layer_norm_bias)
    x = inputs.reshape(tokens, width)
    u, normed_t, mean, scale = project(x, norm_params, weights)

    starts = jnp.cumsum(doc_lengths, axis=-1) - doc_lengths
    places = jnp.arange(length, dtype=jnp.int32)
    hits = (places[None, :, None] == starts[:, None, :]).astype(F32)
    keep = 1.0 - jnp.sum(hits, axis=-1)
    gate_params = jnp.stack([forget_weight, reset_weight, forget_bias, reset_bias]).reshape((4,) + tile)
    mixed, passed, reset_grad, gate_grads, final_state, sums = recur(
        keep, u.reshape(3, rows_here, length, width), inputs, out_grad, gate_params
    )
    final_state = final_state.reshape(rows_here, width)
    sums = sums.reshape(4, width)

    du = jnp.concatenate([gate_grads.reshape(2, tokens, width), reset_grad.reshape(1, tokens, width)])
    weight_part = jnp.einsum("it,ato->aio", normed_t, du, preferred_element_type=F32).astype(BF16)
    dn = jnp.einsum("ato,aio->ti", du, weights, preferred_element_type=F32)
    me = lax.axis_index("ch")
    mine = lax.dynamic_slice_in_dim(dn, me * width, width, 1)
    theirs = lax.dynamic_slice_in_dim(dn, (1 - me) * width, width, 1).astype(BF16)
    dn = mine + lax.ppermute(theirs, "ch", [(0, 1), (1, 0)]).astype(F32)
    scale = scale[:, :1]
    xhat = (x.astype(F32) - mean[:, :1]) * scale
    gain_part = jnp.sum(dn * xhat, axis=0)
    shift_part = jnp.sum(dn, axis=0)
    dxhat = dn * layer_norm_gain
    first, second = lax.psum((jnp.sum(dxhat, axis=1), jnp.sum(dxhat * xhat, axis=1)), "ch")
    back = scale * (dxhat - first[:, None] / full - xhat * second[:, None] / full)
    input_grad = (back.reshape(rows_here, length, width) + passed.astype(F32)).astype(BF16)
    summed = lax.psum(jnp.concatenate([sums, gain_part[None], shift_part[None]]), "rows")
    weight_grad = lax.psum(weight_part, "rows").astype(F32)
    weight_grad = jnp.transpose(weight_grad, (1, 0, 2))
    return (
        mixed, input_grad, final_state, weight_grad, summed[4], summed[5], summed[0], summed[1], summed[2], summed[3],
    )


def solution(mesh):
    rows_ch = P("rows", None, "ch")
    ch = P("ch")
    in_specs = (rows_ch, P("rows", None), ch, ch, P(None, None, "ch"), ch, ch, ch, ch, rows_ch)
    out_specs = (rows_ch, rows_ch, P("rows", "ch"), P(None, None, "ch"), ch, ch, ch, ch, ch, ch)
    return jax.shard_map(on_device, mesh=mesh, in_specs=in_specs, out_specs=out_specs, check_vma=False)
```

```python
import functools

import jax
import jax.numpy as jnp
from jax import lax
from jax.experimental import pallas as pl
from jax.experimental.pallas import tpu as pltpu
from jax.sharding import PartitionSpec as P

MESH = pl.DeviceIdType.MESH
F32 = jnp.float32
BF16 = jnp.bfloat16
EPSILON = 1e-05
LANES = 128
SUBLANES = 8
PROJECT_TOKENS = 128
RECUR_TOKENS = 64
GROUP = 16
ANY = pl.BlockSpec(memory_space=pl.ANY)
VMEM_LIMIT = 60 * 1024 * 1024


def project_kernel(
    x_ref, params_ref, weight_ref,
    u_ref, normed_t_ref, mean_ref, scale_ref,
    both, weights, params, normed, normed_t, mean_out, scale_out, u_out,
    send_sem, recv_sem, own_sem, param_sem, weight_sem, u_sem, t_sem, stat_sem,
):
    ch = lax.axis_index("ch")
    other = 1 - ch
    tokens, width = x_ref.shape
    full = 2 * width
    size = PROJECT_TOKENS
    chunks = tokens // size
    own_columns = pl.ds(pl.multiple_of(ch * width, width), width)

    load_weight = pltpu.make_async_copy(weight_ref, weights, weight_sem)
    load_weight.start()
    own_params = pltpu.make_async_copy(params_ref, params.at[ch], param_sem.at[0])
    own_params.start()

    barrier = pltpu.get_barrier_semaphore()
    pl.semaphore_signal(barrier, inc=1, device_id={"ch": other}, device_id_type=MESH)
    pl.semaphore_wait(barrier, 1)

    send_params = pltpu.make_async_remote_copy(
        src_ref=params_ref, dst_ref=params.at[ch], send_sem=param_sem.at[1], recv_sem=param_sem.at[2],
        device_id={"ch": other}, device_id_type=MESH,
    )
    send_params.start()

    def exchange(chunk):
        rows = pl.ds(pl.multiple_of(chunk * size, size), size)
        return pltpu.make_async_remote_copy(
            src_ref=x_ref.at[rows], dst_ref=both.at[rows, own_columns],
            send_sem=send_sem.at[chunk], recv_sem=recv_sem.at[chunk],
            device_id={"ch": other}, device_id_type=MESH,
        )

    def keep_own(chunk):
        rows = pl.ds(pl.multiple_of(chunk * size, size), size)
        return pltpu.make_async_copy(x_ref.at[rows], both.at[rows, own_columns], own_sem.at[chunk])

    def outputs(chunk, slot):
        rows = pl.ds(pl.multiple_of(chunk * size, size), size)
        return (
            pltpu.make_async_copy(u_out.at[slot], u_ref.at[:, rows], u_sem.at[slot]),
            pltpu.make_async_copy(normed_t.at[slot], normed_t_ref.at[:, rows], t_sem.at[slot]),
            pltpu.make_async_copy(mean_out.at[slot], mean_ref.at[rows], stat_sem.at[0, slot]),
            pltpu.make_async_copy(scale_out.at[slot], scale_ref.at[rows], stat_sem.at[1, slot]),
        )

    def begin(chunk, carry):
        exchange(chunk).start()
        keep_own(chunk).start()
        return carry

    lax.fori_loop(0, chunks, begin, 0)
    own_params.wait()
    send_params.wait()
    load_weight.wait()
    gain = jnp.concatenate([params[0, 0:1], params[1, 0:1]], axis=1)
    shift = jnp.concatenate([params[0, 1:2], params[1, 1:2]], axis=1)

    def work(chunk, carry):
        slot = lax.rem(chunk, 2)
        keep_own(chunk).wait()
        exchange(chunk).wait()

        @pl.when(chunk >= 2)
        def _():
            for copy in outputs(chunk - 2, slot):
                copy.wait()

        @pl.loop(0, size // GROUP)
        def _(part):
            rows = pl.ds(pl.multiple_of(chunk * size + part * GROUP, GROUP), GROUP)
            here = pl.ds(pl.multiple_of(part * GROUP, GROUP), GROUP)
            x = both[rows, :].astype(F32)
            mean = jnp.sum(x, axis=1, keepdims=True) * (1.0 / full)
            centered = x - mean
            variance = jnp.sum(centered * centered, axis=1, keepdims=True) * (1.0 / full)
            scale = lax.rsqrt(variance + EPSILON)
            normed[here, :] = (centered * scale * gain + shift).astype(BF16)
            mean_out[slot, here, :] = jnp.broadcast_to(mean, (GROUP, LANES))
            scale_out[slot, here, :] = jnp.broadcast_to(scale, (GROUP, LANES))

        for gate in range(3):
            u_out[slot, gate] = jnp.dot(normed[...], weights[gate], preferred_element_type=F32)

        @pl.loop(0, full // LANES)
        def _(part):
            columns = pl.ds(pl.multiple_of(part * LANES, LANES), LANES)
            normed_t[slot, columns, :] = normed[:, columns].T

        for copy in outputs(chunk, slot):
            copy.start()
        return carry

    lax.fori_loop(0, chunks, work, 0)
    for chunk in (chunks - 2, chunks - 1):
        for copy in outputs(chunk, chunk % 2):
            copy.wait()


def project(x, params, weight):
    tokens, width = x.shape
    full = 2 * width
    size = PROJECT_TOKENS
    chunks = tokens // size
    dma = pltpu.SemaphoreType.DMA
    return pl.pallas_call(
        project_kernel,
        out_shape=(
            jax.ShapeDtypeStruct((3, tokens, width), F32),
            jax.ShapeDtypeStruct((full, tokens), BF16),
            jax.ShapeDtypeStruct((tokens, LANES), F32),
            jax.ShapeDtypeStruct((tokens, LANES), F32),
        ),
        in_specs=[ANY] * 3,
        out_specs=[ANY] * 4,
        scratch_shapes=[
            pltpu.VMEM((tokens, full), BF16),
            pltpu.VMEM((3, full, width), BF16),
            pltpu.VMEM((2, SUBLANES, width), F32),
            pltpu.VMEM((size, full), BF16),
            pltpu.VMEM((2, full, size), BF16),
            pltpu.VMEM((2, size, LANES), F32),
            pltpu.VMEM((2, size, LANES), F32),
            pltpu.VMEM((2, 3, size, width), F32),
            dma((chunks,)), dma((chunks,)), dma((chunks,)), dma((3,)), dma, dma((2,)), dma((2,)), dma((2, 2)),
        ],
        compiler_params=pltpu.CompilerParams(
            collective_id=0, has_side_effects=True, vmem_limit_bytes=VMEM_LIMIT
        ),
        name="project",
    )(x, params, weight)


def recur_kernel(
    keep_ref, u_ref, x_ref, grad_ref, params_ref,
    mixed_ref, pass_ref, reset_ref, gates_ref, final_ref, sums_ref,
    direct_s, extra_s, forget_s, slope_s, before_s, state_s, sums_s,
):
    step = pl.program_id(0)
    rows_here, size = x_ref.shape[0], x_ref.shape[1]
    blocks = pl.num_programs(0) // 2
    width = x_ref.shape[2]
    block_forward = step
    block_back = 2 * blocks - 1 - step
    forget_weight = params_ref[0]
    reset_weight = params_ref[1]
    forget_bias = params_ref[2]
    reset_bias = params_ref[3]
    half_forget_weight = 0.5 * forget_weight
    half_reset_weight = 0.5 * reset_weight
    half_forget_bias = 0.5 * forget_bias
    half_reset_bias = 0.5 * reset_bias

    def spread(value):
        return value.astype(F32).reshape(GROUP, SUBLANES, LANES)

    def flat(parts):
        return jnp.stack(parts).reshape(GROUP, width).astype(BF16)

    @pl.when(step == 0)
    def _():
        state_s[...] = jnp.zeros_like(state_s)
        sums_s[...] = jnp.zeros_like(sums_s)

    @pl.when(step < blocks)
    def _():
        def group(index, carry):
            here = pl.ds(pl.multiple_of(index * GROUP, GROUP), GROUP)
            state = list(carry[:rows_here])
            weight_sum, bias_sum = carry[rows_here:]
            loaded = []
            for row in range(rows_here):
                loaded.append((
                    u_ref[0, row, here].reshape(GROUP, SUBLANES, LANES),
                    u_ref[1, row, here].reshape(GROUP, SUBLANES, LANES),
                    u_ref[2, row, here].reshape(GROUP, SUBLANES, LANES),
                    spread(x_ref[row, here]),
                    spread(grad_ref[row, here]),
                ))
            out = [([], [], []) for _ in range(rows_here)]
            for k in range(GROUP):
                time = block_forward * size + index * GROUP + k
                for row in range(rows_here):
                    up_x, up_f, up_r, x, grad = (part[k] for part in loaded[row])
                    before = state[row] * keep_ref[row, time]
                    bent = jnp.tanh(0.5 * up_f + half_forget_bias + half_forget_weight * before)
                    gap = before - up_x
                    after = 0.5 * (before + up_x) + bent * (0.5 * gap)
                    state[row] = after
                    forget = 0.5 * bent + 0.5
                    reset = 0.5 * jnp.tanh(0.5 * up_r + half_reset_bias + half_reset_weight * before) + 0.5
                    over = after - x
                    direct = grad * reset
                    reset_grad = direct * over * (1.0 - reset)
                    direct_s[row, time] = direct
                    extra_s[row, time] = reset_grad * reset_weight
                    forget_s[row, time] = forget
                    slope_s[row, time] = gap * forget * (1.0 - forget)
                    before_s[row, time] = before
                    weight_sum = weight_sum + reset_grad * before
                    bias_sum = bias_sum + reset_grad
                    out[row][0].append(x + reset * over)
                    out[row][1].append(grad - direct)
                    out[row][2].append(reset_grad)
            for row in range(rows_here):
                mixed_ref[row, here] = flat(out[row][0])
                pass_ref[row, here] = flat(out[row][1])
                reset_ref[row, here] = flat(out[row][2])
            return (*state, weight_sum, bias_sum)

        carry = lax.fori_loop(
            0, size // GROUP, group, (*[state_s[row] for row in range(rows_here)], sums_s[1], sums_s[3])
        )
        for row in range(rows_here):
            state_s[row] = carry[row]
        sums_s[1] = carry[rows_here]
        sums_s[3] = carry[rows_here + 1]

    @pl.when(step == blocks - 1)
    def _():
        final_ref[...] = state_s[...]
        state_s[...] = jnp.zeros_like(state_s)

    @pl.when(step >= blocks)
    def _():
        def group(turn, carry):
            index = size // GROUP - 1 - turn
            here = pl.ds(pl.multiple_of(index * GROUP, GROUP), GROUP)
            running = list(carry[:rows_here])
            weight_sum, bias_sum = carry[rows_here:]
            out = [([None] * GROUP, [None] * GROUP) for _ in range(rows_here)]
            for k in range(GROUP - 1, -1, -1):
                time = block_back * size + index * GROUP + k
                for row in range(rows_here):
                    forget = forget_s[row, time]
                    slope = slope_s[row, time]
                    keep = keep_ref[row, time]
                    state_grad = direct_s[row, time] + running[row]
                    through = (forget + slope * forget_weight) * keep
                    running[row] = through * state_grad + extra_s[row, time] * keep
                    forget_grad = state_grad * slope
                    weight_sum = weight_sum + forget_grad * before_s[row, time]
                    bias_sum = bias_sum + forget_grad
                    out[row][0][k] = state_grad - state_grad * forget
                    out[row][1][k] = forget_grad
            for row in range(rows_here):
                gates_ref[0, row, here] = flat(out[row][0])
                gates_ref[1, row, here] = flat(out[row][1])
            return (*running, weight_sum, bias_sum)

        carry = lax.fori_loop(
            0, size // GROUP, group, (*[state_s[row] for row in range(rows_here)], sums_s[0], sums_s[2])
        )
        for row in range(rows_here):
            state_s[row] = carry[row]
        sums_s[0] = carry[rows_here]
        sums_s[2] = carry[rows_here + 1]

    @pl.when(step == 2 * blocks - 1)
    def _():
        sums_ref[...] = sums_s[...]


def recur(keep, u, x, grad, params):
    rows_here, length, width = x.shape
    size = RECUR_TOKENS
    blocks = length // size
    ahead = lambda i: jnp.minimum(i, blocks - 1)
    back = lambda i: jnp.minimum(2 * blocks - 1 - i, blocks - 1)
    row_block = lambda place: pl.BlockSpec((rows_here, size, width), lambda i: (0, place(i), 0))
    whole = lambda *shape: pl.BlockSpec(shape, lambda i: (0,) * len(shape))
    tile = (SUBLANES, LANES)
    kept = pltpu.VMEM((rows_here, length) + tile, F32)
    return pl.pallas_call(
        recur_kernel,
        grid=(2 * blocks,),
        out_shape=(
            jax.ShapeDtypeStruct((rows_here, length, width), BF16),
            jax.ShapeDtypeStruct((rows_here, length, width), BF16),
            jax.ShapeDtypeStruct((rows_here, length, width), BF16),
            jax.ShapeDtypeStruct((2, rows_here, length, width), BF16),
            jax.ShapeDtypeStruct((rows_here,) + tile, F32),
            jax.ShapeDtypeStruct((4,) + tile, F32),
        ),
        in_specs=[
            pl.BlockSpec(memory_space=pltpu.SMEM),
            pl.BlockSpec((3, rows_here, size, width), lambda i: (0, 0, ahead(i), 0)),
            row_block(ahead), row_block(ahead), whole(4, *tile),
        ],
        out_specs=(
            row_block(ahead), row_block(ahead), row_block(ahead),
            pl.BlockSpec((2, rows_here, size, width), lambda i: (0, 0, back(i), 0)),
            whole(rows_here, *tile), whole(4, *tile),
        ),
        scratch_shapes=[kept] * 5 + [pltpu.VMEM((rows_here,) + tile, F32), pltpu.VMEM((4,) + tile, F32)],
        compiler_params=pltpu.CompilerParams(vmem_limit_bytes=VMEM_LIMIT),
        name="recur",
    )(keep, u, x, grad, params)


JOB_ROWS = 128
PIECE = 16
SLAB = 48
NORM_TOKENS = 256
RING = 8
SHORT = 4
ENDS = 3


def finish_kernel(
    normed_t_ref, gates_ref, reset_ref, weight_ref, x_ref, mean_ref, scale_ref, pass_ref, gain_ref, sums_ref,
    total_ref, input_grad_ref, small_ref,
    du, weights, rows_in, mine, core_out, core_in, y_out, y_in, down_out, down_in, up_out, up_in, cross_out, cross_in,
    ready, dn_all, dn_own, dn_out, dn_in, moment_out, moment_in, x_in, pass_in, mean_in, scale_in, grad_out,
    norm_sums, small_own, small_in, small_z,
    load_sem, rows_sem, core_send, core_recv, y_send, y_recv, down_send, down_recv, up_send, up_recv,
    cross_send, cross_recv, ready_sem, from_low_send, from_low_recv, from_high_send, from_high_recv,
    pair_send, pair_recv, twin_send, twin_recv, dn_send, dn_recv, moment_send, moment_recv, norm_sem, grad_sem,
    small_send, small_recv,
):
    device = lax.axis_index("rows")
    devices = lax.axis_size("rows")
    ch = lax.axis_index("ch")
    z_stride, y_stride = devices // 4, devices // 8
    z = device // z_stride
    y = (device // y_stride) % 2
    core = device % 2
    twin = device + 1 - 2 * core
    pair = device + y_stride * (1 - 2 * y)
    full, tokens = normed_t_ref.shape
    width = gates_ref.shape[2]
    half = full // 2
    per_gate = half // JOB_ROWS
    jobs = 3 * per_gate
    blocks = tokens // NORM_TOKENS

    def aligned(value, size=PIECE):
        return pl.multiple_of(value, size)

    def place(job, whose):
        return job // per_gate, aligned(whose * half + (job % per_gate) * JOB_ROWS, JOB_ROWS)

    down_row = aligned(PIECE * y)
    up_row = aligned(80 - PIECE * y)
    y_down, y_up = aligned(SLAB * y), aligned(112 - SLAB * y)
    pair_down, pair_up = aligned(SLAB * (1 - y)), aligned(112 - SLAB * (1 - y))

    def load_du(gate):
        source = reset_ref if gate == 2 else gates_ref.at[gate]
        return pltpu.make_async_copy(source, du.at[gate], load_sem.at[gate])

    def load_weight(gate):
        return pltpu.make_async_copy(weight_ref.at[gate], weights.at[gate], load_sem.at[3 + gate])

    def load_rows(job):
        slot = job % 2
        own = aligned(core * half + (job % per_gate) * JOB_ROWS, JOB_ROWS)
        other = aligned((1 - core) * half + (job % per_gate) * JOB_ROWS, JOB_ROWS)
        return (
            pltpu.make_async_copy(
                normed_t_ref.at[pl.ds(own, JOB_ROWS)], rows_in.at[slot, pl.ds(0, JOB_ROWS)], rows_sem.at[0, slot]
            ),
            pltpu.make_async_copy(
                normed_t_ref.at[pl.ds(other, JOB_ROWS)], rows_in.at[slot, pl.ds(JOB_ROWS, JOB_ROWS)],
                rows_sem.at[1, slot],
            ),
        )

    def remote(source, target, send, recv, where):
        return pltpu.make_async_remote_copy(
            src_ref=source, dst_ref=target, send_sem=send, recv_sem=recv, device_id=where, device_id_type=MESH
        )

    def to_core(job):
        return remote(
            core_out.at[job % 2], core_in.at[job % SHORT], core_send.at[job % 2], core_recv.at[job % SHORT],
            {"rows": twin},
        )

    def to_y(job):
        return remote(
            y_out.at[job % SHORT], y_in.at[job % RING], y_send.at[job % SHORT], y_recv.at[job % RING], {"rows": pair}
        )

    def to_down(job):
        return remote(
            down_out.at[job % SHORT], down_in.at[job % RING], down_send.at[job % SHORT], down_recv.at[job % RING],
            {"rows": device - z_stride},
        )

    def to_up(job):
        return remote(
            up_out.at[job % SHORT], up_in.at[job % RING], up_send.at[job % SHORT], up_recv.at[job % RING],
            {"rows": device + z_stride},
        )

    def to_cross(job):
        return remote(
            cross_out.at[job % SHORT], cross_in.at[job % RING], cross_send.at[job % SHORT], cross_recv.at[job % RING],
            {"rows": pair},
        )

    def result(job, offset, size, whose):
        gate, row = place(job, whose)
        return total_ref.at[gate, pl.ds(aligned(row + offset), size)]

    def keep_ready(job, offset):
        return pltpu.make_async_copy(
            ready.at[job % SHORT], result(job, offset, SLAB, core), ready_sem.at[job % SHORT]
        )

    def gather(job, offset, source, send, recv, where):
        return remote(source, result(job, offset, SLAB, core), send.at[job % RING], recv.at[job % RING], where)

    def from_low(job, first=False):
        source = ready.at[job % SHORT] if first else result(job, down_row, SLAB, core)
        return gather(job, down_row, source, from_low_send, from_low_recv, {"rows": device + z_stride})

    def from_high(job, first=False):
        source = ready.at[job % SHORT] if first else result(job, up_row, SLAB, core)
        return gather(job, up_row, source, from_high_send, from_high_recv, {"rows": device - z_stride})

    def to_pair(job):
        return tuple(
            remote(
                result(job, row, PIECE, core), result(job, row, PIECE, core),
                pair_send.at[side, job % RING], pair_recv.at[side, job % RING], {"rows": pair},
            )
            for side, row in enumerate((y_down, y_up))
        )

    def to_twin(job):
        return remote(
            result(job, 0, JOB_ROWS, core), result(job, 0, JOB_ROWS, core),
            twin_send.at[job % RING], twin_recv.at[job % RING], {"rows": twin},
        )

    def to_partner(block):
        return remote(
            dn_out.at[block % 2], dn_in.at[block % SHORT], dn_send.at[block % 2], dn_recv.at[block % SHORT],
            {"ch": 1 - ch},
        )

    def moments(block):
        return remote(
            moment_out.at[block % 2], moment_in.at[block % SHORT], moment_send.at[block % 2],
            moment_recv.at[block % SHORT], {"ch": 1 - ch},
        )

    def load_norm(block):
        rows = pl.ds(aligned(block * NORM_TOKENS, NORM_TOKENS), NORM_TOKENS)
        slot = block % SHORT
        return tuple(
            pltpu.make_async_copy(source.at[rows], target.at[slot], norm_sem.at[index, slot])
            for index, (source, target) in enumerate(
                ((x_ref, x_in), (pass_ref, pass_in), (mean_ref, mean_in), (scale_ref, scale_in))
            )
        )

    def store_grad(block):
        rows = pl.ds(aligned(block * NORM_TOKENS, NORM_TOKENS), NORM_TOKENS)
        return pltpu.make_async_copy(grad_out.at[block % 2], input_grad_ref.at[rows], grad_sem.at[block % 2])

    def small_twin():
        return remote(small_own, small_in.at[0], small_send.at[0], small_recv.at[0], {"rows": twin})

    def small_pair():
        return remote(small_own, small_in.at[1], small_send.at[1], small_recv.at[1], {"rows": pair})

    def small_column(away):
        there = (z + away) % 4
        return remote(
            small_own, small_z.at[z], small_send.at[1 + away], small_recv.at[1 + away],
            {"rows": device + (there - z) * z_stride},
        )

    for gate in range(3):
        load_du(gate).start()
        if gate == 0:
            for copy in load_rows(0):
                copy.start()
        load_weight(gate).start()

    barrier = pltpu.get_barrier_semaphore()
    for where in [{"rows": twin}, {"rows": pair}, {"ch": 1 - ch}] + [
        {"rows": device + ((z + away) % 4 - z) * z_stride} for away in (1, 2, 3)
    ]:
        pl.semaphore_signal(barrier, inc=1, device_id=where, device_id_type=MESH)
    pl.semaphore_wait(barrier, 6)
    norm_sums[...] = jnp.zeros_like(norm_sums)

    def is_job(job):
        return jnp.logical_and(job >= 0, job < jobs)

    def is_block(block):
        return jnp.logical_and(block >= 0, block < blocks)

    def when(*conditions):
        return pl.when(functools.reduce(jnp.logical_and, conditions))

    def tick(t, carry):
        @pl.when(t < 3)
        def _():
            for gate in range(3):
                @pl.when(t == gate)
                def _():
                    load_du(gate).wait()
                    load_weight(gate).wait()

        @when(is_job(t - 2))
        def _():
            to_core(t - 2).wait_send()

        @when(is_job(t))
        def _():
            gate, slot = t // per_gate, t % 2
            for copy in load_rows(t):
                copy.wait()

            @pl.when(t + 1 < jobs)
            def _():
                for copy in load_rows(t + 1):
                    copy.start()

            @pl.loop(0, 2)
            def _(part):
                columns = pl.ds(aligned(part * (width // 2), width // 2), width // 2)
                product = jnp.dot(rows_in[slot], du[gate, :, columns], preferred_element_type=F32)
                mine[t % RING, :, columns] = product[:JOB_ROWS]
                core_out[slot, :, columns] = product[JOB_ROWS:].astype(BF16)

            to_core(t).start()

        job = t - 1

        @when(is_job(job))
        def _():
            to_core(job).wait_recv()
            slot = job % RING
            mine[slot] += core_in[job % SHORT].astype(F32)
            y_out[job % SHORT, 0:PIECE] = mine[slot, pl.ds(pair_down, PIECE)].astype(BF16)
            y_out[job % SHORT, PIECE:2 * PIECE] = mine[slot, pl.ds(pair_up, PIECE)].astype(BF16)
            to_y(job).start()

        @when(is_job(job - 2))
        def _():
            to_y(job - 2).wait_send()

        job = t - 2

        @when(is_job(job))
        def _():
            to_y(job).wait_recv()
            slot = job % RING
            mine[slot, pl.ds(y_down, PIECE)] += y_in[job % RING, 0:PIECE].astype(F32)
            mine[slot, pl.ds(y_up, PIECE)] += y_in[job % RING, PIECE:2 * PIECE].astype(F32)

        def chain(lag, row, y_place, z_place, hop, arrived, out):
            job = t - 2 - lag

            @when(is_job(job), lag > 0)
            def _():
                hop(job).wait_recv()
                mine[job % RING, pl.ds(row, SLAB)] += arrived[job % RING].astype(F32)

            @when(is_job(job), lag < ENDS)
            def _():
                out[job % SHORT] = mine[job % RING, pl.ds(row, SLAB)].astype(BF16)
                hop(job).start()

            @when(is_job(job - 2), lag < ENDS)
            def _():
                hop(job - 2).wait_send()

            @when(is_job(job), lag == ENDS)
            def _():
                ready[job % SHORT, pl.ds(y_place, PIECE)] = mine[
                    job % RING, pl.ds(aligned(row + y_place), PIECE)
                ].astype(BF16)
                cross_out[job % SHORT] = mine[
                    job % RING, pl.ds(aligned(row + z_place), 2 * PIECE)
                ].astype(BF16)
                to_cross(job).start()

            @when(is_job(job - 2), lag == ENDS)
            def _():
                to_cross(job - 2).wait_send()

        y_in_down, z_in_down = aligned(2 * PIECE * y), aligned(PIECE * (1 - y))
        y_in_up, z_in_up = aligned(2 * PIECE * (1 - y)), aligned(PIECE * y)
        chain(ENDS - z, down_row, y_in_down, z_in_down, to_down, down_in, down_out)
        chain(z, up_row, y_in_up, z_in_up, to_up, up_in, up_out)

        def spread(lag, row, z_place, hop):
            job = t - 6 - lag

            @when(is_job(job), lag == 0)
            def _():
                to_cross(job).wait_recv()
                ready[job % SHORT, pl.ds(z_place, 2 * PIECE)] = (
                    cross_out[job % SHORT].astype(F32) + cross_in[job % RING].astype(F32)
                ).astype(BF16)
                keep_ready(job, row).start()
                hop(job, True).start()

            @when(is_job(job - 2), lag == 0)
            def _():
                keep_ready(job - 2, row).wait()
                hop(job - 2, True).wait_send()

            @when(is_job(job), lag > 0)
            def _():
                hop(job).wait_recv()

            @when(is_job(job), lag > 0, lag < ENDS)
            def _():
                hop(job).start()

            @when(is_job(job - 2), lag > 0, lag < ENDS)
            def _():
                hop(job - 2).wait_send()

        spread(z, down_row, z_in_down, from_low)
        spread(ENDS - z, up_row, z_in_up, from_high)

        job = t - 9

        @when(is_job(job))
        def _():
            for copy in to_pair(job):
                copy.start()

        @when(is_job(job - 2))
        def _():
            for copy in to_pair(job - 2):
                copy.wait_send()

        job = t - 10

        @when(is_job(job))
        def _():
            for copy in to_pair(job):
                copy.wait_recv()
            to_twin(job).start()

        @when(is_job(job - 2))
        def _():
            to_twin(job - 2).wait_send()

        job = t - 11

        @when(is_job(job))
        def _():
            to_twin(job).wait_recv()

        block, gate = t // 3, t % 3

        @when(is_block(block))
        def _():
            rows = pl.ds(aligned(block * NORM_TOKENS, NORM_TOKENS), NORM_TOKENS)

            @pl.when(gate == 0)
            def _():
                dn_all[...] = jnp.zeros_like(dn_all)

            @pl.loop(0, full // 512)
            def _(part):
                columns = pl.ds(aligned(part * 512, 512), 512)
                dn_all[:, columns] += lax.dot_general(
                    du[gate, rows, :], weights[gate, columns, :], (((1,), (1,)), ((), ())),
                    preferred_element_type=F32,
                )

        own_columns = pl.ds(aligned(ch * width, width), width)
        other_columns = pl.ds(aligned((1 - ch) * width, width), width)

        @when(is_block(block), gate == 2)
        def _():
            dn_out[block % 2] = dn_all[:, other_columns].astype(BF16)
            dn_own[block % SHORT] = dn_all[:, own_columns]
            to_partner(block).start()
            for copy in load_norm(block):
                copy.start()

        @when(is_block(block - 1), gate == 2)
        def _():
            now = block - 1
            slot = now % SHORT
            to_partner(now).wait()
            for copy in load_norm(now):
                copy.wait()

            def part(index, sums):
                gain_sum, shift_sum = sums
                rows = pl.ds(aligned(index * PIECE), PIECE)
                dn = dn_own[slot, rows, :] + dn_in[slot, rows, :].astype(F32)
                dn_own[slot, rows, :] = dn
                scale = scale_in[slot, rows, 0:1]
                xhat = (x_in[slot, rows, :].astype(F32) - mean_in[slot, rows, 0:1]) * scale
                gained = dn * xhat
                dxhat = dn * gain_ref[0:1, :]
                first = jnp.sum(dxhat, axis=1, keepdims=True)
                second = jnp.sum(dxhat * xhat, axis=1, keepdims=True)
                lane = lax.broadcasted_iota(jnp.int32, (PIECE, LANES), 1)
                moment_out[now % 2, rows, :] = jnp.where(lane < LANES // 2, first, second)
                return (
                    gain_sum + gained[:SUBLANES] + gained[SUBLANES:], shift_sum + dn[:SUBLANES] + dn[SUBLANES:],
                )

            gain_sum, shift_sum = lax.fori_loop(0, NORM_TOKENS // PIECE, part, (norm_sums[0], norm_sums[1]))
            norm_sums[0] = gain_sum
            norm_sums[1] = shift_sum
            moments(now).start()

        @when(is_block(block - 2), gate == 2)
        def _():
            now = block - 2
            slot = now % SHORT
            moments(now).wait()

            @pl.loop(0, NORM_TOKENS // PIECE)
            def _(index):
                rows = pl.ds(aligned(index * PIECE), PIECE)
                both = (moment_out[now % 2, rows, :] + moment_in[slot, rows, :]) * (1.0 / full)
                first, second = both[:, 0:1], both[:, LANES // 2:LANES // 2 + 1]
                scale = scale_in[slot, rows, 0:1]
                xhat = (x_in[slot, rows, :].astype(F32) - mean_in[slot, rows, 0:1]) * scale
                back = scale * (dn_own[slot, rows, :] * gain_ref[0:1, :] - first - xhat * second)
                grad_out[now % 2, rows, :] = (back + pass_in[slot, rows, :].astype(F32)).astype(BF16)

            store_grad(now).start()

        @when(is_block(block - 3), gate == 2)
        def _():
            store_grad(block - 3).wait()

        at = 3 * (blocks + 1)

        @pl.when(t == at)
        def _():
            small_own[...] = jnp.zeros_like(small_own)
            small_own[0:4] = sums_ref[...]
            small_own[4:5] = jnp.sum(norm_sums[0], axis=0, keepdims=True)
            small_own[5:6] = jnp.sum(norm_sums[1], axis=0, keepdims=True)
            small_twin().start()

        @pl.when(t == at + 1)
        def _():
            small_twin().wait()
            small_own[...] += small_in[0]
            small_pair().start()

        @pl.when(t == at + 2)
        def _():
            small_pair().wait()
            small_own[...] += small_in[1]
            for away in (1, 2, 3):
                small_column(away).start()

        @pl.when(t == at + 3)
        def _():
            for away in (1, 2, 3):
                small_column(away).wait()
            small_z[z] = small_own[...]
            small_ref[...] = (small_z[0] + small_z[1]) + (small_z[2] + small_z[3])

        return carry

    lax.fori_loop(0, jobs + 13, tick, 0)


def finish(normed_t, gates, reset, weight, x, mean, scale, passed, gain, sums):
    full, tokens = normed_t.shape
    width = x.shape[1]
    dma = pltpu.SemaphoreType.DMA
    vmem = pl.BlockSpec(memory_space=pltpu.VMEM)
    norm = NORM_TOKENS
    return pl.pallas_call(
        finish_kernel,
        out_shape=(
            jax.ShapeDtypeStruct((3, full, width), BF16),
            jax.ShapeDtypeStruct((tokens, width), BF16),
            jax.ShapeDtypeStruct((SUBLANES, width), F32),
        ),
        in_specs=[ANY] * 8 + [vmem, vmem],
        out_specs=(ANY, ANY, vmem),
        scratch_shapes=[
            pltpu.VMEM((3, tokens, width), BF16),
            pltpu.VMEM((3, full, width), BF16),
            pltpu.VMEM((2, 2 * JOB_ROWS, tokens), BF16),
            pltpu.VMEM((RING, JOB_ROWS, width), F32),
            pltpu.VMEM((2, JOB_ROWS, width), BF16),
            pltpu.VMEM((SHORT, JOB_ROWS, width), BF16),
            pltpu.VMEM((SHORT, 2 * PIECE, width), BF16),
            pltpu.VMEM((RING, 2 * PIECE, width), BF16),
            pltpu.VMEM((SHORT, SLAB, width), BF16),
            pltpu.VMEM((RING, SLAB, width), BF16),
            pltpu.VMEM((SHORT, SLAB, width), BF16),
            pltpu.VMEM((RING, SLAB, width), BF16),
            pltpu.VMEM((SHORT, 2 * PIECE, width), BF16),
            pltpu.VMEM((RING, 2 * PIECE, width), BF16),
            pltpu.VMEM((SHORT, SLAB, width), BF16),
            pltpu.VMEM((norm, full), F32),
            pltpu.VMEM((SHORT, norm, width), F32),
            pltpu.VMEM((2, norm, width), BF16),
            pltpu.VMEM((SHORT, norm, width), BF16),
            pltpu.VMEM((2, norm, LANES), F32),
            pltpu.VMEM((SHORT, norm, LANES), F32),
            pltpu.VMEM((SHORT, norm, width), BF16),
            pltpu.VMEM((SHORT, norm, width), BF16),
            pltpu.VMEM((SHORT, norm, LANES), F32),
            pltpu.VMEM((SHORT, norm, LANES), F32),
            pltpu.VMEM((2, norm, width), BF16),
            pltpu.VMEM((2, SUBLANES, width), F32),
            pltpu.VMEM((SUBLANES, width), F32),
            pltpu.VMEM((2, SUBLANES, width), F32),
            pltpu.VMEM((4, SUBLANES, width), F32),
            dma((6,)), dma((2, 2)),
            dma((2,)), dma((SHORT,)), dma((SHORT,)), dma((RING,)), dma((SHORT,)), dma((RING,)),
            dma((SHORT,)), dma((RING,)), dma((SHORT,)), dma((RING,)), dma((SHORT,)),
            dma((RING,)), dma((RING,)), dma((RING,)), dma((RING,)),
            dma((2, RING)), dma((2, RING)), dma((RING,)), dma((RING,)),
            dma((2,)), dma((SHORT,)), dma((2,)), dma((SHORT,)), dma((4, SHORT)), dma((2,)),
            dma((5,)), dma((5,)),
        ],
        compiler_params=pltpu.CompilerParams(
            collective_id=1, has_side_effects=True, vmem_limit_bytes=VMEM_LIMIT
        ),
        name="finish",
    )(normed_t, gates, reset, weight, x, mean, scale, passed, gain, sums)


def on_device(
    inputs, doc_lengths, layer_norm_gain, layer_norm_bias, weight, forget_weight, reset_weight, forget_bias,
    reset_bias, out_grad,
):
    rows_here, length, width = inputs.shape
    tokens = rows_here * length
    tile = (SUBLANES, LANES)
    weights = jnp.transpose(weight, (1, 0, 2))
    norm_params = jnp.zeros((SUBLANES, width), F32).at[0].set(layer_norm_gain).at[1].set(layer_norm_bias)
    x = inputs.reshape(tokens, width)
    u, normed_t, mean, scale = project(x, norm_params, weights)

    starts = jnp.cumsum(doc_lengths, axis=-1) - doc_lengths
    places = jnp.arange(length, dtype=jnp.int32)
    hits = (places[None, :, None] == starts[:, None, :]).astype(F32)
    keep = 1.0 - jnp.sum(hits, axis=-1)
    gate_params = jnp.stack([forget_weight, reset_weight, forget_bias, reset_bias]).reshape((4,) + tile)
    mixed, passed, reset_grad, gate_grads, final_state, sums = recur(
        keep, u.reshape(3, rows_here, length, width), inputs, out_grad, gate_params
    )
    weight_grad, input_grad, small = finish(
        normed_t, gate_grads.reshape(2, tokens, width), reset_grad.reshape(tokens, width), weights, x, mean, scale,
        passed.reshape(tokens, width), norm_params, sums.reshape(4, width),
    )
    weight_grad = weight_grad.astype(F32)
    devices = lax.axis_size("rows")
    groups = devices // 16
    if groups > 1:
        members = [[] for _ in range(devices // groups)]
        for device in range(devices):
            part, core = device // 2, device % 2
            members[(part // groups) * 2 + core].append(device)
        weight_grad, small = lax.psum((weight_grad, small), "rows", axis_index_groups=members)
    weight_grad = jnp.transpose(weight_grad, (1, 0, 2))
    return (
        mixed, input_grad.reshape(inputs.shape), final_state.reshape(rows_here, width), weight_grad,
        small[4], small[5], small[0], small[1], small[2], small[3],
    )


def solution(mesh):
    rows_ch = P("rows", None, "ch")
    ch = P("ch")
    in_specs = (rows_ch, P("rows", None), ch, ch, P(None, None, "ch"), ch, ch, ch, ch, rows_ch)
    out_specs = (rows_ch, rows_ch, P("rows", "ch"), P(None, None, "ch"), ch, ch, ch, ch, ch, ch)
    return jax.shard_map(on_device, mesh=mesh, in_specs=in_specs, out_specs=out_specs, check_vma=False)
```

```python
import functools

import jax
import jax.numpy as jnp
from jax import lax
from jax.experimental import pallas as pl
from jax.experimental.pallas import tpu as pltpu
from jax.sharding import PartitionSpec as P

MESH = pl.DeviceIdType.MESH
F32 = jnp.float32
BF16 = jnp.bfloat16
EPSILON = 1e-05
LANES = 128
SUBLANES = 8
TILE = (SUBLANES, LANES)
STRETCH = 64
GROUP = 16
ANY = pl.BlockSpec(memory_space=pl.ANY)
IN_VMEM = pl.BlockSpec(memory_space=pltpu.VMEM)
IN_SMEM = pl.BlockSpec(memory_space=pltpu.SMEM)
VMEM_LIMIT = 60 * 1024 * 1024


def aligned(value, size=GROUP):
    return pl.multiple_of(value, size)


def fill_keep(lengths_ref, keep):
    rows_here, length = keep.shape[0], keep.shape[1]
    for row in range(rows_here):
        starts = [jnp.int32(0)]
        for document in range(lengths_ref.shape[1] - 1):
            starts.append(starts[-1] + lengths_ref[row, document])

        @pl.loop(0, length // LANES)
        def _(part):
            place = lax.broadcasted_iota(jnp.int32, (LANES, LANES), 0) + part * LANES
            value = jnp.ones((LANES, LANES), F32)
            for start in starts:
                value = jnp.where(place == start, 0.0, value)
            keep[row, pl.ds(aligned(part * LANES, LANES), LANES), :] = value


def project_kernel(
    lengths_ref, x_ref, gain_ref, shift_ref, weight_ref, grad_ref,
    forget_weight_ref, reset_weight_ref, forget_bias_ref, reset_bias_ref,
    saved_ref, normed_t_ref, mean_ref, scale_ref, mixed_ref, pass_ref, reset_ref, final_ref, sums_ref,
    both, weights, params, keep, normed, normed_t, mean_out, scale_out, u, grad_in, saved, mixed_out, pass_out,
    reset_out, state_s,
    send_sem, recv_sem, own_sem, param_own, param_send, param_recv, weight_sem, grad_sem, out_sem,
):
    ch = lax.axis_index("ch")
    other = 1 - ch
    rows_here, stretches, size, width = x_ref.shape
    full = 2 * width
    tokens = rows_here * size
    own_columns = pl.ds(aligned(ch * width, width), width)

    load_weight = pltpu.make_async_copy(weight_ref, weights, weight_sem)

    def params_of(index, source):
        return (
            pltpu.make_async_copy(source, params.at[ch, index], param_own.at[index]),
            pltpu.make_async_remote_copy(
                src_ref=source, dst_ref=params.at[ch, index], send_sem=param_send.at[index],
                recv_sem=param_recv.at[index], device_id={"ch": other}, device_id_type=MESH,
            ),
        )

    def exchange(stretch):
        return pltpu.make_async_remote_copy(
            src_ref=x_ref.at[:, stretch], dst_ref=both.at[:, stretch, :, own_columns],
            send_sem=send_sem.at[stretch], recv_sem=recv_sem.at[stretch],
            device_id={"ch": other}, device_id_type=MESH,
        )

    def keep_own(stretch):
        return pltpu.make_async_copy(x_ref.at[:, stretch], both.at[:, stretch, :, own_columns], own_sem.at[stretch])

    def load_grad(stretch):
        slot = stretch % 2
        return pltpu.make_async_copy(grad_ref.at[:, stretch], grad_in.at[slot], grad_sem.at[slot])

    def outputs(stretch):
        slot = stretch % 2
        rows = pl.ds(aligned(stretch * tokens, tokens), tokens)
        return tuple(
            pltpu.make_async_copy(source.at[slot], target, out_sem.at[index, slot])
            for index, (source, target) in enumerate((
                (saved, saved_ref.at[stretch]), (normed_t, normed_t_ref.at[:, rows]), (mean_out, mean_ref.at[rows]),
                (scale_out, scale_ref.at[rows]), (mixed_out, mixed_ref.at[:, stretch]), (pass_out, pass_ref.at[rows]),
                (reset_out, reset_ref.at[rows]),
            ))
        )

    load_weight.start()
    load_grad(0).start()
    barrier = pltpu.get_barrier_semaphore()
    pl.semaphore_signal(barrier, inc=1, device_id={"ch": other}, device_id_type=MESH)
    pl.semaphore_wait(barrier, 1)
    for index, source in enumerate((gain_ref, shift_ref)):
        for copy in params_of(index, source):
            copy.start()

    def begin(stretch, carry):
        exchange(stretch).start()
        keep_own(stretch).start()
        return carry

    lax.fori_loop(0, stretches, begin, 0)
    fill_keep(lengths_ref, keep)
    state_s[...] = jnp.zeros_like(state_s)
    sums_ref[...] = jnp.zeros_like(sums_ref)
    for index, source in enumerate((gain_ref, shift_ref)):
        for copy in params_of(index, source):
            copy.wait()
    load_weight.wait()

    def work(stretch, carry):
        slot = stretch % 2
        keep_own(stretch).wait()
        exchange(stretch).wait()
        load_grad(stretch).wait()

        @pl.when(stretch + 1 < stretches)
        def _():
            load_grad(stretch + 1).start()

        @pl.when(stretch >= 2)
        def _():
            for copy in outputs(stretch - 2):
                copy.wait()

        for row in range(rows_here):
            @pl.loop(0, size // GROUP, unroll=2)
            def _(part):
                here = pl.ds(aligned(part * GROUP), GROUP)
                there = pl.ds(aligned(row * size + part * GROUP), GROUP)
                x = both[row, stretch, here, :].astype(F32)
                mean = jnp.sum(x, axis=1, keepdims=True) * (1.0 / full)
                centered = x - mean
                variance = jnp.sum(centered * centered, axis=1, keepdims=True) * (1.0 / full)
                scale = lax.rsqrt(variance + EPSILON)
                gain = jnp.concatenate([params[0, 0], params[1, 0]], axis=1)
                shift = jnp.concatenate([params[0, 1], params[1, 1]], axis=1)
                normed[there, :] = (centered * scale * gain + shift).astype(BF16)
                mean_out[slot, there, :] = jnp.broadcast_to(mean, (GROUP, LANES))
                scale_out[slot, there, :] = jnp.broadcast_to(scale, (GROUP, LANES))

        for gate in range(3):
            u[gate] = jnp.dot(normed[...], weights[gate], preferred_element_type=F32)

        for part in range(full // LANES):
            columns = slice(part * LANES, (part + 1) * LANES)
            normed_t[slot, columns, :] = normed[:, columns].T

        forget_weight = 0.5 * forget_weight_ref[...]
        reset_weight = reset_weight_ref[...]
        half_reset_weight = 0.5 * reset_weight
        forget_bias = 0.5 * forget_bias_ref[...]
        reset_bias = 0.5 * reset_bias_ref[...]

        def group(index, carry):
            state = list(carry[:rows_here])
            weight_sum, bias_sum = carry[rows_here:]
            here = pl.ds(aligned(index * GROUP), GROUP)
            there = [pl.ds(aligned(row * size + index * GROUP), GROUP) for row in range(rows_here)]
            spread = lambda value: value.astype(F32).reshape((GROUP,) + TILE)
            loaded = [
                (
                    spread(u[0, there[row], :]), spread(u[1, there[row], :]), spread(u[2, there[row], :]),
                    spread(both[row, stretch, here, own_columns]), spread(grad_in[slot, row, here, :]),
                )
                for row in range(rows_here)
            ]
            out = [([], [], []) for _ in range(rows_here)]
            for k in range(GROUP):
                time = index * GROUP + k
                for row in range(rows_here):
                    up_x, up_f, up_r, x, grad = (part[k] for part in loaded[row])
                    before = state[row] * keep[row, pl.ds(stretch * size + time, 1), :]
                    bent = jnp.tanh(0.5 * up_f + forget_bias + forget_weight * before)
                    gap = before - up_x
                    after = 0.5 * (before + up_x) + bent * (0.5 * gap)
                    state[row] = after
                    forget = 0.5 * bent + 0.5
                    reset = 0.5 * jnp.tanh(0.5 * up_r + reset_bias + half_reset_weight * before) + 0.5
                    over = after - x
                    direct = grad * reset
                    reset_grad = direct * over * (1.0 - reset)
                    saved[slot, 0, row, time] = direct
                    saved[slot, 1, row, time] = reset_grad * reset_weight
                    saved[slot, 2, row, time] = forget
                    saved[slot, 3, row, time] = gap * forget * (1.0 - forget)
                    saved[slot, 4, row, time] = before
                    weight_sum = weight_sum + reset_grad * before
                    bias_sum = bias_sum + reset_grad
                    out[row][0].append(x + reset * over)
                    out[row][1].append(grad - direct)
                    out[row][2].append(reset_grad)
            flat = lambda parts: jnp.stack(parts).reshape(GROUP, width).astype(BF16)
            for row in range(rows_here):
                mixed_out[slot, row, here, :] = flat(out[row][0])
                pass_out[slot, there[row], :] = flat(out[row][1])
                reset_out[slot, there[row], :] = flat(out[row][2])
            return (*state, weight_sum, bias_sum)

        carried = lax.fori_loop(
            0, size // GROUP, group, (*[state_s[row] for row in range(rows_here)], sums_ref[0], sums_ref[1])
        )
        for row in range(rows_here):
            state_s[row] = carried[row]
        sums_ref[0] = carried[rows_here]
        sums_ref[1] = carried[rows_here + 1]
        for copy in outputs(stretch):
            copy.start()
        return carry

    lax.fori_loop(0, stretches, work, 0)
    for row in range(rows_here):
        final_ref[row:row + 1, :] = state_s[row].reshape(1, width)
    for stretch in (stretches - 2, stretches - 1):
        for copy in outputs(stretch):
            copy.wait()


def project(lengths, x, gain, shift, weight, grad, forget_weight, reset_weight, forget_bias, reset_bias):
    rows_here, stretches, size, width = x.shape
    full = 2 * width
    part = rows_here * size
    tokens = part * stretches
    kept = (5, rows_here, size) + TILE
    dma = pltpu.SemaphoreType.DMA
    shape = jax.ShapeDtypeStruct
    return pl.pallas_call(
        project_kernel,
        out_shape=(
            shape((stretches,) + kept, F32),
            shape((full, tokens), BF16),
            shape((tokens, LANES), F32),
            shape((tokens, LANES), F32),
            shape(x.shape, BF16),
            shape((tokens, width), BF16),
            shape((tokens, width), BF16),
            shape((rows_here, width), F32),
            shape((2,) + TILE, F32),
        ),
        in_specs=[IN_SMEM] + [ANY] * 5 + [IN_VMEM] * 4,
        out_specs=[ANY] * 7 + [IN_VMEM] * 2,
        scratch_shapes=[
            pltpu.VMEM((rows_here, stretches, size, full), BF16),
            pltpu.VMEM((3, full, width), BF16),
            pltpu.VMEM((2, 2, 1, width), F32),
            pltpu.VMEM((rows_here, stretches * size, LANES), F32),
            pltpu.VMEM((part, full), BF16),
            pltpu.VMEM((2, full, part), BF16),
            pltpu.VMEM((2, part, LANES), F32),
            pltpu.VMEM((2, part, LANES), F32),
            pltpu.VMEM((3, part, width), F32),
            pltpu.VMEM((2, rows_here, size, width), BF16),
            pltpu.VMEM((2,) + kept, F32),
            pltpu.VMEM((2, rows_here, size, width), BF16),
            pltpu.VMEM((2, part, width), BF16),
            pltpu.VMEM((2, part, width), BF16),
            pltpu.VMEM((rows_here,) + TILE, F32),
            dma((stretches,)), dma((stretches,)), dma((stretches,)), dma((2,)), dma((2,)), dma((2,)), dma, dma((2,)),
            dma((7, 2)),
        ],
        compiler_params=pltpu.CompilerParams(
            collective_id=0, has_side_effects=True, vmem_limit_bytes=VMEM_LIMIT
        ),
        name="project",
    )(lengths, x, gain, shift, weight, grad, forget_weight, reset_weight, forget_bias, reset_bias)


JOB_ROWS = 128
PIECE = 16
SLAB = 48
NORM_TOKENS = 256
HALF = 32
RING = 8
SHORT = 4
ENDS = 3
SPLIT = 1
UNROLL = 4
HOP = 2
BASE = 1 + HOP
BACK = BASE + (ENDS + 1) * HOP
PAIR = BACK + ENDS * HOP
TWIN = PAIR + HOP
LATE = 3
MINE = BASE + ENDS * HOP + 1
PERIOD = 4
KEPT = 3
AHEAD = 4


def finish_kernel(
    lengths_ref, saved_ref, normed_t_ref, reset_ref, weight_ref, x_ref, mean_ref, scale_ref, pass_ref, gain_ref,
    forget_weight_ref, sums_ref,
    total_ref, input_grad_ref, small_ref,
    du, weights, rows_in, mine, core_out, core_in, y_out, y_in, down_out, down_in, up_out, up_in, cross_out, cross_in,
    ready, dn_own, dn_out, dn_in, moment_out, moment_in, x_in, pass_in, mean_in, scale_in, grad_out,
    norm_sums, keep, saved, state_s, gate_sums, small_own, small_in, small_z,
    load_sem, rows_sem, saved_sem, core_send, core_recv, y_send, y_recv, down_send, down_recv, up_send, up_recv,
    cross_send, cross_recv, ready_sem, from_low_send, from_low_recv, from_high_send, from_high_recv,
    pair_send, pair_recv, twin_send, twin_recv, dn_send, dn_recv, moment_send, moment_recv, norm_sem, grad_sem,
    small_send, small_recv,
):
    device = lax.axis_index("rows")
    devices = lax.axis_size("rows")
    ch = lax.axis_index("ch")
    z_stride, y_stride = devices // 4, devices // 8
    z = device // z_stride
    y = (device // y_stride) % 2
    core = device % 2
    twin = device + 1 - 2 * core
    pair = device + y_stride * (1 - 2 * y)
    full, tokens = normed_t_ref.shape
    rows_here, stretches, size, width = x_ref.shape
    half = full // 2
    narrow = width // SPLIT
    per_part = half // JOB_ROWS
    per_gate = per_part * SPLIT
    jobs = 3 * per_gate
    blocks = tokens // NORM_TOKENS

    def gate_of(job):
        return (job // per_gate + 2) % 3

    def place(job, whose):
        row = aligned(whose * half + (job % per_part) * JOB_ROWS, JOB_ROWS)
        column = aligned(((job // per_part) % SPLIT) * narrow, narrow)
        return gate_of(job), row, column

    down_row = aligned(PIECE * y)
    up_row = aligned(80 - PIECE * y)
    y_down, y_up = aligned(SLAB * y), aligned(112 - SLAB * y)
    pair_down, pair_up = aligned(SLAB * (1 - y)), aligned(112 - SLAB * (1 - y))

    load_reset = pltpu.make_async_copy(reset_ref, du.at[2], load_sem.at[3])

    def load_weight(gate):
        return pltpu.make_async_copy(weight_ref.at[gate], weights.at[gate], load_sem.at[gate])

    def load_rows(job):
        slot = job % 2
        own = aligned(core * half + (job % per_part) * JOB_ROWS, JOB_ROWS)
        other = aligned((1 - core) * half + (job % per_part) * JOB_ROWS, JOB_ROWS)
        return (
            pltpu.make_async_copy(
                normed_t_ref.at[pl.ds(own, JOB_ROWS)], rows_in.at[slot, pl.ds(0, JOB_ROWS)], rows_sem.at[0, slot]
            ),
            pltpu.make_async_copy(
                normed_t_ref.at[pl.ds(other, JOB_ROWS)], rows_in.at[slot, pl.ds(JOB_ROWS, JOB_ROWS)],
                rows_sem.at[1, slot],
            ),
        )

    def remote(source, target, send, recv, where):
        return pltpu.make_async_remote_copy(
            src_ref=source, dst_ref=target, send_sem=send, recv_sem=recv, device_id=where, device_id_type=MESH
        )

    def to_core(job):
        return remote(
            core_out.at[job % 2], core_in.at[job % SHORT], core_send.at[job % 2], core_recv.at[job % SHORT],
            {"rows": twin},
        )

    def to_y(job):
        return remote(
            y_out.at[job % SHORT], y_in.at[job % RING], y_send.at[job % SHORT], y_recv.at[job % RING], {"rows": pair}
        )

    def to_down(job):
        return remote(
            down_out.at[job % SHORT], down_in.at[job % RING], down_send.at[job % SHORT], down_recv.at[job % RING],
            {"rows": device - z_stride},
        )

    def to_up(job):
        return remote(
            up_out.at[job % SHORT], up_in.at[job % RING], up_send.at[job % SHORT], up_recv.at[job % RING],
            {"rows": device + z_stride},
        )

    def to_cross(job):
        return remote(
            cross_out.at[job % SHORT], cross_in.at[job % RING], cross_send.at[job % SHORT], cross_recv.at[job % RING],
            {"rows": pair},
        )

    def result(job, offset, size, whose):
        gate, row, column = place(job, whose)
        return total_ref.at[gate, pl.ds(aligned(row + offset), size), pl.ds(column, narrow)]

    def keep_ready(job, offset):
        return pltpu.make_async_copy(
            ready.at[job % RING], result(job, offset, SLAB, core), ready_sem.at[job % RING]
        )

    def gather(job, offset, source, send, recv, where):
        return remote(source, result(job, offset, SLAB, core), send.at[job % RING], recv.at[job % RING], where)

    def from_low(job, first=False):
        source = ready.at[job % RING] if first else result(job, down_row, SLAB, core)
        return gather(job, down_row, source, from_low_send, from_low_recv, {"rows": device + z_stride})

    def from_high(job, first=False):
        source = ready.at[job % RING] if first else result(job, up_row, SLAB, core)
        return gather(job, up_row, source, from_high_send, from_high_recv, {"rows": device - z_stride})

    def to_pair(job):
        return tuple(
            remote(
                result(job, row, PIECE, core), result(job, row, PIECE, core),
                pair_send.at[side, job % RING], pair_recv.at[side, job % RING], {"rows": pair},
            )
            for side, row in enumerate((y_down, y_up))
        )

    def to_twin(job):
        return remote(
            result(job, 0, JOB_ROWS, core), result(job, 0, JOB_ROWS, core),
            twin_send.at[job % RING], twin_recv.at[job % RING], {"rows": twin},
        )

    def to_partner(block):
        return remote(
            dn_out.at[block % 2], dn_in.at[block % SHORT], dn_send.at[block % 2], dn_recv.at[block % SHORT],
            {"ch": 1 - ch},
        )

    def moments(block):
        return remote(
            moment_out.at[block % 2], moment_in.at[block % SHORT], moment_send.at[block % 2],
            moment_recv.at[block % SHORT], {"ch": 1 - ch},
        )

    pieces = NORM_TOKENS // (rows_here * size)

    def first_row(block):
        return aligned(tokens - NORM_TOKENS * (block + 1), NORM_TOKENS)

    def load_norm(block):
        rows = pl.ds(first_row(block), NORM_TOKENS)
        slot = block % KEPT
        return tuple(
            pltpu.make_async_copy(source.at[rows], target.at[slot], norm_sem.at[index, slot])
            for index, (source, target) in enumerate(((pass_ref, pass_in), (mean_ref, mean_in), (scale_ref, scale_in)))
        ) + tuple(
            pltpu.make_async_copy(
                x_ref.at[:, stretches - pieces * (block + 1) + piece], x_in.at[slot, piece],
                norm_sem.at[3 + piece, slot],
            )
            for piece in range(pieces)
        )

    def store_grad(block):
        return tuple(
            pltpu.make_async_copy(
                grad_out.at[block % 2, piece], input_grad_ref.at[:, stretches - pieces * (block + 1) + piece],
                grad_sem.at[piece, block % 2],
            )
            for piece in range(pieces)
        )

    def load_saved(turn):
        slot = turn % AHEAD
        return pltpu.make_async_copy(
            saved_ref.at[stretches - 1 - turn // 2, :, :, pl.ds(aligned((1 - turn % 2) * HALF, HALF), HALF)],
            saved.at[slot], saved_sem.at[slot],
        )

    def small_twin():
        return remote(small_own, small_in.at[0], small_send.at[0], small_recv.at[0], {"rows": twin})

    def small_pair():
        return remote(small_own, small_in.at[1], small_send.at[1], small_recv.at[1], {"rows": pair})

    def small_column(away):
        there = (z + away) % 4
        return remote(
            small_own, small_z.at[z], small_send.at[1 + away], small_recv.at[1 + away],
            {"rows": device + (there - z) * z_stride},
        )

    load_reset.start()
    for copy in load_rows(0):
        copy.start()
    for turn in range(AHEAD - 1):
        load_saved(turn).start()
    for gate in range(3):
        load_weight(gate).start()

    barrier = pltpu.get_barrier_semaphore()
    for where in [{"rows": twin}, {"rows": pair}, {"ch": 1 - ch}] + [
        {"rows": device + ((z + away) % 4 - z) * z_stride} for away in (1, 2, 3)
    ]:
        pl.semaphore_signal(barrier, inc=1, device_id=where, device_id_type=MESH)
    pl.semaphore_wait(barrier, 6)
    norm_sums[...] = jnp.zeros_like(norm_sums)
    state_s[...] = jnp.zeros_like(state_s)
    gate_sums[...] = jnp.zeros_like(gate_sums)
    fill_keep(lengths_ref, keep)
    turns = 2 * stretches
    turns_tick = turns // per_gate
    load_reset.wait()

    def is_job(job):
        return jnp.logical_and(job >= 0, job < jobs)

    def is_block(block):
        return jnp.logical_and(block >= 0, block < blocks)

    def when(*conditions):
        return pl.when(functools.reduce(jnp.logical_and, conditions))

    def tick(t, carry):
        job = t - 1

        @when(is_job(job))
        def _():
            to_core(job).wait_recv()
            slot = job % MINE
            mine[slot] += core_in[job % SHORT].astype(F32)
            y_out[job % SHORT, 0:PIECE] = mine[slot, pl.ds(pair_down, PIECE)].astype(BF16)
            y_out[job % SHORT, PIECE:2 * PIECE] = mine[slot, pl.ds(pair_up, PIECE)].astype(BF16)
            to_y(job).start()

        @when(is_job(job - LATE))
        def _():
            to_y(job - LATE).wait_send()

        job = t - BASE

        @when(is_job(job))
        def _():
            to_y(job).wait_recv()
            slot = job % MINE
            mine[slot, pl.ds(y_down, PIECE)] += y_in[job % RING, 0:PIECE].astype(F32)
            mine[slot, pl.ds(y_up, PIECE)] += y_in[job % RING, PIECE:2 * PIECE].astype(F32)

        def chain(lag, row, y_place, z_place, hop, arrived, out):
            job = t - BASE - HOP * lag

            @when(is_job(job), lag > 0)
            def _():
                hop(job).wait_recv()
                mine[job % MINE, pl.ds(row, SLAB)] += arrived[job % RING].astype(F32)

            @when(is_job(job), lag < ENDS)
            def _():
                out[job % SHORT] = mine[job % MINE, pl.ds(row, SLAB)].astype(BF16)
                hop(job).start()

            @when(is_job(job - LATE), lag < ENDS)
            def _():
                hop(job - LATE).wait_send()

            @when(is_job(job), lag == ENDS)
            def _():
                ready[job % RING, pl.ds(y_place, PIECE)] = mine[
                    job % MINE, pl.ds(aligned(row + y_place), PIECE)
                ].astype(BF16)
                cross_out[job % SHORT] = mine[
                    job % MINE, pl.ds(aligned(row + z_place), 2 * PIECE)
                ].astype(BF16)
                to_cross(job).start()

            @when(is_job(job - LATE), lag == ENDS)
            def _():
                to_cross(job - LATE).wait_send()

        y_in_down, z_in_down = aligned(2 * PIECE * y), aligned(PIECE * (1 - y))
        y_in_up, z_in_up = aligned(2 * PIECE * (1 - y)), aligned(PIECE * y)
        chain(ENDS - z, down_row, y_in_down, z_in_down, to_down, down_in, down_out)
        chain(z, up_row, y_in_up, z_in_up, to_up, up_in, up_out)

        def spread(lag, row, z_place, hop):
            job = t - BACK - HOP * lag

            @when(is_job(job), lag == 0)
            def _():
                to_cross(job).wait_recv()
                ready[job % RING, pl.ds(z_place, 2 * PIECE)] = (
                    cross_out[job % SHORT].astype(F32) + cross_in[job % RING].astype(F32)
                ).astype(BF16)
                keep_ready(job, row).start()
                hop(job, True).start()

            @when(is_job(job - LATE), lag == 0)
            def _():
                keep_ready(job - LATE, row).wait()
                hop(job - LATE, True).wait_send()

            @when(is_job(job), lag > 0)
            def _():
                hop(job).wait_recv()

            @when(is_job(job), lag > 0, lag < ENDS)
            def _():
                hop(job).start()

            @when(is_job(job - LATE), lag > 0, lag < ENDS)
            def _():
                hop(job - LATE).wait_send()

        spread(z, down_row, z_in_down, from_low)
        spread(ENDS - z, up_row, z_in_up, from_high)

        job = t - PAIR

        @when(is_job(job))
        def _():
            for copy in to_pair(job):
                copy.start()

        @when(is_job(job - LATE))
        def _():
            for copy in to_pair(job - LATE):
                copy.wait_send()

        job = t - TWIN

        @when(is_job(job))
        def _():
            for copy in to_pair(job):
                copy.wait_recv()
            to_twin(job).start()

        @when(is_job(job - LATE))
        def _():
            to_twin(job - LATE).wait_send()

        job = t - TWIN - 1

        @when(is_job(job))
        def _():
            to_twin(job).wait_recv()

        @when(is_job(t - 2))
        def _():
            to_core(t - 2).wait_send()

        @when(is_job(t))
        def _():
            gate, slot = gate_of(t), t % 2
            for copy in load_rows(t):
                copy.wait()

            @pl.when(t + 1 < jobs)
            def _():
                for copy in load_rows(t + 1):
                    copy.start()

            columns = pl.ds(aligned(((t // per_part) % SPLIT) * narrow, narrow), narrow)
            product = jnp.dot(rows_in[slot], du[gate, :, columns], preferred_element_type=F32)
            mine[t % MINE] = product[:JOB_ROWS]
            core_out[slot] = product[JOB_ROWS:].astype(BF16)
            to_core(t).start()

        @pl.when(t < per_gate)
        def _():
            forget_weight = forget_weight_ref[...]

            def back_half(turn, carry):
                load_saved(turn).wait()

                @pl.when(turn + AHEAD - 1 < turns)
                def _():
                    load_saved(turn + AHEAD - 1).start()

                slot = turn % AHEAD
                stretch, start = stretches - 1 - turn // 2, (1 - turn % 2) * HALF

                def group(back, carry):
                    index = HALF // PIECE - 1 - back
                    running = list(carry[:rows_here])
                    weight_sum, bias_sum = carry[rows_here:]
                    out = [([None] * PIECE, [None] * PIECE) for _ in range(rows_here)]
                    for k in range(PIECE - 1, -1, -1):
                        time = index * PIECE + k
                        for row in range(rows_here):
                            direct, extra, forget, slope, before = (saved[slot, kind, row, time] for kind in range(5))
                            kept = keep[row, pl.ds(stretch * size + start + time, 1), :]
                            state_grad = direct + running[row]
                            through = (forget + slope * forget_weight) * kept
                            running[row] = through * state_grad + extra * kept
                            forget_grad = state_grad * slope
                            weight_sum = weight_sum + forget_grad * before
                            bias_sum = bias_sum + forget_grad
                            out[row][0][k] = state_grad - state_grad * forget
                            out[row][1][k] = forget_grad
                    for row in range(rows_here):
                        rows = pl.ds(aligned((stretch * rows_here + row) * size + start + index * PIECE), PIECE)
                        for gate in range(2):
                            du[gate, rows, :] = jnp.stack(out[row][gate]).reshape(PIECE, width).astype(BF16)
                    return (*running, weight_sum, bias_sum)

                return lax.fori_loop(0, HALF // PIECE, group, carry)

            carried = lax.fori_loop(
                t * turns_tick, (t + 1) * turns_tick, back_half,
                (*[state_s[row] for row in range(rows_here)], gate_sums[0], gate_sums[1]),
            )
            for row in range(rows_here):
                state_s[row] = carried[row]
            gate_sums[0] = carried[rows_here]
            gate_sums[1] = carried[rows_here + 1]

        @pl.when(t == 1)
        def _():
            for gate in range(3):
                load_weight(gate).wait()

        block, phase = (t - 1) // (PERIOD * SPLIT), (t - 1) % (PERIOD * SPLIT)
        rows = pl.ds(first_row(block), NORM_TOKENS)

        def split(index):
            each = size // PIECE
            return index // (rows_here * each), (index // each) % rows_here, pl.ds(aligned(index % each * PIECE), PIECE)

        def back(whose, part):
            columns = pl.ds(aligned(whose * width + part * narrow, narrow), narrow)
            return sum(
                lax.dot_general(
                    du[gate, rows, :], weights[gate, columns, :], (((1,), (1,)), ((), ())),
                    preferred_element_type=F32,
                )
                for gate in range(3)
            )

        @when(is_block(block), phase < SPLIT)
        def _():
            columns = pl.ds(aligned(phase * narrow, narrow), narrow)
            dn_out[block % 2, :, columns] = back(1 - ch, phase).astype(BF16)

        @when(is_block(block), phase == SPLIT - 1)
        def _():
            to_partner(block).start()
            for copy in load_norm(block):
                copy.start()

        @when(is_block(block), phase >= SPLIT, phase < 2 * SPLIT)
        def _():
            columns = pl.ds(aligned((phase - SPLIT) * narrow, narrow), narrow)
            dn_own[block % KEPT, :, columns] = back(ch, phase - SPLIT)

        @when(is_block(block - 1), phase == 2 * SPLIT)
        def _():
            now = block - 1
            slot = now % KEPT
            to_partner(now).wait()
            for copy in load_norm(now):
                copy.wait()

            def part(index, sums):
                gain_sum, shift_sum = sums
                rows = pl.ds(aligned(index * PIECE), PIECE)
                piece, row, inner = split(index)
                dn = dn_own[slot, rows, :] + dn_in[now % SHORT, rows, :].astype(F32)
                dn_own[slot, rows, :] = dn
                scale = scale_in[slot, rows, 0:1]
                xhat = (x_in[slot, piece, row, inner, :].astype(F32) - mean_in[slot, rows, 0:1]) * scale
                gained = dn * xhat
                dxhat = dn * gain_ref[0:1, :]
                first = jnp.sum(dxhat, axis=1, keepdims=True)
                second = jnp.sum(dxhat * xhat, axis=1, keepdims=True)
                lane = lax.broadcasted_iota(jnp.int32, (PIECE, LANES), 1)
                moment_out[now % 2, rows, :] = jnp.where(lane < LANES // 2, first, second)
                return (
                    gain_sum + gained[:SUBLANES] + gained[SUBLANES:], shift_sum + dn[:SUBLANES] + dn[SUBLANES:],
                )

            gain_sum, shift_sum = lax.fori_loop(
                0, NORM_TOKENS // PIECE, part, (norm_sums[0], norm_sums[1]), unroll=UNROLL
            )
            norm_sums[0] = gain_sum
            norm_sums[1] = shift_sum
            moments(now).start()

        @when(is_block(block - 2), phase == 3 * SPLIT)
        def _():
            now = block - 2
            slot = now % KEPT
            moments(now).wait()

            @pl.loop(0, NORM_TOKENS // PIECE, unroll=UNROLL)
            def _(index):
                rows = pl.ds(aligned(index * PIECE), PIECE)
                piece, row, inner = split(index)
                both = (moment_out[now % 2, rows, :] + moment_in[now % SHORT, rows, :]) * (1.0 / full)
                first, second = both[:, 0:1], both[:, LANES // 2:LANES // 2 + 1]
                scale = scale_in[slot, rows, 0:1]
                xhat = (x_in[slot, piece, row, inner, :].astype(F32) - mean_in[slot, rows, 0:1]) * scale
                back = scale * (dn_own[slot, rows, :] * gain_ref[0:1, :] - first - xhat * second)
                grad_out[now % 2, piece, row, inner, :] = (back + pass_in[slot, rows, :].astype(F32)).astype(BF16)

            for copy in store_grad(now):
                copy.start()

        @when(is_block(block - 3), phase == 0)
        def _():
            for copy in store_grad(block - 3):
                copy.wait()

        at = PERIOD * SPLIT * (blocks + 1)

        @pl.when(t == at)
        def _():
            small_own[...] = jnp.zeros_like(small_own)
            small_own[0:1] = gate_sums[0].reshape(1, width)
            small_own[1:2] = sums_ref[0].reshape(1, width)
            small_own[2:3] = gate_sums[1].reshape(1, width)
            small_own[3:4] = sums_ref[1].reshape(1, width)
            small_own[4:5] = jnp.sum(norm_sums[0], axis=0, keepdims=True)
            small_own[5:6] = jnp.sum(norm_sums[1], axis=0, keepdims=True)
            small_twin().start()

        @pl.when(t == at + 1)
        def _():
            small_twin().wait()
            small_own[...] += small_in[0]
            small_pair().start()

        @pl.when(t == at + 1 + HOP)
        def _():
            small_pair().wait()
            small_own[...] += small_in[1]
            for away in (1, 2, 3):
                small_column(away).start()

        @pl.when(t == at + 1 + 2 * HOP)
        def _():
            for away in (1, 2, 3):
                small_column(away).wait()
            small_z[z] = small_own[...]
            small_ref[...] = (small_z[0] + small_z[1]) + (small_z[2] + small_z[3])

        return carry

    lax.fori_loop(0, jobs + TWIN + LATE, tick, 0)


def finish(lengths, saved, normed_t, reset, weight, x, mean, scale, passed, gain, forget_weight, sums):
    full, tokens = normed_t.shape
    rows_here, stretches, size, width = x.shape
    dma = pltpu.SemaphoreType.DMA
    vmem = IN_VMEM
    norm = NORM_TOKENS
    narrow = width // SPLIT
    pieces = norm // (rows_here * size)
    return pl.pallas_call(
        finish_kernel,
        out_shape=(
            jax.ShapeDtypeStruct((3, full, width), BF16),
            jax.ShapeDtypeStruct(x.shape, BF16),
            jax.ShapeDtypeStruct((SUBLANES, width), F32),
        ),
        in_specs=[IN_SMEM] + [ANY] * 8 + [vmem] * 3,
        out_specs=(ANY, ANY, vmem),
        scratch_shapes=[
            pltpu.VMEM((3, tokens, width), BF16),
            pltpu.VMEM((3, full, width), BF16),
            pltpu.VMEM((2, 2 * JOB_ROWS, tokens), BF16),
            pltpu.VMEM((MINE, JOB_ROWS, narrow), F32),
            pltpu.VMEM((2, JOB_ROWS, narrow), BF16),
            pltpu.VMEM((SHORT, JOB_ROWS, narrow), BF16),
            pltpu.VMEM((SHORT, 2 * PIECE, narrow), BF16),
            pltpu.VMEM((RING, 2 * PIECE, narrow), BF16),
            pltpu.VMEM((SHORT, SLAB, narrow), BF16),
            pltpu.VMEM((RING, SLAB, narrow), BF16),
            pltpu.VMEM((SHORT, SLAB, narrow), BF16),
            pltpu.VMEM((RING, SLAB, narrow), BF16),
            pltpu.VMEM((SHORT, 2 * PIECE, narrow), BF16),
            pltpu.VMEM((RING, 2 * PIECE, narrow), BF16),
            pltpu.VMEM((RING, SLAB, narrow), BF16),
            pltpu.VMEM((KEPT, norm, width), F32),
            pltpu.VMEM((2, norm, width), BF16),
            pltpu.VMEM((SHORT, norm, width), BF16),
            pltpu.VMEM((2, norm, LANES), F32),
            pltpu.VMEM((SHORT, norm, LANES), F32),
            pltpu.VMEM((KEPT, pieces, rows_here, size, width), BF16),
            pltpu.VMEM((KEPT, norm, width), BF16),
            pltpu.VMEM((KEPT, norm, LANES), F32),
            pltpu.VMEM((KEPT, norm, LANES), F32),
            pltpu.VMEM((2, pieces, rows_here, size, width), BF16),
            pltpu.VMEM((2, SUBLANES, width), F32),
            pltpu.VMEM((rows_here, stretches * size, LANES), F32),
            pltpu.VMEM((AHEAD, 5, rows_here, HALF) + TILE, F32),
            pltpu.VMEM((rows_here,) + TILE, F32),
            pltpu.VMEM((2,) + TILE, F32),
            pltpu.VMEM((SUBLANES, width), F32),
            pltpu.VMEM((2, SUBLANES, width), F32),
            pltpu.VMEM((4, SUBLANES, width), F32),
            dma((4,)), dma((2, 2)), dma((AHEAD,)),
            dma((2,)), dma((SHORT,)), dma((SHORT,)), dma((RING,)), dma((SHORT,)), dma((RING,)),
            dma((SHORT,)), dma((RING,)), dma((SHORT,)), dma((RING,)), dma((RING,)),
            dma((RING,)), dma((RING,)), dma((RING,)), dma((RING,)),
            dma((2, RING)), dma((2, RING)), dma((RING,)), dma((RING,)),
            dma((2,)), dma((SHORT,)), dma((2,)), dma((SHORT,)), dma((3 + pieces, KEPT)), dma((pieces, 2)),
            dma((5,)), dma((5,)),
        ],
        compiler_params=pltpu.CompilerParams(
            collective_id=1, has_side_effects=True, vmem_limit_bytes=VMEM_LIMIT
        ),
        name="finish",
    )(lengths, saved, normed_t, reset, weight, x, mean, scale, passed, gain, forget_weight, sums)


def on_device(
    inputs, doc_lengths, layer_norm_gain, layer_norm_bias, weight, forget_weight, reset_weight, forget_bias,
    reset_bias, out_grad,
):
    rows_here, length, width = inputs.shape
    weights = jnp.transpose(weight, (1, 0, 2))
    stretched = (rows_here, length // STRETCH, STRETCH, width)
    x = inputs.reshape(stretched)
    gain = layer_norm_gain.reshape(1, width)
    vectors = [vector.reshape(TILE) for vector in (forget_weight, reset_weight, forget_bias, reset_bias)]
    saved, normed_t, mean, scale, mixed, passed, reset_grad, final_state, sums = project(
        doc_lengths, x, gain, layer_norm_bias.reshape(1, width), weights, out_grad.reshape(stretched), *vectors
    )
    weight_grad, input_grad, small = finish(
        doc_lengths, saved, normed_t, reset_grad, weights, x, mean, scale, passed, gain, vectors[0], sums
    )
    weight_grad = weight_grad.astype(F32)
    devices = lax.axis_size("rows")
    groups = devices // 16
    if groups > 1:
        members = [[] for _ in range(devices // groups)]
        for device in range(devices):
            part, core = device // 2, device % 2
            members[(part // groups) * 2 + core].append(device)
        weight_grad, small = lax.psum((weight_grad, small), "rows", axis_index_groups=members)
    weight_grad = jnp.transpose(weight_grad, (1, 0, 2))
    return (
        mixed.reshape(inputs.shape), input_grad.reshape(inputs.shape), final_state, weight_grad,
        small[4], small[5], small[0], small[1], small[2], small[3],
    )


def solution(mesh):
    rows_ch = P("rows", None, "ch")
    ch = P("ch")
    in_specs = (rows_ch, P("rows", None), ch, ch, P(None, None, "ch"), ch, ch, ch, ch, rows_ch)
    out_specs = (rows_ch, rows_ch, P("rows", "ch"), P(None, None, "ch"), ch, ch, ch, ch, ch, ch)
    return jax.shard_map(on_device, mesh=mesh, in_specs=in_specs, out_specs=out_specs, check_vma=False)
```

```python
import functools

import jax
import jax.numpy as jnp
from jax import lax
from jax.experimental import pallas as pl
from jax.experimental.pallas import tpu as pltpu
from jax.sharding import PartitionSpec as P

MESH = pl.DeviceIdType.MESH
F32 = jnp.float32
BF16 = jnp.bfloat16
EPSILON = 1e-05
LANES = 128
SUBLANES = 8
TILE = (SUBLANES, LANES)
STRETCH = 64
GROUP = 16
ANY = pl.BlockSpec(memory_space=pl.ANY)
IN_VMEM = pl.BlockSpec(memory_space=pltpu.VMEM)
IN_SMEM = pl.BlockSpec(memory_space=pltpu.SMEM)
VMEM_LIMIT = 60 * 1024 * 1024


def aligned(value, size=GROUP):
    return pl.multiple_of(value, size)


def fill_keep(lengths_ref, keep):
    rows_here, length = keep.shape[0], keep.shape[1]
    for row in range(rows_here):
        starts = [jnp.int32(0)]
        for document in range(lengths_ref.shape[1] - 1):
            starts.append(starts[-1] + lengths_ref[row, document])

        @pl.loop(0, length // LANES)
        def _(part):
            place = lax.broadcasted_iota(jnp.int32, (LANES, LANES), 0) + part * LANES
            value = jnp.ones((LANES, LANES), F32)
            for start in starts:
                value = jnp.where(place == start, 0.0, value)
            keep[row, pl.ds(aligned(part * LANES, LANES), LANES), :] = value


def project_kernel(
    lengths_ref, x_ref, gain_ref, shift_ref, weight_ref, grad_ref,
    forget_weight_ref, reset_weight_ref, forget_bias_ref, reset_bias_ref,
    saved_ref, forget_ref, normed_t_ref, mean_ref, scale_ref, mixed_ref, pass_ref, reset_ref, final_ref, sums_ref,
    both, weights, params, keep, normed, normed_t, mean_out, scale_out, u, grad_in, saved, forget_out, mixed_out, pass_out,
    reset_out, state_s,
    send_sem, recv_sem, own_sem, param_own, param_send, param_recv, weight_sem, grad_sem, out_sem,
):
    ch = lax.axis_index("ch")
    other = 1 - ch
    rows_here, stretches, size, width = x_ref.shape
    full = 2 * width
    tokens = rows_here * size
    own_columns = pl.ds(aligned(ch * width, width), width)

    load_weight = pltpu.make_async_copy(weight_ref, weights, weight_sem)

    def params_of(index, source):
        return (
            pltpu.make_async_copy(source, params.at[ch, index], param_own.at[index]),
            pltpu.make_async_remote_copy(
                src_ref=source, dst_ref=params.at[ch, index], send_sem=param_send.at[index],
                recv_sem=param_recv.at[index], device_id={"ch": other}, device_id_type=MESH,
            ),
        )

    def exchange(stretch):
        return pltpu.make_async_remote_copy(
            src_ref=x_ref.at[:, stretch], dst_ref=both.at[:, stretch, :, own_columns],
            send_sem=send_sem.at[stretch], recv_sem=recv_sem.at[stretch],
            device_id={"ch": other}, device_id_type=MESH,
        )

    def keep_own(stretch):
        return pltpu.make_async_copy(x_ref.at[:, stretch], both.at[:, stretch, :, own_columns], own_sem.at[stretch])

    def load_grad(stretch):
        slot = stretch % 2
        return pltpu.make_async_copy(grad_ref.at[:, stretch], grad_in.at[slot], grad_sem.at[slot])

    def outputs(stretch):
        slot = stretch % 2
        rows = pl.ds(aligned(stretch * tokens, tokens), tokens)
        return tuple(
            pltpu.make_async_copy(source.at[slot], target, out_sem.at[index, slot])
            for index, (source, target) in enumerate((
                (saved, saved_ref.at[stretch]), (forget_out, forget_ref.at[stretch]), (normed_t, normed_t_ref.at[:, rows]), (mean_out, mean_ref.at[rows]),
                (scale_out, scale_ref.at[rows]), (mixed_out, mixed_ref.at[:, stretch]), (pass_out, pass_ref.at[rows]),
                (reset_out, reset_ref.at[rows]),
            ))
        )

    load_weight.start()
    load_grad(0).start()
    barrier = pltpu.get_barrier_semaphore()
    pl.semaphore_signal(barrier, inc=1, device_id={"ch": other}, device_id_type=MESH)
    pl.semaphore_wait(barrier, 1)
    for index, source in enumerate((gain_ref, shift_ref)):
        for copy in params_of(index, source):
            copy.start()

    def begin(stretch, carry):
        exchange(stretch).start()
        keep_own(stretch).start()
        return carry

    lax.fori_loop(0, stretches, begin, 0)
    fill_keep(lengths_ref, keep)
    state_s[...] = jnp.zeros_like(state_s)
    sums_ref[...] = jnp.zeros_like(sums_ref)
    for index, source in enumerate((gain_ref, shift_ref)):
        for copy in params_of(index, source):
            copy.wait()
    load_weight.wait()

    def work(stretch, carry):
        slot = stretch % 2
        keep_own(stretch).wait()
        exchange(stretch).wait()
        load_grad(stretch).wait()

        @pl.when(stretch + 1 < stretches)
        def _():
            load_grad(stretch + 1).start()

        @pl.when(stretch >= 2)
        def _():
            for copy in outputs(stretch - 2):
                copy.wait()

        for row in range(rows_here):
            @pl.loop(0, size // GROUP, unroll=2)
            def _(part):
                here = pl.ds(aligned(part * GROUP), GROUP)
                there = pl.ds(aligned(row * size + part * GROUP), GROUP)
                x = both[row, stretch, here, :].astype(F32)
                mean = jnp.sum(x, axis=1, keepdims=True) * (1.0 / full)
                centered = x - mean
                variance = jnp.sum(centered * centered, axis=1, keepdims=True) * (1.0 / full)
                scale = lax.rsqrt(variance + EPSILON)
                gain = jnp.concatenate([params[0, 0], params[1, 0]], axis=1)
                shift = jnp.concatenate([params[0, 1], params[1, 1]], axis=1)
                normed[there, :] = (centered * scale * gain + shift).astype(BF16)
                mean_out[slot, there, :] = jnp.broadcast_to(mean, (GROUP, LANES))
                scale_out[slot, there, :] = jnp.broadcast_to(scale, (GROUP, LANES))

        for gate in range(3):
            u[gate] = jnp.dot(normed[...], weights[gate], preferred_element_type=F32)

        for part in range(full // LANES):
            columns = slice(part * LANES, (part + 1) * LANES)
            normed_t[slot, columns, :] = normed[:, columns].T

        forget_weight = 0.5 * forget_weight_ref[...]
        half_reset_weight = 0.5 * reset_weight_ref[...]
        forget_bias = 0.5 * forget_bias_ref[...]
        reset_bias = 0.5 * reset_bias_ref[...]

        def group(index, carry):
            state = list(carry[:rows_here])
            weight_sum, bias_sum = carry[rows_here:]
            here = pl.ds(aligned(index * GROUP), GROUP)
            there = [pl.ds(aligned(row * size + index * GROUP), GROUP) for row in range(rows_here)]
            spread = lambda value: value.astype(F32).reshape((GROUP,) + TILE)
            loaded = [
                (
                    spread(u[0, there[row], :]), spread(u[1, there[row], :]), spread(u[2, there[row], :]),
                    spread(both[row, stretch, here, own_columns]), spread(grad_in[slot, row, here, :]),
                )
                for row in range(rows_here)
            ]
            out = [([], [], []) for _ in range(rows_here)]
            held = [None] * rows_here
            for k in range(GROUP):
                time = index * GROUP + k
                for row in range(rows_here):
                    up_x, up_f, up_r, x, grad = (part[k] for part in loaded[row])
                    before = state[row] * keep[row, pl.ds(stretch * size + time, 1), :]
                    bent = jnp.tanh(0.5 * up_f + forget_bias + forget_weight * before)
                    gap = before - up_x
                    after = 0.5 * (before + up_x) + bent * (0.5 * gap)
                    state[row] = after
                    forget = 0.5 * bent + 0.5
                    reset = 0.5 * jnp.tanh(0.5 * up_r + reset_bias + half_reset_weight * before) + 0.5
                    over = after - x
                    direct = grad * reset
                    reset_grad = direct * over * (1.0 - reset)
                    forget_out[slot, row, time] = forget
                    kinds = (direct, gap * forget * (1.0 - forget), before)
                    if k % 2 == 0:
                        held[row] = kinds
                    else:
                        for kind in range(3):
                            both_steps = jnp.concatenate([held[row][kind], kinds[kind]], axis=0)
                            saved[slot, kind, row, index * (GROUP // 2) + k // 2] = both_steps.astype(BF16)
                    weight_sum = weight_sum + reset_grad * before
                    bias_sum = bias_sum + reset_grad
                    out[row][0].append(x + reset * over)
                    out[row][1].append(grad - direct)
                    out[row][2].append(reset_grad)
            flat = lambda parts: jnp.stack(parts).reshape(GROUP, width).astype(BF16)
            for row in range(rows_here):
                mixed_out[slot, row, here, :] = flat(out[row][0])
                pass_out[slot, there[row], :] = flat(out[row][1])
                reset_out[slot, there[row], :] = flat(out[row][2])
            return (*state, weight_sum, bias_sum)

        carried = lax.fori_loop(
            0, size // GROUP, group, (*[state_s[row] for row in range(rows_here)], sums_ref[0], sums_ref[1])
        )
        for row in range(rows_here):
            state_s[row] = carried[row]
        sums_ref[0] = carried[rows_here]
        sums_ref[1] = carried[rows_here + 1]
        for copy in outputs(stretch):
            copy.start()
        return carry

    lax.fori_loop(0, stretches, work, 0)
    for row in range(rows_here):
        final_ref[row:row + 1, :] = state_s[row].reshape(1, width)
    for stretch in (stretches - 2, stretches - 1):
        for copy in outputs(stretch):
            copy.wait()


def project(lengths, x, gain, shift, weight, grad, forget_weight, reset_weight, forget_bias, reset_bias):
    rows_here, stretches, size, width = x.shape
    full = 2 * width
    part = rows_here * size
    tokens = part * stretches
    kept = (3, rows_here, size // 2, 2 * SUBLANES, LANES)
    kept_forget = (rows_here, size) + TILE
    dma = pltpu.SemaphoreType.DMA
    shape = jax.ShapeDtypeStruct
    return pl.pallas_call(
        project_kernel,
        out_shape=(
            shape((stretches,) + kept, BF16),
            shape((stretches,) + kept_forget, F32),
            shape((full, tokens), BF16),
            shape((tokens, LANES), F32),
            shape((tokens, LANES), F32),
            shape(x.shape, BF16),
            shape((tokens, width), BF16),
            shape((tokens, width), BF16),
            shape((rows_here, width), F32),
            shape((2,) + TILE, F32),
        ),
        in_specs=[IN_SMEM] + [ANY] * 5 + [IN_VMEM] * 4,
        out_specs=[ANY] * 8 + [IN_VMEM] * 2,
        scratch_shapes=[
            pltpu.VMEM((rows_here, stretches, size, full), BF16),
            pltpu.VMEM((3, full, width), BF16),
            pltpu.VMEM((2, 2, 1, width), F32),
            pltpu.VMEM((rows_here, stretches * size, LANES), F32),
            pltpu.VMEM((part, full), BF16),
            pltpu.VMEM((2, full, part), BF16),
            pltpu.VMEM((2, part, LANES), F32),
            pltpu.VMEM((2, part, LANES), F32),
            pltpu.VMEM((3, part, width), F32),
            pltpu.VMEM((2, rows_here, size, width), BF16),
            pltpu.VMEM((2,) + kept, BF16),
            pltpu.VMEM((2,) + kept_forget, F32),
            pltpu.VMEM((2, rows_here, size, width), BF16),
            pltpu.VMEM((2, part, width), BF16),
            pltpu.VMEM((2, part, width), BF16),
            pltpu.VMEM((rows_here,) + TILE, F32),
            dma((stretches,)), dma((stretches,)), dma((stretches,)), dma((2,)), dma((2,)), dma((2,)), dma, dma((2,)),
            dma((8, 2)),
        ],
        compiler_params=pltpu.CompilerParams(
            collective_id=0, has_side_effects=True, vmem_limit_bytes=VMEM_LIMIT
        ),
        name="project",
    )(lengths, x, gain, shift, weight, grad, forget_weight, reset_weight, forget_bias, reset_bias)


JOB_ROWS = 128
PIECE = 16
SLAB = 48
NORM_TOKENS = 256
HALF = 32
RING = 8
SHORT = 4
ENDS = 3
SPLIT = 1
UNROLL = 4
HOP = 2
BASE = 1 + HOP
BACK = BASE + (ENDS + 1) * HOP
PAIR = BACK + ENDS * HOP
TWIN = PAIR + HOP
LATE = 3
MINE = BASE + ENDS * HOP + 1
PERIOD = 3
OFFSET = 8
MEET = 2
LEAVE = 3
KEPT = 3
AHEAD = 4


def finish_kernel(
    lengths_ref, saved_ref, forget_ref, normed_t_ref, reset_ref, weight_ref, x_ref, mean_ref, scale_ref, pass_ref, gain_ref,
    forget_weight_ref, reset_weight_ref, sums_ref,
    total_ref, input_grad_ref, small_ref,
    du, weights, rows_in, mine, core_out, core_in, y_out, y_in, down_out, down_in, up_out, up_in, cross_out, cross_in,
    ready, dn_own, dn_out, dn_in, moment_own, moment_out, moment_in, x_in, pass_in, mean_in, scale_in, grad_out,
    norm_sums, keep, saved, forgets, state_s, gate_sums, small_own, small_in, small_z,
    load_sem, rows_sem, saved_sem, core_send, core_recv, y_send, y_recv, down_send, down_recv, up_send, up_recv,
    cross_send, cross_recv, ready_sem, from_low_send, from_low_recv, from_high_send, from_high_recv,
    pair_send, pair_recv, twin_send, twin_recv, dn_send, dn_recv, moment_send, moment_recv, norm_sem, grad_sem,
    small_send, small_recv,
):
    device = lax.axis_index("rows")
    devices = lax.axis_size("rows")
    ch = lax.axis_index("ch")
    z_stride, y_stride = devices // 4, devices // 8
    z = device // z_stride
    y = (device // y_stride) % 2
    core = device % 2
    twin = device + 1 - 2 * core
    pair = device + y_stride * (1 - 2 * y)
    full, tokens = normed_t_ref.shape
    rows_here, stretches, size, width = x_ref.shape
    half = full // 2
    narrow = width // SPLIT
    per_part = half // JOB_ROWS
    per_gate = per_part * SPLIT
    jobs = 3 * per_gate
    blocks = tokens // NORM_TOKENS

    def gate_of(job):
        return (job // per_gate + 2) % 3

    def place(job, whose):
        row = aligned(whose * half + (job // SPLIT % per_part) * JOB_ROWS, JOB_ROWS)
        column = aligned((job % SPLIT) * narrow, narrow)
        return gate_of(job), row, column

    down_row = aligned(PIECE * y)
    up_row = aligned(80 - PIECE * y)
    y_down, y_up = aligned(SLAB * y), aligned(112 - SLAB * y)
    pair_down, pair_up = aligned(SLAB * (1 - y)), aligned(112 - SLAB * (1 - y))

    load_reset = pltpu.make_async_copy(reset_ref, du.at[2], load_sem.at[3])

    def load_weight(gate):
        return pltpu.make_async_copy(weight_ref.at[gate], weights.at[gate], load_sem.at[gate])

    def load_rows(turn):
        slot = turn % 2
        own = aligned(core * half + (turn % per_part) * JOB_ROWS, JOB_ROWS)
        other = aligned((1 - core) * half + (turn % per_part) * JOB_ROWS, JOB_ROWS)
        return (
            pltpu.make_async_copy(
                normed_t_ref.at[pl.ds(own, JOB_ROWS)], rows_in.at[slot, pl.ds(0, JOB_ROWS)], rows_sem.at[0, slot]
            ),
            pltpu.make_async_copy(
                normed_t_ref.at[pl.ds(other, JOB_ROWS)], rows_in.at[slot, pl.ds(JOB_ROWS, JOB_ROWS)],
                rows_sem.at[1, slot],
            ),
        )

    def remote(source, target, send, recv, where):
        return pltpu.make_async_remote_copy(
            src_ref=source, dst_ref=target, send_sem=send, recv_sem=recv, device_id=where, device_id_type=MESH
        )

    def to_core(job):
        return remote(
            core_out.at[job % 2], core_in.at[job % SHORT], core_send.at[job % 2], core_recv.at[job % SHORT],
            {"rows": twin},
        )

    def to_y(job):
        return remote(
            y_out.at[job % SHORT], y_in.at[job % RING], y_send.at[job % SHORT], y_recv.at[job % RING], {"rows": pair}
        )

    def to_down(job):
        return remote(
            down_out.at[job % SHORT], down_in.at[job % RING], down_send.at[job % SHORT], down_recv.at[job % RING],
            {"rows": device - z_stride},
        )

    def to_up(job):
        return remote(
            up_out.at[job % SHORT], up_in.at[job % RING], up_send.at[job % SHORT], up_recv.at[job % RING],
            {"rows": device + z_stride},
        )

    def to_cross(job):
        return remote(
            cross_out.at[job % SHORT], cross_in.at[job % RING], cross_send.at[job % SHORT], cross_recv.at[job % RING],
            {"rows": pair},
        )

    def result(job, offset, size, whose):
        gate, row, column = place(job, whose)
        return total_ref.at[gate, pl.ds(aligned(row + offset), size), pl.ds(column, narrow)]

    def keep_ready(job, offset):
        return pltpu.make_async_copy(
            ready.at[job % RING], result(job, offset, SLAB, core), ready_sem.at[job % RING]
        )

    def gather(job, offset, source, send, recv, where):
        return remote(source, result(job, offset, SLAB, core), send.at[job % RING], recv.at[job % RING], where)

    def from_low(job, first=False):
        source = ready.at[job % RING] if first else result(job, down_row, SLAB, core)
        return gather(job, down_row, source, from_low_send, from_low_recv, {"rows": device + z_stride})

    def from_high(job, first=False):
        source = ready.at[job % RING] if first else result(job, up_row, SLAB, core)
        return gather(job, up_row, source, from_high_send, from_high_recv, {"rows": device - z_stride})

    def to_pair(job):
        return tuple(
            remote(
                result(job, row, PIECE, core), result(job, row, PIECE, core),
                pair_send.at[side, job % RING], pair_recv.at[side, job % RING], {"rows": pair},
            )
            for side, row in enumerate((y_down, y_up))
        )

    def to_twin(job):
        return remote(
            result(job, 0, JOB_ROWS, core), result(job, 0, JOB_ROWS, core),
            twin_send.at[job % RING], twin_recv.at[job % RING], {"rows": twin},
        )

    def to_partner(block):
        return remote(
            dn_out.at[block % KEPT], dn_in.at[block % RING], dn_send.at[block % KEPT], dn_recv.at[block % RING],
            {"ch": 1 - ch},
        )

    def moments(block):
        return remote(
            moment_out.at[block % 2], moment_in.at[block % RING], moment_send.at[block % 2],
            moment_recv.at[block % RING], {"ch": 1 - ch},
        )

    pieces = NORM_TOKENS // (rows_here * size)

    def first_row(block):
        return aligned(tokens - NORM_TOKENS * (block + 1), NORM_TOKENS)

    def load_norm(block):
        rows = pl.ds(first_row(block), NORM_TOKENS)
        slot = block % KEPT
        return tuple(
            pltpu.make_async_copy(source.at[rows], target.at[slot], norm_sem.at[index, slot])
            for index, (source, target) in enumerate(((pass_ref, pass_in), (mean_ref, mean_in), (scale_ref, scale_in)))
        ) + tuple(
            pltpu.make_async_copy(
                x_ref.at[:, stretches - pieces * (block + 1) + piece], x_in.at[slot, piece],
                norm_sem.at[3 + piece, slot],
            )
            for piece in range(pieces)
        )

    def store_grad(block):
        return tuple(
            pltpu.make_async_copy(
                grad_out.at[block % 2, piece], input_grad_ref.at[:, stretches - pieces * (block + 1) + piece],
                grad_sem.at[piece, block % 2],
            )
            for piece in range(pieces)
        )

    def load_saved(turn):
        slot, stretch, part = turn % AHEAD, stretches - 1 - turn // 2, 1 - turn % 2
        return (
            pltpu.make_async_copy(
                saved_ref.at[stretch, :, :, pl.ds(aligned(part * (HALF // 2), HALF // 2), HALF // 2)],
                saved.at[slot], saved_sem.at[0, slot],
            ),
            pltpu.make_async_copy(
                forget_ref.at[stretch, :, pl.ds(aligned(part * HALF, HALF), HALF)], forgets.at[slot],
                saved_sem.at[1, slot],
            ),
        )

    def small_twin():
        return remote(small_own, small_in.at[0], small_send.at[0], small_recv.at[0], {"rows": twin})

    def small_pair():
        return remote(small_own, small_in.at[1], small_send.at[1], small_recv.at[1], {"rows": pair})

    def small_column(away):
        there = (z + away) % 4
        return remote(
            small_own, small_z.at[z], small_send.at[1 + away], small_recv.at[1 + away],
            {"rows": device + (there - z) * z_stride},
        )

    load_reset.start()
    for copy in load_rows(0):
        copy.start()
    for turn in range(AHEAD - 1):
        for copy in load_saved(turn):
            copy.start()

    barrier = pltpu.get_barrier_semaphore()
    for where in [{"rows": twin}, {"rows": pair}, {"ch": 1 - ch}] + [
        {"rows": device + ((z + away) % 4 - z) * z_stride} for away in (1, 2, 3)
    ]:
        pl.semaphore_signal(barrier, inc=1, device_id=where, device_id_type=MESH)
    pl.semaphore_wait(barrier, 6)
    norm_sums[...] = jnp.zeros_like(norm_sums)
    state_s[...] = jnp.zeros_like(state_s)
    gate_sums[...] = jnp.zeros_like(gate_sums)
    fill_keep(lengths_ref, keep)
    turns = 2 * stretches
    turns_tick = turns // per_gate
    load_reset.wait()
    for gate in range(3):
        load_weight(gate).start()

    def is_job(job):
        return jnp.logical_and(job >= 0, job < jobs)

    def is_block(block):
        return jnp.logical_and(block >= 0, block < blocks)

    def when(*conditions):
        return pl.when(functools.reduce(jnp.logical_and, conditions))

    def tick(t, carry):
        job = t - 1

        @when(is_job(job))
        def _():
            to_core(job).wait_recv()
            slot = job % MINE
            mine[slot] += core_in[job % SHORT].astype(F32)
            y_out[job % SHORT, 0:PIECE] = mine[slot, pl.ds(pair_down, PIECE)].astype(BF16)
            y_out[job % SHORT, PIECE:2 * PIECE] = mine[slot, pl.ds(pair_up, PIECE)].astype(BF16)
            to_y(job).start()

        @when(is_job(job - LATE))
        def _():
            to_y(job - LATE).wait_send()

        job = t - BASE

        @when(is_job(job))
        def _():
            to_y(job).wait_recv()
            slot = job % MINE
            mine[slot, pl.ds(y_down, PIECE)] += y_in[job % RING, 0:PIECE].astype(F32)
            mine[slot, pl.ds(y_up, PIECE)] += y_in[job % RING, PIECE:2 * PIECE].astype(F32)

        def chain(lag, row, y_place, z_place, hop, arrived, out):
            job = t - BASE - HOP * lag

            @when(is_job(job), lag > 0)
            def _():
                hop(job).wait_recv()
                mine[job % MINE, pl.ds(row, SLAB)] += arrived[job % RING].astype(F32)

            @when(is_job(job), lag < ENDS)
            def _():
                out[job % SHORT] = mine[job % MINE, pl.ds(row, SLAB)].astype(BF16)
                hop(job).start()

            @when(is_job(job - LATE), lag < ENDS)
            def _():
                hop(job - LATE).wait_send()

            @when(is_job(job), lag == ENDS)
            def _():
                ready[job % RING, pl.ds(y_place, PIECE)] = mine[
                    job % MINE, pl.ds(aligned(row + y_place), PIECE)
                ].astype(BF16)
                cross_out[job % SHORT] = mine[
                    job % MINE, pl.ds(aligned(row + z_place), 2 * PIECE)
                ].astype(BF16)
                to_cross(job).start()

            @when(is_job(job - LATE), lag == ENDS)
            def _():
                to_cross(job - LATE).wait_send()

        y_in_down, z_in_down = aligned(2 * PIECE * y), aligned(PIECE * (1 - y))
        y_in_up, z_in_up = aligned(2 * PIECE * (1 - y)), aligned(PIECE * y)
        chain(ENDS - z, down_row, y_in_down, z_in_down, to_down, down_in, down_out)
        chain(z, up_row, y_in_up, z_in_up, to_up, up_in, up_out)

        def spread(lag, row, z_place, hop):
            job = t - BACK - HOP * lag

            @when(is_job(job), lag == 0)
            def _():
                to_cross(job).wait_recv()
                ready[job % RING, pl.ds(z_place, 2 * PIECE)] = (
                    cross_out[job % SHORT].astype(F32) + cross_in[job % RING].astype(F32)
                ).astype(BF16)
                keep_ready(job, row).start()
                hop(job, True).start()

            @when(is_job(job - LATE), lag == 0)
            def _():
                keep_ready(job - LATE, row).wait()
                hop(job - LATE, True).wait_send()

            @when(is_job(job), lag > 0)
            def _():
                hop(job).wait_recv()

            @when(is_job(job), lag > 0, lag < ENDS)
            def _():
                hop(job).start()

            @when(is_job(job - LATE), lag > 0, lag < ENDS)
            def _():
                hop(job - LATE).wait_send()

        spread(z, down_row, z_in_down, from_low)
        spread(ENDS - z, up_row, z_in_up, from_high)

        job = t - PAIR

        @when(is_job(job))
        def _():
            for copy in to_pair(job):
                copy.start()

        @when(is_job(job - LATE))
        def _():
            for copy in to_pair(job - LATE):
                copy.wait_send()

        job = t - TWIN

        @when(is_job(job))
        def _():
            for copy in to_pair(job):
                copy.wait_recv()
            to_twin(job).start()

        @when(is_job(job - LATE))
        def _():
            to_twin(job - LATE).wait_send()

        job = t - TWIN - 1

        @when(is_job(job))
        def _():
            to_twin(job).wait_recv()

        @when(is_job(t - 2))
        def _():
            to_core(t - 2).wait_send()

        @when(is_job(t))
        def _():
            gate, slot, turn = gate_of(t), t % 2, t // SPLIT

            @pl.when(t % SPLIT == 0)
            def _():
                for copy in load_rows(turn):
                    copy.wait()

            @when(t % SPLIT == 0, t + SPLIT < jobs)
            def _():
                for copy in load_rows(turn + 1):
                    copy.start()

            columns = pl.ds(aligned((t % SPLIT) * narrow, narrow), narrow)
            product = jnp.dot(rows_in[turn % 2], du[gate, :, columns], preferred_element_type=F32)
            mine[t % MINE] = product[:JOB_ROWS]
            core_out[slot] = product[JOB_ROWS:].astype(BF16)
            to_core(t).start()

        @pl.when(t < per_gate)
        def _():
            forget_weight = forget_weight_ref[...]
            reset_weight = reset_weight_ref[...]

            def back_half(turn, carry):
                for copy in load_saved(turn):
                    copy.wait()

                @pl.when(turn + AHEAD - 1 < turns)
                def _():
                    for copy in load_saved(turn + AHEAD - 1):
                        copy.start()

                slot = turn % AHEAD
                stretch, start = stretches - 1 - turn // 2, (1 - turn % 2) * HALF

                def group(back, carry):
                    index = HALF // PIECE - 1 - back
                    running = list(carry[:rows_here])
                    weight_sum, bias_sum = carry[rows_here:]
                    out = [([None] * PIECE, [None] * PIECE) for _ in range(rows_here)]
                    rows = [
                        pl.ds(aligned((stretch * rows_here + row) * size + start + index * PIECE), PIECE)
                        for row in range(rows_here)
                    ]
                    resets = [du[2, rows[row], :].astype(F32).reshape((PIECE,) + TILE) for row in range(rows_here)]
                    pairs = [None] * rows_here
                    for k in range(PIECE - 1, -1, -1):
                        time = index * PIECE + k
                        for row in range(rows_here):
                            if k % 2:
                                pairs[row] = [
                                    saved[slot, kind, row, index * (PIECE // 2) + k // 2].astype(F32)
                                    for kind in range(3)
                                ]
                            lanes = slice(SUBLANES, 2 * SUBLANES) if k % 2 else slice(0, SUBLANES)
                            direct, slope, before = (pair[lanes] for pair in pairs[row])
                            forget = forgets[slot, row, time]
                            kept = keep[row, pl.ds(stretch * size + start + time, 1), :]
                            state_grad = direct + running[row]
                            through = (forget + slope * forget_weight) * kept
                            running[row] = through * state_grad + resets[row][k] * reset_weight * kept
                            forget_grad = state_grad * slope
                            weight_sum = weight_sum + forget_grad * before
                            bias_sum = bias_sum + forget_grad
                            out[row][0][k] = state_grad - state_grad * forget
                            out[row][1][k] = forget_grad
                    for row in range(rows_here):
                        for gate in range(2):
                            du[gate, rows[row], :] = jnp.stack(out[row][gate]).reshape(PIECE, width).astype(BF16)
                    return (*running, weight_sum, bias_sum)

                return lax.fori_loop(0, HALF // PIECE, group, carry)

            carried = lax.fori_loop(
                t * turns_tick, (t + 1) * turns_tick, back_half,
                (*[state_s[row] for row in range(rows_here)], gate_sums[0], gate_sums[1]),
            )
            for row in range(rows_here):
                state_s[row] = carried[row]
            gate_sums[0] = carried[rows_here]
            gate_sums[1] = carried[rows_here + 1]

        @pl.when(t == OFFSET)
        def _():
            for gate in range(3):
                load_weight(gate).wait()

        block, phase = (t - OFFSET) // PERIOD, (t - OFFSET) % PERIOD

        def split(index):
            each = size // PIECE
            return index // (rows_here * each), (index // each) % rows_here, pl.ds(aligned(index % each * PIECE), PIECE)

        def back(block, whose, part):
            rows = pl.ds(first_row(block), NORM_TOKENS)
            columns = pl.ds(aligned(whose * width + part * narrow, narrow), narrow)
            return sum(
                lax.dot_general(
                    du[gate, rows, :], weights[gate, columns, :], (((1,), (1,)), ((), ())),
                    preferred_element_type=F32,
                )
                for gate in range(3)
            )

        @when(is_block(block), phase < SPLIT)
        def _():
            columns = pl.ds(aligned(phase * narrow, narrow), narrow)
            dn_out[block % KEPT, :, columns] = back(block, 1 - ch, phase).astype(BF16)

        @when(is_block(block), phase == SPLIT - 1)
        def _():
            to_partner(block).start()

        @when(is_block(block - MEET + 1), phase == SPLIT)
        def _():
            for copy in load_norm(block - MEET + 1):
                copy.start()

        @when(is_block(block - MEET), phase >= SPLIT, phase < 2 * SPLIT)
        def _():
            columns = pl.ds(aligned((phase - SPLIT) * narrow, narrow), narrow)
            dn_own[(block - MEET) % KEPT, :, columns] = back(block - MEET, ch, phase - SPLIT)

        @when(is_block(block - MEET), phase == 2 * SPLIT)
        def _():
            now = block - MEET
            slot = now % KEPT
            to_partner(now).wait()
            for copy in load_norm(now):
                copy.wait()

            def part(index, sums):
                gain_sum, shift_sum = sums
                rows = pl.ds(aligned(index * PIECE), PIECE)
                piece, row, inner = split(index)
                dn = dn_own[slot, rows, :] + dn_in[now % RING, rows, :].astype(F32)
                dn_own[slot, rows, :] = dn
                scale = scale_in[slot, rows, 0:1]
                xhat = (x_in[slot, piece, row, inner, :].astype(F32) - mean_in[slot, rows, 0:1]) * scale
                gained = dn * xhat
                dxhat = dn * gain_ref[0:1, :]
                first = jnp.sum(dxhat, axis=1, keepdims=True)
                second = jnp.sum(dxhat * xhat, axis=1, keepdims=True)
                lane = lax.broadcasted_iota(jnp.int32, (PIECE, LANES), 1)
                moment_own[rows, :] = jnp.where(lane == 0, first, second)
                return (
                    gain_sum + gained[:SUBLANES] + gained[SUBLANES:], shift_sum + dn[:SUBLANES] + dn[SUBLANES:],
                )

            gain_sum, shift_sum = lax.fori_loop(
                0, NORM_TOKENS // PIECE, part, (norm_sums[0], norm_sums[1]), unroll=UNROLL
            )
            norm_sums[0] = gain_sum
            norm_sums[1] = shift_sum
            for part in range(NORM_TOKENS // LANES):
                moment_out[now % 2, part] = moment_own[part * LANES:(part + 1) * LANES, :].T[:SUBLANES]
            moments(now).start()

        @when(is_block(block - LEAVE), phase == PERIOD - 1)
        def _():
            now = block - LEAVE
            slot = now % KEPT
            moments(now).wait()
            for part in range(NORM_TOKENS // LANES):
                both = (moment_out[now % 2, part] + moment_in[now % RING, part]) * (1.0 / full)
                moment_own[part * LANES:(part + 1) * LANES, :] = jnp.concatenate([both] * (LANES // SUBLANES), axis=0).T

            @pl.loop(0, NORM_TOKENS // PIECE, unroll=UNROLL)
            def _(index):
                rows = pl.ds(aligned(index * PIECE), PIECE)
                piece, row, inner = split(index)
                first, second = moment_own[rows, 0:1], moment_own[rows, 1:2]
                scale = scale_in[slot, rows, 0:1]
                xhat = (x_in[slot, piece, row, inner, :].astype(F32) - mean_in[slot, rows, 0:1]) * scale
                back = scale * (dn_own[slot, rows, :] * gain_ref[0:1, :] - first - xhat * second)
                grad_out[now % 2, piece, row, inner, :] = (back + pass_in[slot, rows, :].astype(F32)).astype(BF16)

            for copy in store_grad(now):
                copy.start()

        @when(is_block(block - LEAVE - 1), phase == 0)
        def _():
            for copy in store_grad(block - LEAVE - 1):
                copy.wait()

        at = OFFSET + PERIOD * (blocks - 1 + MEET) + 2 * SPLIT + 1

        @pl.when(t == at)
        def _():
            small_own[...] = jnp.zeros_like(small_own)
            small_own[0:1] = gate_sums[0].reshape(1, width)
            small_own[1:2] = sums_ref[0].reshape(1, width)
            small_own[2:3] = gate_sums[1].reshape(1, width)
            small_own[3:4] = sums_ref[1].reshape(1, width)
            small_own[4:5] = jnp.sum(norm_sums[0], axis=0, keepdims=True)
            small_own[5:6] = jnp.sum(norm_sums[1], axis=0, keepdims=True)
            small_twin().start()

        @pl.when(t == at + 1)
        def _():
            small_twin().wait()
            small_own[...] += small_in[0]
            small_pair().start()

        @pl.when(t == at + 1 + HOP)
        def _():
            small_pair().wait()
            small_own[...] += small_in[1]
            for away in (1, 2, 3):
                small_column(away).start()

        @pl.when(t == at + 1 + 2 * HOP)
        def _():
            for away in (1, 2, 3):
                small_column(away).wait()
            small_z[z] = small_own[...]
            small_ref[...] = (small_z[0] + small_z[1]) + (small_z[2] + small_z[3])

        return carry

    last = max(
        jobs + TWIN + LATE, OFFSET + PERIOD * (blocks + LEAVE) + 1,
        OFFSET + PERIOD * (blocks - 1 + MEET) + 2 * SPLIT + 3 + 2 * HOP,
    )
    lax.fori_loop(0, last, tick, 0)


def finish(
    lengths, saved, forgets, normed_t, reset, weight, x, mean, scale, passed, gain, forget_weight, reset_weight,
    sums,
):
    full, tokens = normed_t.shape
    rows_here, stretches, size, width = x.shape
    dma = pltpu.SemaphoreType.DMA
    vmem = IN_VMEM
    norm = NORM_TOKENS
    narrow = width // SPLIT
    pieces = norm // (rows_here * size)
    return pl.pallas_call(
        finish_kernel,
        out_shape=(
            jax.ShapeDtypeStruct((3, full, width), BF16),
            jax.ShapeDtypeStruct(x.shape, BF16),
            jax.ShapeDtypeStruct((SUBLANES, width), F32),
        ),
        in_specs=[IN_SMEM] + [ANY] * 9 + [vmem] * 4,
        out_specs=(ANY, ANY, vmem),
        scratch_shapes=[
            pltpu.VMEM((3, tokens, width), BF16),
            pltpu.VMEM((3, full, width), BF16),
            pltpu.VMEM((2, 2 * JOB_ROWS, tokens), BF16),
            pltpu.VMEM((MINE, JOB_ROWS, narrow), F32),
            pltpu.VMEM((2, JOB_ROWS, narrow), BF16),
            pltpu.VMEM((SHORT, JOB_ROWS, narrow), BF16),
            pltpu.VMEM((SHORT, 2 * PIECE, narrow), BF16),
            pltpu.VMEM((RING, 2 * PIECE, narrow), BF16),
            pltpu.VMEM((SHORT, SLAB, narrow), BF16),
            pltpu.VMEM((RING, SLAB, narrow), BF16),
            pltpu.VMEM((SHORT, SLAB, narrow), BF16),
            pltpu.VMEM((RING, SLAB, narrow), BF16),
            pltpu.VMEM((SHORT, 2 * PIECE, narrow), BF16),
            pltpu.VMEM((RING, 2 * PIECE, narrow), BF16),
            pltpu.VMEM((RING, SLAB, narrow), BF16),
            pltpu.VMEM((KEPT, norm, width), F32),
            pltpu.VMEM((KEPT, norm, width), BF16),
            pltpu.VMEM((RING, norm, width), BF16),
            pltpu.VMEM((norm, LANES), F32),
            pltpu.VMEM((2, norm // LANES, SUBLANES, LANES), F32),
            pltpu.VMEM((RING, norm // LANES, SUBLANES, LANES), F32),
            pltpu.VMEM((KEPT, pieces, rows_here, size, width), BF16),
            pltpu.VMEM((KEPT, norm, width), BF16),
            pltpu.VMEM((KEPT, norm, LANES), F32),
            pltpu.VMEM((KEPT, norm, LANES), F32),
            pltpu.VMEM((2, pieces, rows_here, size, width), BF16),
            pltpu.VMEM((2, SUBLANES, width), F32),
            pltpu.VMEM((rows_here, stretches * size, LANES), F32),
            pltpu.VMEM((AHEAD, 3, rows_here, HALF // 2, 2 * SUBLANES, LANES), BF16),
            pltpu.VMEM((AHEAD, rows_here, HALF) + TILE, F32),
            pltpu.VMEM((rows_here,) + TILE, F32),
            pltpu.VMEM((2,) + TILE, F32),
            pltpu.VMEM((SUBLANES, width), F32),
            pltpu.VMEM((2, SUBLANES, width), F32),
            pltpu.VMEM((4, SUBLANES, width), F32),
            dma((4,)), dma((2, 2)), dma((2, AHEAD)),
            dma((2,)), dma((SHORT,)), dma((SHORT,)), dma((RING,)), dma((SHORT,)), dma((RING,)),
            dma((SHORT,)), dma((RING,)), dma((SHORT,)), dma((RING,)), dma((RING,)),
            dma((RING,)), dma((RING,)), dma((RING,)), dma((RING,)),
            dma((2, RING)), dma((2, RING)), dma((RING,)), dma((RING,)),
            dma((KEPT,)), dma((RING,)), dma((2,)), dma((RING,)), dma((3 + pieces, KEPT)), dma((pieces, 2)),
            dma((5,)), dma((5,)),
        ],
        compiler_params=pltpu.CompilerParams(
            collective_id=1, has_side_effects=True, vmem_limit_bytes=VMEM_LIMIT
        ),
        name="finish",
    )(
        lengths, saved, forgets, normed_t, reset, weight, x, mean, scale, passed, gain, forget_weight, reset_weight, sums
    )


COLLECT_STEPS = 8


def collect_kernel(
    total_ref, mixed_ref, input_grad_ref, final_ref, small_ref,
    weight_grad_ref, mixed_out, input_grad_out, final_out, gain_out, shift_out, forget_weight_out, reset_weight_out,
    forget_bias_out, reset_bias_out,
):
    weight_grad_ref[...] = total_ref[...].astype(F32)
    mixed_out[...] = mixed_ref[...]
    input_grad_out[...] = input_grad_ref[...]

    @pl.when(pl.program_id(0) == 0)
    def _():
        final_out[...] = final_ref[...]
        outs = (forget_weight_out, reset_weight_out, forget_bias_out, reset_bias_out, gain_out, shift_out)
        for index, out in enumerate(outs):
            out[...] = small_ref[index:index + 1, :].reshape(TILE)


def collect(total, mixed, input_grad, final_state, small):
    gates, full, width = total.shape
    total = total.reshape(gates * full, width)
    mixed, input_grad = (array.reshape(-1, width) for array in (mixed, input_grad))
    arrays = (total, mixed, input_grad)
    blocks = [pl.BlockSpec((array.shape[0] // COLLECT_STEPS, width), lambda i: (i, 0)) for array in arrays]
    whole = lambda *shape: pl.BlockSpec(shape, lambda i: (0,) * len(shape))
    shape = jax.ShapeDtypeStruct
    weight_grad, *others = pl.pallas_call(
        collect_kernel,
        grid=(COLLECT_STEPS,),
        out_shape=(
            shape(total.shape, F32), shape(mixed.shape, BF16), shape(input_grad.shape, BF16),
            shape(final_state.shape, F32),
        ) + (shape(TILE, F32),) * 6,
        in_specs=blocks + [whole(*final_state.shape), whole(*small.shape)],
        out_specs=blocks + [whole(*final_state.shape)] + [whole(*TILE)] * 6,
        compiler_params=pltpu.CompilerParams(vmem_limit_bytes=VMEM_LIMIT),
        name="collect",
    )(total, mixed, input_grad, final_state, small)
    return weight_grad.reshape(gates, full, width), *others


def on_device(
    inputs, doc_lengths, layer_norm_gain, layer_norm_bias, weight, forget_weight, reset_weight, forget_bias,
    reset_bias, out_grad,
):
    rows_here, length, width = inputs.shape
    weights = jnp.transpose(weight, (1, 0, 2))
    stretched = (rows_here, length // STRETCH, STRETCH, width)
    x = inputs.reshape(stretched)
    gain = layer_norm_gain.reshape(1, width)
    vectors = [vector.reshape(TILE) for vector in (forget_weight, reset_weight, forget_bias, reset_bias)]
    saved, forgets, normed_t, mean, scale, mixed, passed, reset_grad, final_state, sums = project(
        doc_lengths, x, gain, layer_norm_bias.reshape(1, width), weights, out_grad.reshape(stretched), *vectors
    )
    weight_grad, input_grad, small = finish(
        doc_lengths, saved, forgets, normed_t, reset_grad, weights, x, mean, scale, passed, gain, vectors[0],
        vectors[1], sums,
    )
    weight_grad, mixed, input_grad, final_state, *vectors = collect(weight_grad, mixed, input_grad, final_state, small)
    devices = lax.axis_size("rows")
    groups = devices // 16
    if groups > 1:
        members = [[] for _ in range(devices // groups)]
        for device in range(devices):
            part, core = device // 2, device % 2
            members[(part // groups) * 2 + core].append(device)
        weight_grad, vectors = lax.psum((weight_grad, vectors), "rows", axis_index_groups=members)
    weight_grad = jnp.transpose(weight_grad, (1, 0, 2))
    return (
        mixed.reshape(inputs.shape), input_grad.reshape(inputs.shape), final_state, weight_grad,
        *[vector.reshape(width) for vector in vectors],
    )


def solution(mesh):
    rows_ch = P("rows", None, "ch")
    ch = P("ch")
    in_specs = (rows_ch, P("rows", None), ch, ch, P(None, None, "ch"), ch, ch, ch, ch, rows_ch)
    out_specs = (rows_ch, rows_ch, P("rows", "ch"), P(None, None, "ch"), ch, ch, ch, ch, ch, ch)
    return jax.shard_map(on_device, mesh=mesh, in_specs=in_specs, out_specs=out_specs, check_vma=False)
```

```python
import functools

import jax
import jax.numpy as jnp
from jax import lax
from jax.experimental import pallas as pl
from jax.experimental.pallas import tpu as pltpu
from jax.sharding import PartitionSpec as P

MESH = pl.DeviceIdType.MESH
F32 = jnp.float32
BF16 = jnp.bfloat16
EPSILON = 1e-05
LANES = 128
SUBLANES = 8
TILE = (SUBLANES, LANES)
STRETCH = 64
GROUP = 16
ANY = pl.BlockSpec(memory_space=pl.ANY)
IN_VMEM = pl.BlockSpec(memory_space=pltpu.VMEM)
IN_SMEM = pl.BlockSpec(memory_space=pltpu.SMEM)
VMEM_LIMIT = 60 * 1024 * 1024


def aligned(value, size=GROUP):
    return pl.multiple_of(value, size)


def fill_keep(lengths_ref, keep):
    rows_here, length = keep.shape[0], keep.shape[1]
    for row in range(rows_here):
        starts = [jnp.int32(0)]
        for document in range(lengths_ref.shape[1] - 1):
            starts.append(starts[-1] + lengths_ref[row, document])

        @pl.loop(0, length // LANES)
        def _(part):
            place = lax.broadcasted_iota(jnp.int32, (LANES, LANES), 0) + part * LANES
            value = jnp.ones((LANES, LANES), F32)
            for start in starts:
                value = jnp.where(place == start, 0.0, value)
            keep[row, pl.ds(aligned(part * LANES, LANES), LANES), :] = value


def project_kernel(
    lengths_ref, x_ref, gain_ref, shift_ref, weight_ref, grad_ref,
    forget_weight_ref, reset_weight_ref, forget_bias_ref, reset_bias_ref,
    saved_ref, forget_ref, normed_t_ref, mean_ref, scale_ref, mixed_ref, pass_ref, reset_ref, final_ref, sums_ref,
    both, weights, params, keep, normed, normed_t, mean_out, scale_out, u, grad_in, saved, forget_out, mixed_out, pass_out,
    reset_out, state_s,
    send_sem, recv_sem, own_sem, param_own, param_send, param_recv, weight_sem, grad_sem, out_sem,
):
    ch = lax.axis_index("ch")
    other = 1 - ch
    rows_here, stretches, size, width = x_ref.shape
    full = 2 * width
    tokens = rows_here * size
    own_columns = pl.ds(aligned(ch * width, width), width)

    load_weight = pltpu.make_async_copy(weight_ref, weights, weight_sem)

    def params_of(index, source):
        return (
            pltpu.make_async_copy(source, params.at[ch, index], param_own.at[index]),
            pltpu.make_async_remote_copy(
                src_ref=source, dst_ref=params.at[ch, index], send_sem=param_send.at[index],
                recv_sem=param_recv.at[index], device_id={"ch": other}, device_id_type=MESH,
            ),
        )

    def exchange(stretch):
        return pltpu.make_async_remote_copy(
            src_ref=x_ref.at[:, stretch], dst_ref=both.at[:, stretch, :, own_columns],
            send_sem=send_sem.at[stretch], recv_sem=recv_sem.at[stretch],
            device_id={"ch": other}, device_id_type=MESH,
        )

    def keep_own(stretch):
        return pltpu.make_async_copy(x_ref.at[:, stretch], both.at[:, stretch, :, own_columns], own_sem.at[stretch])

    def load_grad(stretch):
        slot = stretch % 2
        return pltpu.make_async_copy(grad_ref.at[:, stretch], grad_in.at[slot], grad_sem.at[slot])

    def outputs(stretch):
        slot = stretch % 2
        rows = pl.ds(aligned(stretch * tokens, tokens), tokens)
        return tuple(
            pltpu.make_async_copy(source.at[slot], target, out_sem.at[index, slot])
            for index, (source, target) in enumerate((
                (saved, saved_ref.at[stretch]), (forget_out, forget_ref.at[stretch]), (normed_t, normed_t_ref.at[:, rows]), (mean_out, mean_ref.at[rows]),
                (scale_out, scale_ref.at[rows]), (mixed_out, mixed_ref.at[:, stretch]), (pass_out, pass_ref.at[rows]),
                (reset_out, reset_ref.at[rows]),
            ))
        )

    load_weight.start()
    load_grad(0).start()
    barrier = pltpu.get_barrier_semaphore()
    pl.semaphore_signal(barrier, inc=1, device_id={"ch": other}, device_id_type=MESH)
    pl.semaphore_wait(barrier, 1)
    for index, source in enumerate((gain_ref, shift_ref)):
        for copy in params_of(index, source):
            copy.start()

    def begin(stretch, carry):
        exchange(stretch).start()
        keep_own(stretch).start()
        return carry

    lax.fori_loop(0, stretches, begin, 0)
    fill_keep(lengths_ref, keep)
    state_s[...] = jnp.zeros_like(state_s)
    sums_ref[...] = jnp.zeros_like(sums_ref)
    for index, source in enumerate((gain_ref, shift_ref)):
        for copy in params_of(index, source):
            copy.wait()
    load_weight.wait()

    def work(stretch, carry):
        slot = stretch % 2
        keep_own(stretch).wait()
        exchange(stretch).wait()
        load_grad(stretch).wait()

        @pl.when(stretch + 1 < stretches)
        def _():
            load_grad(stretch + 1).start()

        @pl.when(stretch >= 2)
        def _():
            for copy in outputs(stretch - 2):
                copy.wait()

        for row in range(rows_here):
            @pl.loop(0, size // GROUP, unroll=2)
            def _(part):
                here = pl.ds(aligned(part * GROUP), GROUP)
                there = pl.ds(aligned(row * size + part * GROUP), GROUP)
                x = both[row, stretch, here, :].astype(F32)
                mean = jnp.sum(x, axis=1, keepdims=True) * (1.0 / full)
                centered = x - mean
                variance = jnp.sum(centered * centered, axis=1, keepdims=True) * (1.0 / full)
                scale = lax.rsqrt(variance + EPSILON)
                gain = jnp.concatenate([params[0, 0], params[1, 0]], axis=1)
                shift = jnp.concatenate([params[0, 1], params[1, 1]], axis=1)
                normed[there, :] = (centered * scale * gain + shift).astype(BF16)
                mean_out[slot, there, :] = jnp.broadcast_to(mean, (GROUP, LANES))
                scale_out[slot, there, :] = jnp.broadcast_to(scale, (GROUP, LANES))

        for gate in range(3):
            u[gate] = jnp.dot(normed[...], weights[gate], preferred_element_type=F32)

        for part in range(full // LANES):
            columns = slice(part * LANES, (part + 1) * LANES)
            normed_t[slot, columns, :] = normed[:, columns].T

        forget_weight = 0.5 * forget_weight_ref[...]
        half_reset_weight = 0.5 * reset_weight_ref[...]
        forget_bias = 0.5 * forget_bias_ref[...]
        reset_bias = 0.5 * reset_bias_ref[...]

        def group(index, carry):
            state = list(carry[:rows_here])
            weight_sum, bias_sum = carry[rows_here:]
            here = pl.ds(aligned(index * GROUP), GROUP)
            there = [pl.ds(aligned(row * size + index * GROUP), GROUP) for row in range(rows_here)]
            spread = lambda value: value.astype(F32).reshape((GROUP,) + TILE)
            loaded = [
                (
                    spread(u[0, there[row], :]), spread(u[1, there[row], :]), spread(u[2, there[row], :]),
                    spread(both[row, stretch, here, own_columns]), spread(grad_in[slot, row, here, :]),
                )
                for row in range(rows_here)
            ]
            out = [([], [], []) for _ in range(rows_here)]
            held = [None] * rows_here
            for k in range(GROUP):
                time = index * GROUP + k
                for row in range(rows_here):
                    up_x, up_f, up_r, x, grad = (part[k] for part in loaded[row])
                    before = state[row] * keep[row, pl.ds(stretch * size + time, 1), :]
                    bent = jnp.tanh(0.5 * up_f + forget_bias + forget_weight * before)
                    gap = before - up_x
                    after = 0.5 * (before + up_x) + bent * (0.5 * gap)
                    state[row] = after
                    forget = 0.5 * bent + 0.5
                    reset = 0.5 * jnp.tanh(0.5 * up_r + reset_bias + half_reset_weight * before) + 0.5
                    over = after - x
                    direct = grad * reset
                    reset_grad = direct * over * (1.0 - reset)
                    forget_out[slot, row, time] = forget
                    kinds = (direct, gap * forget * (1.0 - forget), before)
                    if k % 2 == 0:
                        held[row] = kinds
                    else:
                        for kind in range(3):
                            both_steps = jnp.concatenate([held[row][kind], kinds[kind]], axis=0)
                            saved[slot, kind, row, index * (GROUP // 2) + k // 2] = both_steps.astype(BF16)
                    weight_sum = weight_sum + reset_grad * before
                    bias_sum = bias_sum + reset_grad
                    out[row][0].append(x + reset * over)
                    out[row][1].append(grad - direct)
                    out[row][2].append(reset_grad)
            flat = lambda parts: jnp.stack(parts).reshape(GROUP, width).astype(BF16)
            for row in range(rows_here):
                mixed_out[slot, row, here, :] = flat(out[row][0])
                pass_out[slot, there[row], :] = flat(out[row][1])
                reset_out[slot, there[row], :] = flat(out[row][2])
            return (*state, weight_sum, bias_sum)

        carried = lax.fori_loop(
            0, size // GROUP, group, (*[state_s[row] for row in range(rows_here)], sums_ref[0], sums_ref[1])
        )
        for row in range(rows_here):
            state_s[row] = carried[row]
        sums_ref[0] = carried[rows_here]
        sums_ref[1] = carried[rows_here + 1]
        for copy in outputs(stretch):
            copy.start()
        return carry

    lax.fori_loop(0, stretches, work, 0)
    for row in range(rows_here):
        final_ref[row:row + 1, :] = state_s[row].reshape(1, width)
    for stretch in (stretches - 2, stretches - 1):
        for copy in outputs(stretch):
            copy.wait()


def project(lengths, x, gain, shift, weight, grad, forget_weight, reset_weight, forget_bias, reset_bias):
    rows_here, stretches, size, width = x.shape
    full = 2 * width
    part = rows_here * size
    tokens = part * stretches
    kept = (3, rows_here, size // 2, 2 * SUBLANES, LANES)
    kept_forget = (rows_here, size) + TILE
    dma = pltpu.SemaphoreType.DMA
    shape = jax.ShapeDtypeStruct
    return pl.pallas_call(
        project_kernel,
        out_shape=(
            shape((stretches,) + kept, BF16),
            shape((stretches,) + kept_forget, F32),
            shape((full, tokens), BF16),
            shape((tokens, LANES), F32),
            shape((tokens, LANES), F32),
            shape(x.shape, BF16),
            shape((tokens, width), BF16),
            shape((tokens, width), BF16),
            shape((rows_here, width), F32),
            shape((2,) + TILE, F32),
        ),
        in_specs=[IN_SMEM] + [ANY] * 5 + [IN_VMEM] * 4,
        out_specs=[ANY] * 8 + [IN_VMEM] * 2,
        scratch_shapes=[
            pltpu.VMEM((rows_here, stretches, size, full), BF16),
            pltpu.VMEM((3, full, width), BF16),
            pltpu.VMEM((2, 2, 1, width), F32),
            pltpu.VMEM((rows_here, stretches * size, LANES), F32),
            pltpu.VMEM((part, full), BF16),
            pltpu.VMEM((2, full, part), BF16),
            pltpu.VMEM((2, part, LANES), F32),
            pltpu.VMEM((2, part, LANES), F32),
            pltpu.VMEM((3, part, width), F32),
            pltpu.VMEM((2, rows_here, size, width), BF16),
            pltpu.VMEM((2,) + kept, BF16),
            pltpu.VMEM((2,) + kept_forget, F32),
            pltpu.VMEM((2, rows_here, size, width), BF16),
            pltpu.VMEM((2, part, width), BF16),
            pltpu.VMEM((2, part, width), BF16),
            pltpu.VMEM((rows_here,) + TILE, F32),
            dma((stretches,)), dma((stretches,)), dma((stretches,)), dma((2,)), dma((2,)), dma((2,)), dma, dma((2,)),
            dma((8, 2)),
        ],
        compiler_params=pltpu.CompilerParams(
            collective_id=0, has_side_effects=True, vmem_limit_bytes=VMEM_LIMIT
        ),
        name="project",
    )(lengths, x, gain, shift, weight, grad, forget_weight, reset_weight, forget_bias, reset_bias)


JOB_ROWS = 128
PIECE = 16
QUARTER = 32
NORM_TOKENS = 256
HALF = 32
RING = 8
LONG = 12
SHORT = 4
SPLIT = 1
UNROLL = 4
HOP = 2
CORE = 1
AT_Y = CORE + HOP
AT_MIDDLE = AT_Y + HOP
AT_READY = AT_MIDDLE + HOP
AT_GATHER = AT_READY + HOP
AT_TWIN = AT_GATHER + HOP
MINE = AT_MIDDLE + 1
LATE = 3
PERIOD = 3
OFFSET = 4
MEET = 1
LEAVE = 2
KEPT = 3
AHEAD = 4


def finish_kernel(
    lengths_ref, saved_ref, forget_ref, normed_t_ref, reset_ref, weight_ref, x_ref, mean_ref, scale_ref, pass_ref, gain_ref,
    forget_weight_ref, reset_weight_ref, sums_ref,
    total_ref, input_grad_ref, small_ref,
    du, weights, rows_in, mine, core_out, core_in, y_out, y_in, slab_out, slab_in, side_out, side_in, half_out, half_in,
    swap_out, swap_in, cross_out, cross_in,
    ready, dn_own, dn_out, dn_in, moment_own, moment_out, moment_in, x_in, pass_in, mean_in, scale_in, grad_out,
    norm_sums, keep, saved, forgets, state_s, gate_sums, small_own, small_in, small_z,
    load_sem, rows_sem, saved_sem, core_send, core_recv, y_send, y_recv, slab_send, slab_recv, side_send, side_recv,
    half_send, half_recv, swap_send, swap_recv, cross_send, cross_recv, ready_sem,
    gather_send, gather_recv, over_send, over_recv, last_send, last_recv, pair_send, pair_recv, twin_send, twin_recv,
    dn_send, dn_recv, moment_send, moment_recv, norm_sem, grad_sem,
    small_send, small_recv,
):
    device = lax.axis_index("rows")
    devices = lax.axis_size("rows")
    ch = lax.axis_index("ch")
    z_stride, y_stride = devices // 4, devices // 8
    z = device // z_stride
    y = (device // y_stride) % 2
    core = device % 2
    twin = device + 1 - 2 * core
    pair = device + y_stride * (1 - 2 * y)
    full, tokens = normed_t_ref.shape
    rows_here, stretches, size, width = x_ref.shape
    half = full // 2
    narrow = width // SPLIT
    per_part = half // JOB_ROWS
    per_gate = per_part * SPLIT
    jobs = 3 * per_gate
    blocks = tokens // NORM_TOKENS

    def gate_of(job):
        return (job // per_gate + 2) % 3

    def place(job, whose):
        row = aligned(whose * half + (job // SPLIT % per_part) * JOB_ROWS, JOB_ROWS)
        column = aligned((job % SPLIT) * narrow, narrow)
        return gate_of(job), row, column

    outer = jnp.logical_or(z == 0, z == 3)
    inner = jnp.logical_not(outer)
    inward = device + z_stride * (1 - 2 * (z // 2))
    outward = device - z_stride * (1 - 2 * (z // 2))
    y_row, pair_row = aligned(3 * QUARTER * y, QUARTER), aligned(3 * QUARTER * (1 - y), QUARTER)
    own_half, other_half = aligned(QUARTER * (1 + z // 2), QUARTER), aligned(QUARTER * (2 - z // 2), QUARTER)

    load_reset = pltpu.make_async_copy(reset_ref, du.at[2], load_sem.at[3])

    def load_weight(gate):
        return pltpu.make_async_copy(weight_ref.at[gate], weights.at[gate], load_sem.at[gate])

    def load_rows(turn):
        slot = turn % 2
        own = aligned(core * half + (turn % per_part) * JOB_ROWS, JOB_ROWS)
        other = aligned((1 - core) * half + (turn % per_part) * JOB_ROWS, JOB_ROWS)
        return (
            pltpu.make_async_copy(
                normed_t_ref.at[pl.ds(own, JOB_ROWS)], rows_in.at[slot, pl.ds(0, JOB_ROWS)], rows_sem.at[0, slot]
            ),
            pltpu.make_async_copy(
                normed_t_ref.at[pl.ds(other, JOB_ROWS)], rows_in.at[slot, pl.ds(JOB_ROWS, JOB_ROWS)],
                rows_sem.at[1, slot],
            ),
        )

    def remote(source, target, send, recv, where):
        return pltpu.make_async_remote_copy(
            src_ref=source, dst_ref=target, send_sem=send, recv_sem=recv, device_id=where, device_id_type=MESH
        )

    def to_core(job):
        return remote(
            core_out.at[job % 2], core_in.at[job % SHORT], core_send.at[job % 2], core_recv.at[job % SHORT],
            {"rows": twin},
        )

    def to_y(job):
        return remote(
            y_out.at[job % SHORT], y_in.at[job % RING], y_send.at[job % SHORT], y_recv.at[job % RING], {"rows": pair}
        )

    def ring(source, target, send, recv, job, where, size=RING):
        return remote(
            source.at[job % SHORT], target.at[job % size], send.at[job % SHORT], recv.at[job % size], {"rows": where}
        )

    def to_slab(job):
        return ring(slab_out, slab_in, slab_send, slab_recv, job, inward, LONG)

    def to_side(job):
        return ring(side_out, side_in, side_send, side_recv, job, inward, LONG)

    def to_half(job):
        return ring(half_out, half_in, half_send, half_recv, job, inward)

    def to_swap(job):
        return ring(swap_out, swap_in, swap_send, swap_recv, job, inward)

    def to_cross(job):
        return ring(cross_out, cross_in, cross_send, cross_recv, job, pair)

    def result(job, offset, size, whose):
        gate, row, column = place(job, whose)
        return total_ref.at[gate, pl.ds(aligned(row + offset), size), pl.ds(column, narrow)]

    def keep_ready(job):
        return tuple(
            pltpu.make_async_copy(
                ready.at[job % SHORT, kind], result(job, row, QUARTER, core), ready_sem.at[kind, job % SHORT]
            )
            for kind, row in enumerate((y_row, own_half))
        )

    def gather(job):
        return tuple(
            remote(
                ready.at[job % SHORT, kind], result(job, row, QUARTER, core), gather_send.at[kind, job % LONG],
                gather_recv.at[kind, job % LONG], {"rows": outward},
            )
            for kind, row in enumerate((y_row, own_half))
        )

    def over(job):
        return remote(
            ready.at[job % SHORT, 1], result(job, own_half, QUARTER, core), over_send.at[job % LONG],
            over_recv.at[job % LONG], {"rows": inward},
        )

    def last_half(job):
        return remote(
            result(job, other_half, QUARTER, core), result(job, other_half, QUARTER, core), last_send.at[job % LONG],
            last_recv.at[job % LONG], {"rows": outward},
        )

    def to_pair(job, first=False):
        source = ready.at[job % SHORT, 0] if first else result(job, y_row, QUARTER, core)
        return remote(
            source, result(job, y_row, QUARTER, core), pair_send.at[job % LONG], pair_recv.at[job % LONG],
            {"rows": pair},
        )

    def to_twin(job):
        return remote(
            result(job, 0, JOB_ROWS, core), result(job, 0, JOB_ROWS, core),
            twin_send.at[job % LONG], twin_recv.at[job % LONG], {"rows": twin},
        )

    def to_partner(block):
        return remote(
            dn_out.at[block % KEPT], dn_in.at[block % RING], dn_send.at[block % KEPT], dn_recv.at[block % RING],
            {"ch": 1 - ch},
        )

    def moments(block):
        return remote(
            moment_out.at[block % 2], moment_in.at[block % RING], moment_send.at[block % 2],
            moment_recv.at[block % RING], {"ch": 1 - ch},
        )

    pieces = NORM_TOKENS // (rows_here * size)

    def first_row(block):
        return aligned(tokens - NORM_TOKENS * (block + 1), NORM_TOKENS)

    def load_norm(block):
        rows = pl.ds(first_row(block), NORM_TOKENS)
        slot = block % KEPT
        return tuple(
            pltpu.make_async_copy(source.at[rows], target.at[slot], norm_sem.at[index, slot])
            for index, (source, target) in enumerate(((pass_ref, pass_in), (mean_ref, mean_in), (scale_ref, scale_in)))
        ) + tuple(
            pltpu.make_async_copy(
                x_ref.at[:, stretches - pieces * (block + 1) + piece], x_in.at[slot, piece],
                norm_sem.at[3 + piece, slot],
            )
            for piece in range(pieces)
        )

    def store_grad(block):
        return tuple(
            pltpu.make_async_copy(
                grad_out.at[block % 2, piece], input_grad_ref.at[:, stretches - pieces * (block + 1) + piece],
                grad_sem.at[piece, block % 2],
            )
            for piece in range(pieces)
        )

    def load_saved(turn):
        slot, stretch, part = turn % AHEAD, stretches - 1 - turn // 2, 1 - turn % 2
        return (
            pltpu.make_async_copy(
                saved_ref.at[stretch, :, :, pl.ds(aligned(part * (HALF // 2), HALF // 2), HALF // 2)],
                saved.at[slot], saved_sem.at[0, slot],
            ),
            pltpu.make_async_copy(
                forget_ref.at[stretch, :, pl.ds(aligned(part * HALF, HALF), HALF)], forgets.at[slot],
                saved_sem.at[1, slot],
            ),
        )

    def small_twin():
        return remote(small_own, small_in.at[0], small_send.at[0], small_recv.at[0], {"rows": twin})

    def small_pair():
        return remote(small_own, small_in.at[1], small_send.at[1], small_recv.at[1], {"rows": pair})

    def small_column(away):
        there = (z + away) % 4
        return remote(
            small_own, small_z.at[z], small_send.at[1 + away], small_recv.at[1 + away],
            {"rows": device + (there - z) * z_stride},
        )

    load_reset.start()
    for copy in load_rows(0):
        copy.start()
    for turn in range(AHEAD - 1):
        for copy in load_saved(turn):
            copy.start()

    def is_job(job):
        return jnp.logical_and(job >= 0, job < jobs)

    def is_block(block):
        return jnp.logical_and(block >= 0, block < blocks)

    def when(*conditions):
        return pl.when(functools.reduce(jnp.logical_and, conditions))

    def multiply(t):
        gate, slot, turn = gate_of(t), t % 2, t // SPLIT

        @pl.when(t % SPLIT == 0)
        def _():
            for copy in load_rows(turn):
                copy.wait()

        @when(t % SPLIT == 0, t + SPLIT < jobs)
        def _():
            for copy in load_rows(turn + 1):
                copy.start()

        columns = pl.ds(aligned((t % SPLIT) * narrow, narrow), narrow)
        product = jnp.dot(rows_in[turn % 2], du[gate, :, columns], preferred_element_type=F32)
        mine[t % MINE] = product[:JOB_ROWS]
        core_out[slot] = product[JOB_ROWS:].astype(BF16)

    barrier = pltpu.get_barrier_semaphore()
    for where in [{"rows": twin}, {"rows": pair}, {"ch": 1 - ch}] + [
        {"rows": device + ((z + away) % 4 - z) * z_stride} for away in (1, 2, 3)
    ]:
        pl.semaphore_signal(barrier, inc=1, device_id=where, device_id_type=MESH)
    norm_sums[...] = jnp.zeros_like(norm_sums)
    state_s[...] = jnp.zeros_like(state_s)
    gate_sums[...] = jnp.zeros_like(gate_sums)
    fill_keep(lengths_ref, keep)
    turns = 2 * stretches
    turns_tick = turns // per_gate
    load_reset.wait()
    for gate in range(3):
        load_weight(gate).start()

    multiply(0)
    pl.semaphore_wait(barrier, 6)

    def tick(t, carry):
        job = t - AT_TWIN - 1

        @when(is_job(job))
        def _():
            to_twin(job).wait_recv()

        job = t - AT_TWIN

        @when(is_job(job), outer)
        def _():
            last_half(job).wait_recv()

        @when(is_job(job))
        def _():
            to_pair(job).wait_recv()
            to_twin(job).start()

        @when(is_job(job - LATE))
        def _():
            to_twin(job - LATE).wait_send()

        job = t - AT_GATHER

        @when(is_job(job), outer)
        def _():
            for copy in gather(job):
                copy.wait_recv()
            to_pair(job).start()

        @when(is_job(job), inner)
        def _():
            over(job).wait_recv()
            last_half(job).start()

        @when(is_job(job - LATE), outer)
        def _():
            to_pair(job - LATE).wait_send()

        @when(is_job(job - LATE), inner)
        def _():
            last_half(job - LATE).wait_send()

        job = t - AT_READY

        @when(is_job(job), inner)
        def _():
            slot = job % SHORT
            to_swap(job).wait_recv()
            ready[slot, 0] = (swap_out[slot].astype(F32) + swap_in[job % RING].astype(F32)).astype(BF16)
            to_cross(job).wait_recv()
            ready[slot, 1] = (cross_out[slot].astype(F32) + cross_in[job % RING].astype(F32)).astype(BF16)
            over(job).start()
            for copy in gather(job):
                copy.start()
            to_pair(job, True).start()
            for copy in keep_ready(job):
                copy.start()

        @when(is_job(job - LATE), inner)
        def _():
            over(job - LATE).wait_send()
            for copy in gather(job - LATE):
                copy.wait_send()
            to_pair(job - LATE, True).wait_send()
            for copy in keep_ready(job - LATE):
                copy.wait()

        job = t - AT_MIDDLE

        @when(is_job(job), inner)
        def _():
            slot = job % MINE
            to_half(job).wait_recv()
            mine[slot, pl.ds(own_half, QUARTER)] += half_in[job % RING].astype(F32)
            cross_out[job % SHORT] = mine[slot, pl.ds(own_half, QUARTER)].astype(BF16)
            to_cross(job).start()
            to_side(job).wait_recv()
            mine[slot, pl.ds(y_row, QUARTER)] += side_in[job % LONG].astype(F32)
            swap_out[job % SHORT] = mine[slot, pl.ds(y_row, QUARTER)].astype(BF16)
            to_swap(job).start()

        @when(is_job(job - LATE), inner)
        def _():
            to_cross(job - LATE).wait_send()
            to_swap(job - LATE).wait_send()

        job = t - AT_Y

        @when(is_job(job))
        def _():
            to_y(job).wait_recv()
            mine[job % MINE, pl.ds(y_row, QUARTER)] += y_in[job % RING].astype(F32)

        @when(is_job(job), outer)
        def _():
            side_out[job % SHORT] = mine[job % MINE, pl.ds(y_row, QUARTER)].astype(BF16)
            to_side(job).start()

        @when(is_job(job), inner)
        def _():
            slot = job % MINE
            to_slab(job).wait_recv()
            mine[slot, QUARTER:3 * QUARTER] += slab_in[job % LONG].astype(F32)
            half_out[job % SHORT] = mine[slot, pl.ds(other_half, QUARTER)].astype(BF16)
            to_half(job).start()

        @when(is_job(job - LATE), outer)
        def _():
            to_side(job - LATE).wait_send()

        @when(is_job(job - LATE), inner)
        def _():
            to_half(job - LATE).wait_send()

        job = t - CORE

        @when(is_job(job))
        def _():
            to_core(job).wait_recv()
            slot = job % MINE
            mine[slot] += core_in[job % SHORT].astype(F32)
            y_out[job % SHORT] = mine[slot, pl.ds(pair_row, QUARTER)].astype(BF16)
            to_y(job).start()

        @when(is_job(job), outer)
        def _():
            slab_out[job % SHORT] = mine[job % MINE, QUARTER:3 * QUARTER].astype(BF16)
            to_slab(job).start()

        @when(is_job(job - LATE))
        def _():
            to_y(job - LATE).wait_send()

        @when(is_job(job - LATE), outer)
        def _():
            to_slab(job - LATE).wait_send()

        @when(is_job(t - 2))
        def _():
            to_core(t - 2).wait_send()

        @when(t > 0, is_job(t))
        def _():
            multiply(t)

        @when(is_job(t))
        def _():
            to_core(t).start()

        @pl.when(t < per_gate)
        def _():
            forget_weight = forget_weight_ref[...]
            reset_weight = reset_weight_ref[...]

            def back_half(turn, carry):
                for copy in load_saved(turn):
                    copy.wait()

                @pl.when(turn + AHEAD - 1 < turns)
                def _():
                    for copy in load_saved(turn + AHEAD - 1):
                        copy.start()

                slot = turn % AHEAD
                stretch, start = stretches - 1 - turn // 2, (1 - turn % 2) * HALF

                def group(back, carry):
                    index = HALF // PIECE - 1 - back
                    running = list(carry[:rows_here])
                    weight_sum, bias_sum = carry[rows_here:]
                    out = [([None] * PIECE, [None] * PIECE) for _ in range(rows_here)]
                    rows = [
                        pl.ds(aligned((stretch * rows_here + row) * size + start + index * PIECE), PIECE)
                        for row in range(rows_here)
                    ]
                    resets = [du[2, rows[row], :].astype(F32).reshape((PIECE,) + TILE) for row in range(rows_here)]
                    pairs = [None] * rows_here
                    for k in range(PIECE - 1, -1, -1):
                        time = index * PIECE + k
                        for row in range(rows_here):
                            if k % 2:
                                pairs[row] = [
                                    saved[slot, kind, row, index * (PIECE // 2) + k // 2].astype(F32)
                                    for kind in range(3)
                                ]
                            lanes = slice(SUBLANES, 2 * SUBLANES) if k % 2 else slice(0, SUBLANES)
                            direct, slope, before = (pair[lanes] for pair in pairs[row])
                            forget = forgets[slot, row, time]
                            kept = keep[row, pl.ds(stretch * size + start + time, 1), :]
                            state_grad = direct + running[row]
                            through = (forget + slope * forget_weight) * kept
                            running[row] = through * state_grad + resets[row][k] * reset_weight * kept
                            forget_grad = state_grad * slope
                            weight_sum = weight_sum + forget_grad * before
                            bias_sum = bias_sum + forget_grad
                            out[row][0][k] = state_grad - state_grad * forget
                            out[row][1][k] = forget_grad
                    for row in range(rows_here):
                        for gate in range(2):
                            du[gate, rows[row], :] = jnp.stack(out[row][gate]).reshape(PIECE, width).astype(BF16)
                    return (*running, weight_sum, bias_sum)

                return lax.fori_loop(0, HALF // PIECE, group, carry)

            carried = lax.fori_loop(
                t * turns_tick, (t + 1) * turns_tick, back_half,
                (*[state_s[row] for row in range(rows_here)], gate_sums[0], gate_sums[1]),
            )
            for row in range(rows_here):
                state_s[row] = carried[row]
            gate_sums[0] = carried[rows_here]
            gate_sums[1] = carried[rows_here + 1]

        @pl.when(t == OFFSET)
        def _():
            for gate in range(3):
                load_weight(gate).wait()

        block, phase = (t - OFFSET) // PERIOD, (t - OFFSET) % PERIOD

        def split(index):
            each = size // PIECE
            return index // (rows_here * each), (index // each) % rows_here, pl.ds(aligned(index % each * PIECE), PIECE)

        def back(block, whose, part):
            rows = pl.ds(first_row(block), NORM_TOKENS)
            columns = pl.ds(aligned(whose * width + part * narrow, narrow), narrow)
            return sum(
                lax.dot_general(
                    du[gate, rows, :], weights[gate, columns, :], (((1,), (1,)), ((), ())),
                    preferred_element_type=F32,
                )
                for gate in range(3)
            )

        @when(is_block(block), phase < SPLIT)
        def _():
            columns = pl.ds(aligned(phase * narrow, narrow), narrow)
            dn_out[block % KEPT, :, columns] = back(block, 1 - ch, phase).astype(BF16)

        @when(is_block(block), phase == SPLIT - 1)
        def _():
            to_partner(block).start()

        @when(is_block(block - MEET + 1), phase == SPLIT)
        def _():
            for copy in load_norm(block - MEET + 1):
                copy.start()

        @when(is_block(block - MEET), phase >= SPLIT, phase < 2 * SPLIT)
        def _():
            columns = pl.ds(aligned((phase - SPLIT) * narrow, narrow), narrow)
            dn_own[(block - MEET) % KEPT, :, columns] = back(block - MEET, ch, phase - SPLIT)

        @when(is_block(block - MEET), phase == 2 * SPLIT)
        def _():
            now = block - MEET
            slot = now % KEPT
            to_partner(now).wait()
            for copy in load_norm(now):
                copy.wait()

            def part(index, sums):
                gain_sum, shift_sum = sums
                rows = pl.ds(aligned(index * PIECE), PIECE)
                piece, row, inner = split(index)
                dn = dn_own[slot, rows, :] + dn_in[now % RING, rows, :].astype(F32)
                dn_own[slot, rows, :] = dn
                scale = scale_in[slot, rows, 0:1]
                xhat = (x_in[slot, piece, row, inner, :].astype(F32) - mean_in[slot, rows, 0:1]) * scale
                gained = dn * xhat
                dxhat = dn * gain_ref[0:1, :]
                first = jnp.sum(dxhat, axis=1, keepdims=True)
                second = jnp.sum(dxhat * xhat, axis=1, keepdims=True)
                lane = lax.broadcasted_iota(jnp.int32, (PIECE, LANES), 1)
                moment_own[rows, :] = jnp.where(lane == 0, first, second)
                return (
                    gain_sum + gained[:SUBLANES] + gained[SUBLANES:], shift_sum + dn[:SUBLANES] + dn[SUBLANES:],
                )

            gain_sum, shift_sum = lax.fori_loop(
                0, NORM_TOKENS // PIECE, part, (norm_sums[0], norm_sums[1]), unroll=UNROLL
            )
            norm_sums[0] = gain_sum
            norm_sums[1] = shift_sum
            for part in range(NORM_TOKENS // LANES):
                moment_out[now % 2, part] = moment_own[part * LANES:(part + 1) * LANES, :].T[:SUBLANES]
            moments(now).start()

        @when(is_block(block - LEAVE), phase == PERIOD - 1)
        def _():
            now = block - LEAVE
            slot = now % KEPT
            moments(now).wait()
            for part in range(NORM_TOKENS // LANES):
                both = (moment_out[now % 2, part] + moment_in[now % RING, part]) * (1.0 / full)
                moment_own[part * LANES:(part + 1) * LANES, :] = jnp.concatenate([both] * (LANES // SUBLANES), axis=0).T

            @pl.loop(0, NORM_TOKENS // PIECE, unroll=UNROLL)
            def _(index):
                rows = pl.ds(aligned(index * PIECE), PIECE)
                piece, row, inner = split(index)
                first, second = moment_own[rows, 0:1], moment_own[rows, 1:2]
                scale = scale_in[slot, rows, 0:1]
                xhat = (x_in[slot, piece, row, inner, :].astype(F32) - mean_in[slot, rows, 0:1]) * scale
                back = scale * (dn_own[slot, rows, :] * gain_ref[0:1, :] - first - xhat * second)
                grad_out[now % 2, piece, row, inner, :] = (back + pass_in[slot, rows, :].astype(F32)).astype(BF16)

            for copy in store_grad(now):
                copy.start()

        @when(is_block(block - LEAVE - 1), phase == 0)
        def _():
            for copy in store_grad(block - LEAVE - 1):
                copy.wait()

        at = OFFSET + PERIOD * (blocks - 1 + MEET) + 2 * SPLIT + 1

        @pl.when(t == at)
        def _():
            small_own[...] = jnp.zeros_like(small_own)
            small_own[0:1] = gate_sums[0].reshape(1, width)
            small_own[1:2] = sums_ref[0].reshape(1, width)
            small_own[2:3] = gate_sums[1].reshape(1, width)
            small_own[3:4] = sums_ref[1].reshape(1, width)
            small_own[4:5] = jnp.sum(norm_sums[0], axis=0, keepdims=True)
            small_own[5:6] = jnp.sum(norm_sums[1], axis=0, keepdims=True)
            small_twin().start()

        @pl.when(t == at + 1)
        def _():
            small_twin().wait()
            small_own[...] += small_in[0]
            small_pair().start()

        @pl.when(t == at + 1 + HOP)
        def _():
            small_pair().wait()
            small_own[...] += small_in[1]
            for away in (1, 2, 3):
                small_column(away).start()

        @pl.when(t == at + 1 + 2 * HOP)
        def _():
            for away in (1, 2, 3):
                small_column(away).wait()
            small_z[z] = small_own[...]
            small_ref[...] = (small_z[0] + small_z[1]) + (small_z[2] + small_z[3])

        return carry

    last = max(
        jobs + AT_TWIN + LATE, OFFSET + PERIOD * (blocks + LEAVE) + 1,
        OFFSET + PERIOD * (blocks - 1 + MEET) + 2 * SPLIT + 3 + 2 * HOP,
    )
    lax.fori_loop(0, last, tick, 0)


def finish(
    lengths, saved, forgets, normed_t, reset, weight, x, mean, scale, passed, gain, forget_weight, reset_weight,
    sums,
):
    full, tokens = normed_t.shape
    rows_here, stretches, size, width = x.shape
    dma = pltpu.SemaphoreType.DMA
    vmem = IN_VMEM
    norm = NORM_TOKENS
    narrow = width // SPLIT
    pieces = norm // (rows_here * size)
    return pl.pallas_call(
        finish_kernel,
        out_shape=(
            jax.ShapeDtypeStruct((3, full, width), BF16),
            jax.ShapeDtypeStruct(x.shape, BF16),
            jax.ShapeDtypeStruct((SUBLANES, width), F32),
        ),
        in_specs=[IN_SMEM] + [ANY] * 9 + [vmem] * 4,
        out_specs=(ANY, ANY, vmem),
        scratch_shapes=[
            pltpu.VMEM((3, tokens, width), BF16),
            pltpu.VMEM((3, full, width), BF16),
            pltpu.VMEM((2, 2 * JOB_ROWS, tokens), BF16),
            pltpu.VMEM((MINE, JOB_ROWS, narrow), F32),
            pltpu.VMEM((2, JOB_ROWS, narrow), BF16),
            pltpu.VMEM((SHORT, JOB_ROWS, narrow), BF16),
            pltpu.VMEM((SHORT, QUARTER, narrow), BF16),
            pltpu.VMEM((RING, QUARTER, narrow), BF16),
            pltpu.VMEM((SHORT, 2 * QUARTER, narrow), BF16),
            pltpu.VMEM((LONG, 2 * QUARTER, narrow), BF16),
            pltpu.VMEM((SHORT, QUARTER, narrow), BF16),
            pltpu.VMEM((LONG, QUARTER, narrow), BF16),
            pltpu.VMEM((SHORT, QUARTER, narrow), BF16),
            pltpu.VMEM((RING, QUARTER, narrow), BF16),
            pltpu.VMEM((SHORT, QUARTER, narrow), BF16),
            pltpu.VMEM((RING, QUARTER, narrow), BF16),
            pltpu.VMEM((SHORT, QUARTER, narrow), BF16),
            pltpu.VMEM((RING, QUARTER, narrow), BF16),
            pltpu.VMEM((SHORT, 2, QUARTER, narrow), BF16),
            pltpu.VMEM((KEPT, norm, width), F32),
            pltpu.VMEM((KEPT, norm, width), BF16),
            pltpu.VMEM((RING, norm, width), BF16),
            pltpu.VMEM((norm, LANES), F32),
            pltpu.VMEM((2, norm // LANES, SUBLANES, LANES), F32),
            pltpu.VMEM((RING, norm // LANES, SUBLANES, LANES), F32),
            pltpu.VMEM((KEPT, pieces, rows_here, size, width), BF16),
            pltpu.VMEM((KEPT, norm, width), BF16),
            pltpu.VMEM((KEPT, norm, LANES), F32),
            pltpu.VMEM((KEPT, norm, LANES), F32),
            pltpu.VMEM((2, pieces, rows_here, size, width), BF16),
            pltpu.VMEM((2, SUBLANES, width), F32),
            pltpu.VMEM((rows_here, stretches * size, LANES), F32),
            pltpu.VMEM((AHEAD, 3, rows_here, HALF // 2, 2 * SUBLANES, LANES), BF16),
            pltpu.VMEM((AHEAD, rows_here, HALF) + TILE, F32),
            pltpu.VMEM((rows_here,) + TILE, F32),
            pltpu.VMEM((2,) + TILE, F32),
            pltpu.VMEM((SUBLANES, width), F32),
            pltpu.VMEM((2, SUBLANES, width), F32),
            pltpu.VMEM((4, SUBLANES, width), F32),
            dma((4,)), dma((2, 2)), dma((2, AHEAD)),
            dma((2,)), dma((SHORT,)), dma((SHORT,)), dma((RING,)), dma((SHORT,)), dma((LONG,)),
            dma((SHORT,)), dma((LONG,)), dma((SHORT,)), dma((RING,)), dma((SHORT,)), dma((RING,)),
            dma((SHORT,)), dma((RING,)), dma((2, SHORT)),
            dma((2, LONG)), dma((2, LONG)), dma((LONG,)), dma((LONG,)), dma((LONG,)), dma((LONG,)),
            dma((LONG,)), dma((LONG,)), dma((LONG,)), dma((LONG,)),
            dma((KEPT,)), dma((RING,)), dma((2,)), dma((RING,)), dma((3 + pieces, KEPT)), dma((pieces, 2)),
            dma((5,)), dma((5,)),
        ],
        compiler_params=pltpu.CompilerParams(
            collective_id=1, has_side_effects=True, vmem_limit_bytes=VMEM_LIMIT
        ),
        name="finish",
    )(
        lengths, saved, forgets, normed_t, reset, weight, x, mean, scale, passed, gain, forget_weight, reset_weight, sums
    )


COLLECT_STEPS = 8


def collect_kernel(
    total_ref, mixed_ref, input_grad_ref, final_ref, small_ref,
    weight_grad_ref, mixed_out, input_grad_out, final_out, gain_out, shift_out, forget_weight_out, reset_weight_out,
    forget_bias_out, reset_bias_out,
):
    weight_grad_ref[...] = total_ref[...].astype(F32)
    mixed_out[...] = mixed_ref[...]
    input_grad_out[...] = input_grad_ref[...]

    @pl.when(pl.program_id(0) == 0)
    def _():
        final_out[...] = final_ref[...]
        outs = (forget_weight_out, reset_weight_out, forget_bias_out, reset_bias_out, gain_out, shift_out)
        for index, out in enumerate(outs):
            out[...] = small_ref[index:index + 1, :].reshape(TILE)


def collect(total, mixed, input_grad, final_state, small):
    gates, full, width = total.shape
    total = total.reshape(gates * full, width)
    mixed, input_grad = (array.reshape(-1, width) for array in (mixed, input_grad))
    arrays = (total, mixed, input_grad)
    blocks = [pl.BlockSpec((array.shape[0] // COLLECT_STEPS, width), lambda i: (i, 0)) for array in arrays]
    whole = lambda *shape: pl.BlockSpec(shape, lambda i: (0,) * len(shape))
    shape = jax.ShapeDtypeStruct
    weight_grad, *others = pl.pallas_call(
        collect_kernel,
        grid=(COLLECT_STEPS,),
        out_shape=(
            shape(total.shape, F32), shape(mixed.shape, BF16), shape(input_grad.shape, BF16),
            shape(final_state.shape, F32),
        ) + (shape(TILE, F32),) * 6,
        in_specs=blocks + [whole(*final_state.shape), whole(*small.shape)],
        out_specs=blocks + [whole(*final_state.shape)] + [whole(*TILE)] * 6,
        compiler_params=pltpu.CompilerParams(vmem_limit_bytes=VMEM_LIMIT),
        name="collect",
    )(total, mixed, input_grad, final_state, small)
    return weight_grad.reshape(gates, full, width), *others


def on_device(
    inputs, doc_lengths, layer_norm_gain, layer_norm_bias, weight, forget_weight, reset_weight, forget_bias,
    reset_bias, out_grad,
):
    rows_here, length, width = inputs.shape
    weights = jnp.transpose(weight, (1, 0, 2))
    stretched = (rows_here, length // STRETCH, STRETCH, width)
    x = inputs.reshape(stretched)
    gain = layer_norm_gain.reshape(1, width)
    vectors = [vector.reshape(TILE) for vector in (forget_weight, reset_weight, forget_bias, reset_bias)]
    saved, forgets, normed_t, mean, scale, mixed, passed, reset_grad, final_state, sums = project(
        doc_lengths, x, gain, layer_norm_bias.reshape(1, width), weights, out_grad.reshape(stretched), *vectors
    )
    weight_grad, input_grad, small = finish(
        doc_lengths, saved, forgets, normed_t, reset_grad, weights, x, mean, scale, passed, gain, vectors[0],
        vectors[1], sums,
    )
    weight_grad, mixed, input_grad, final_state, *vectors = collect(weight_grad, mixed, input_grad, final_state, small)
    devices = lax.axis_size("rows")
    groups = devices // 16
    if groups > 1:
        members = [[] for _ in range(devices // groups)]
        for device in range(devices):
            part, core = device // 2, device % 2
            members[(part // groups) * 2 + core].append(device)
        weight_grad, vectors = lax.psum((weight_grad, vectors), "rows", axis_index_groups=members)
    weight_grad = jnp.transpose(weight_grad, (1, 0, 2))
    return (
        mixed.reshape(inputs.shape), input_grad.reshape(inputs.shape), final_state, weight_grad,
        *[vector.reshape(width) for vector in vectors],
    )


def solution(mesh):
    rows_ch = P("rows", None, "ch")
    ch = P("ch")
    in_specs = (rows_ch, P("rows", None), ch, ch, P(None, None, "ch"), ch, ch, ch, ch, rows_ch)
    out_specs = (rows_ch, rows_ch, P("rows", "ch"), P(None, None, "ch"), ch, ch, ch, ch, ch, ch)
    return jax.shard_map(on_device, mesh=mesh, in_specs=in_specs, out_specs=out_specs, check_vma=False)
```

```python
import functools

import jax
import jax.numpy as jnp
from jax import lax
from jax.experimental import pallas as pl
from jax.experimental.pallas import tpu as pltpu
from jax.sharding import PartitionSpec as P

MESH = pl.DeviceIdType.MESH
F32 = jnp.float32
BF16 = jnp.bfloat16
EPSILON = 1e-05
LANES = 128
SUBLANES = 8
TILE = (SUBLANES, LANES)
STRETCH = 64
GROUP = 16
ANY = pl.BlockSpec(memory_space=pl.ANY)
IN_SMEM = pl.BlockSpec(memory_space=pltpu.SMEM)
VMEM_LIMIT = 60 * 1024 * 1024


def aligned(value, size=GROUP):
    return pl.multiple_of(value, size)


def fill_keep(lengths_ref, keep):
    rows_here, length = keep.shape[0], keep.shape[1]
    for row in range(rows_here):
        starts = [jnp.int32(0)]
        for document in range(lengths_ref.shape[1] - 1):
            starts.append(starts[-1] + lengths_ref[row, document])

        @pl.loop(0, length // LANES)
        def _(part):
            place = lax.broadcasted_iota(jnp.int32, (LANES, LANES), 0) + part * LANES
            value = jnp.ones((LANES, LANES), F32)
            for start in starts:
                value = jnp.where(place == start, 0.0, value)
            keep[row, pl.ds(aligned(part * LANES, LANES), LANES), :] = value


def project_kernel(
    lengths_ref, x_ref, gain_ref, shift_ref, weight_ref, grad_ref,
    forget_weight_in, reset_weight_in, forget_bias_in, reset_bias_in,
    saved_ref, forget_ref, normed_t_ref, mean_ref, scale_ref, mixed_ref, pass_ref, reset_ref, final_out, sums_out,
    both, weights, params, keep, normed, normed_t, mean_out, scale_out, u, grad_in, saved, forget_out, mixed_out, pass_out,
    reset_out, state_s, vectors, final_ref, sums_ref,
    send_sem, recv_sem, own_sem, param_own, param_send, param_recv, weight_sem, grad_sem, out_sem, small_sem,
):
    ch = lax.axis_index("ch")
    other = 1 - ch
    rows_here, stretches, size, width = x_ref.shape
    full = 2 * width
    tokens = rows_here * size
    own_columns = pl.ds(aligned(ch * width, width), width)

    load_weight = pltpu.make_async_copy(weight_ref, weights, weight_sem)

    def params_of(index, source):
        return (
            pltpu.make_async_copy(source, params.at[ch, index], param_own.at[index]),
            pltpu.make_async_remote_copy(
                src_ref=source, dst_ref=params.at[ch, index], send_sem=param_send.at[index],
                recv_sem=param_recv.at[index], device_id={"ch": other}, device_id_type=MESH,
            ),
        )

    def exchange(stretch):
        return pltpu.make_async_remote_copy(
            src_ref=x_ref.at[:, stretch], dst_ref=both.at[:, stretch, :, own_columns],
            send_sem=send_sem.at[stretch], recv_sem=recv_sem.at[stretch],
            device_id={"ch": other}, device_id_type=MESH,
        )

    def keep_own(stretch):
        return pltpu.make_async_copy(x_ref.at[:, stretch], both.at[:, stretch, :, own_columns], own_sem.at[stretch])

    def load_grad(stretch):
        slot = stretch % 2
        return pltpu.make_async_copy(grad_ref.at[:, stretch], grad_in.at[slot], grad_sem.at[slot])

    def outputs(stretch):
        slot = stretch % 2
        rows = pl.ds(aligned(stretch * tokens, tokens), tokens)
        return tuple(
            pltpu.make_async_copy(source.at[slot], target, out_sem.at[index, slot])
            for index, (source, target) in enumerate((
                (saved, saved_ref.at[stretch]), (forget_out, forget_ref.at[stretch]), (normed_t, normed_t_ref.at[:, rows]), (mean_out, mean_ref.at[rows]),
                (scale_out, scale_ref.at[rows]), (mixed_out, mixed_ref.at[:, stretch]), (pass_out, pass_ref.at[rows]),
                (reset_out, reset_ref.at[rows]),
            ))
        )

    loads = [
        pltpu.make_async_copy(source, vectors.at[index], small_sem.at[index])
        for index, source in enumerate((forget_weight_in, reset_weight_in, forget_bias_in, reset_bias_in))
    ]
    load_weight.start()
    load_grad(0).start()
    for copy in loads:
        copy.start()
    barrier = pltpu.get_barrier_semaphore()
    pl.semaphore_signal(barrier, inc=1, device_id={"ch": other}, device_id_type=MESH)
    pl.semaphore_wait(barrier, 1)
    for index, source in enumerate((gain_ref, shift_ref)):
        for copy in params_of(index, source):
            copy.start()

    def begin(stretch, carry):
        exchange(stretch).start()
        keep_own(stretch).start()
        return carry

    lax.fori_loop(0, stretches, begin, 0)
    fill_keep(lengths_ref, keep)
    state_s[...] = jnp.zeros_like(state_s)
    sums_ref[...] = jnp.zeros_like(sums_ref)
    for index, source in enumerate((gain_ref, shift_ref)):
        for copy in params_of(index, source):
            copy.wait()
    for copy in loads:
        copy.wait()
    load_weight.wait()

    def work(stretch, carry):
        slot = stretch % 2
        keep_own(stretch).wait()
        exchange(stretch).wait()
        load_grad(stretch).wait()

        @pl.when(stretch + 1 < stretches)
        def _():
            load_grad(stretch + 1).start()

        @pl.when(stretch >= 2)
        def _():
            for copy in outputs(stretch - 2):
                copy.wait()

        for row in range(rows_here):
            @pl.loop(0, size // GROUP, unroll=4)
            def _(part):
                here = pl.ds(aligned(part * GROUP), GROUP)
                there = pl.ds(aligned(row * size + part * GROUP), GROUP)
                x = both[row, stretch, here, :].astype(F32)
                mean = jnp.sum(x, axis=1, keepdims=True) * (1.0 / full)
                centered = x - mean
                variance = jnp.sum(centered * centered, axis=1, keepdims=True) * (1.0 / full)
                scale = lax.rsqrt(variance + EPSILON)
                gain = jnp.concatenate([params[0, 0], params[1, 0]], axis=1)
                shift = jnp.concatenate([params[0, 1], params[1, 1]], axis=1)
                normed[there, :] = (centered * scale * gain + shift).astype(BF16)
                mean_out[slot, there, :] = jnp.broadcast_to(mean, (GROUP, LANES))
                scale_out[slot, there, :] = jnp.broadcast_to(scale, (GROUP, LANES))

        for gate in range(3):
            u[gate] = jnp.dot(normed[...], weights[gate], preferred_element_type=F32)

        for part in range(full // LANES):
            columns = slice(part * LANES, (part + 1) * LANES)
            normed_t[slot, columns, :] = normed[:, columns].T

        forget_weight, half_reset_weight, forget_bias, reset_bias = (0.5 * vectors[index] for index in range(4))

        def group(index, carry):
            state = list(carry[:rows_here])
            weight_sum, bias_sum = carry[rows_here:]
            here = pl.ds(aligned(index * GROUP), GROUP)
            there = [pl.ds(aligned(row * size + index * GROUP), GROUP) for row in range(rows_here)]
            spread = lambda value: value.astype(F32).reshape((GROUP,) + TILE)
            loaded = [
                (
                    spread(u[0, there[row], :]), spread(u[1, there[row], :]), spread(u[2, there[row], :]),
                    spread(both[row, stretch, here, own_columns]), spread(grad_in[slot, row, here, :]),
                )
                for row in range(rows_here)
            ]
            out = [([], [], []) for _ in range(rows_here)]
            held = [None] * rows_here
            for k in range(GROUP):
                time = index * GROUP + k
                for row in range(rows_here):
                    up_x, up_f, up_r, x, grad = (part[k] for part in loaded[row])
                    before = state[row] * keep[row, pl.ds(stretch * size + time, 1), :]
                    bent = jnp.tanh(0.5 * up_f + forget_bias + forget_weight * before)
                    gap = before - up_x
                    after = 0.5 * (before + up_x) + bent * (0.5 * gap)
                    state[row] = after
                    forget = 0.5 * bent + 0.5
                    reset = 0.5 * jnp.tanh(0.5 * up_r + reset_bias + half_reset_weight * before) + 0.5
                    over = after - x
                    direct = grad * reset
                    reset_grad = direct * over * (1.0 - reset)
                    forget_out[slot, row, time] = forget
                    kinds = (direct, gap * forget * (1.0 - forget), before)
                    if k % 2 == 0:
                        held[row] = kinds
                    else:
                        for kind in range(3):
                            both_steps = jnp.concatenate([held[row][kind], kinds[kind]], axis=0)
                            saved[slot, kind, row, index * (GROUP // 2) + k // 2] = both_steps.astype(BF16)
                    weight_sum = weight_sum + reset_grad * before
                    bias_sum = bias_sum + reset_grad
                    out[row][0].append(x + reset * over)
                    out[row][1].append(grad - direct)
                    out[row][2].append(reset_grad)
            flat = lambda parts: jnp.stack(parts).reshape(GROUP, width).astype(BF16)
            for row in range(rows_here):
                mixed_out[slot, row, here, :] = flat(out[row][0])
                pass_out[slot, there[row], :] = flat(out[row][1])
                reset_out[slot, there[row], :] = flat(out[row][2])
            return (*state, weight_sum, bias_sum)

        carried = lax.fori_loop(
            0, size // GROUP, group, (*[state_s[row] for row in range(rows_here)], sums_ref[0], sums_ref[1])
        )
        for row in range(rows_here):
            state_s[row] = carried[row]
        sums_ref[0] = carried[rows_here]
        sums_ref[1] = carried[rows_here + 1]
        for copy in outputs(stretch):
            copy.start()
        return carry

    lax.fori_loop(0, stretches, work, 0)
    for row in range(rows_here):
        final_ref[row:row + 1, :] = state_s[row].reshape(1, width)
    stores = [
        pltpu.make_async_copy(final_ref, final_out, small_sem.at[4]),
        pltpu.make_async_copy(sums_ref, sums_out, small_sem.at[5]),
    ]
    for copy in stores:
        copy.start()
    for stretch in (stretches - 2, stretches - 1):
        for copy in outputs(stretch):
            copy.wait()
    for copy in stores:
        copy.wait()


def project(lengths, x, gain, shift, weight, grad, forget_weight, reset_weight, forget_bias, reset_bias):
    rows_here, stretches, size, width = x.shape
    full = 2 * width
    part = rows_here * size
    tokens = part * stretches
    kept = (3, rows_here, size // 2, 2 * SUBLANES, LANES)
    kept_forget = (rows_here, size) + TILE
    dma = pltpu.SemaphoreType.DMA
    shape = jax.ShapeDtypeStruct
    return pl.pallas_call(
        project_kernel,
        out_shape=(
            shape((stretches,) + kept, BF16),
            shape((stretches,) + kept_forget, F32),
            shape((full, tokens), BF16),
            shape((tokens, LANES), F32),
            shape((tokens, LANES), F32),
            shape(x.shape, BF16),
            shape((tokens, width), BF16),
            shape((tokens, width), BF16),
            shape((rows_here, width), F32),
            shape((2,) + TILE, F32),
        ),
        in_specs=[IN_SMEM] + [ANY] * 9,
        out_specs=[ANY] * 10,
        scratch_shapes=[
            pltpu.VMEM((rows_here, stretches, size, full), BF16),
            pltpu.VMEM((3, full, width), BF16),
            pltpu.VMEM((2, 2, 1, width), F32),
            pltpu.VMEM((rows_here, stretches * size, LANES), F32),
            pltpu.VMEM((part, full), BF16),
            pltpu.VMEM((2, full, part), BF16),
            pltpu.VMEM((2, part, LANES), F32),
            pltpu.VMEM((2, part, LANES), F32),
            pltpu.VMEM((3, part, width), F32),
            pltpu.VMEM((2, rows_here, size, width), BF16),
            pltpu.VMEM((2,) + kept, BF16),
            pltpu.VMEM((2,) + kept_forget, F32),
            pltpu.VMEM((2, rows_here, size, width), BF16),
            pltpu.VMEM((2, part, width), BF16),
            pltpu.VMEM((2, part, width), BF16),
            pltpu.VMEM((rows_here,) + TILE, F32),
            pltpu.VMEM((4,) + TILE, F32),
            pltpu.VMEM((rows_here, width), F32),
            pltpu.VMEM((2,) + TILE, F32),
            dma((stretches,)), dma((stretches,)), dma((stretches,)), dma((2,)), dma((2,)), dma((2,)), dma, dma((2,)),
            dma((8, 2)), dma((6,)),
        ],
        compiler_params=pltpu.CompilerParams(
            collective_id=0, has_side_effects=True, vmem_limit_bytes=VMEM_LIMIT
        ),
        name="project",
    )(lengths, x, gain, shift, weight, grad, forget_weight, reset_weight, forget_bias, reset_bias)


JOB_ROWS = 128
PIECE = 16
QUARTER = 32
NORM_TOKENS = 256
HALF = 32
RING = 8
LONG = 12
SHORT = 4
SPLIT = 1
UNROLL = 4
HOP = 2
CORE = 1
AT_Y = CORE + HOP
AT_MIDDLE = AT_Y + HOP
AT_READY = AT_MIDDLE + HOP
AT_GATHER = AT_READY + HOP
AT_TWIN = AT_GATHER + HOP
MINE = AT_MIDDLE + 1
LATE = 3
PERIOD = 3
OFFSET = 3
MEET = 1
LEAVE = 2
KEPT = 3
AHEAD = 4


def finish_kernel(
    lengths_ref, saved_ref, forget_ref, normed_t_ref, reset_ref, weight_ref, x_ref, mean_ref, scale_ref, pass_ref, gain_in,
    forget_weight_in, reset_weight_in, sums_in,
    total_ref, input_grad_ref, small_out,
    du, weights, rows_in, mine, core_out, core_in, y_out, y_in, slab_out, slab_in, side_out, side_in, half_out, half_in,
    swap_out, swap_in, cross_out, cross_in,
    ready, dn_own, dn_out, dn_in, moment_own, moment_out, moment_in, x_in, pass_in, mean_in, scale_in, grad_out,
    norm_sums, keep, saved, forgets, state_s, gate_sums, small_own, small_in, small_z, gain_ref, vectors, sums_ref, small_ref,
    load_sem, rows_sem, saved_sem, core_send, core_recv, y_send, y_recv, slab_send, slab_recv, side_send, side_recv,
    half_send, half_recv, swap_send, swap_recv, cross_send, cross_recv, ready_sem,
    gather_send, gather_recv, over_send, over_recv, last_send, last_recv, pair_send, pair_recv, twin_send, twin_recv,
    dn_send, dn_recv, moment_send, moment_recv, norm_sem, grad_sem,
    small_send, small_recv, vector_sem,
):
    device = lax.axis_index("rows")
    devices = lax.axis_size("rows")
    ch = lax.axis_index("ch")
    z_stride, y_stride = devices // 4, devices // 8
    z = device // z_stride
    y = (device // y_stride) % 2
    core = device % 2
    twin = device + 1 - 2 * core
    pair = device + y_stride * (1 - 2 * y)
    full, tokens = normed_t_ref.shape
    rows_here, stretches, size, width = x_ref.shape
    half = full // 2
    narrow = width // SPLIT
    per_part = half // JOB_ROWS
    per_gate = per_part * SPLIT
    jobs = 3 * per_gate
    blocks = tokens // NORM_TOKENS

    def gate_of(job):
        return (job // per_gate + 2) % 3

    def place(job, whose):
        row = aligned(whose * half + (job // SPLIT % per_part) * JOB_ROWS, JOB_ROWS)
        column = aligned((job % SPLIT) * narrow, narrow)
        return gate_of(job), row, column

    outer = jnp.logical_or(z == 0, z == 3)
    inner = jnp.logical_not(outer)
    inward = device + z_stride * (1 - 2 * (z // 2))
    outward = device - z_stride * (1 - 2 * (z // 2))
    y_row, pair_row = aligned(3 * QUARTER * y, QUARTER), aligned(3 * QUARTER * (1 - y), QUARTER)
    own_half, other_half = aligned(QUARTER * (1 + z // 2), QUARTER), aligned(QUARTER * (2 - z // 2), QUARTER)

    load_reset = pltpu.make_async_copy(reset_ref, du.at[2], load_sem.at[3])

    def load_weight(gate):
        return pltpu.make_async_copy(weight_ref.at[gate], weights.at[gate], load_sem.at[gate])

    def load_rows(turn):
        slot = turn % 2
        own = aligned(core * half + (turn % per_part) * JOB_ROWS, JOB_ROWS)
        other = aligned((1 - core) * half + (turn % per_part) * JOB_ROWS, JOB_ROWS)
        return (
            pltpu.make_async_copy(
                normed_t_ref.at[pl.ds(own, JOB_ROWS)], rows_in.at[slot, pl.ds(0, JOB_ROWS)], rows_sem.at[0, slot]
            ),
            pltpu.make_async_copy(
                normed_t_ref.at[pl.ds(other, JOB_ROWS)], rows_in.at[slot, pl.ds(JOB_ROWS, JOB_ROWS)],
                rows_sem.at[1, slot],
            ),
        )

    def remote(source, target, send, recv, where):
        return pltpu.make_async_remote_copy(
            src_ref=source, dst_ref=target, send_sem=send, recv_sem=recv, device_id=where, device_id_type=MESH
        )

    def to_core(job):
        return remote(
            core_out.at[job % 2], core_in.at[job % SHORT], core_send.at[job % 2], core_recv.at[job % SHORT],
            {"rows": twin},
        )

    def to_y(job):
        return remote(
            y_out.at[job % SHORT], y_in.at[job % RING], y_send.at[job % SHORT], y_recv.at[job % RING], {"rows": pair}
        )

    def ring(source, target, send, recv, job, where, size=RING):
        return remote(
            source.at[job % SHORT], target.at[job % size], send.at[job % SHORT], recv.at[job % size], {"rows": where}
        )

    def to_slab(job):
        return ring(slab_out, slab_in, slab_send, slab_recv, job, inward, LONG)

    def to_side(job):
        return ring(side_out, side_in, side_send, side_recv, job, inward, LONG)

    def to_half(job):
        return ring(half_out, half_in, half_send, half_recv, job, inward)

    def to_swap(job):
        return ring(swap_out, swap_in, swap_send, swap_recv, job, inward)

    def to_cross(job):
        return ring(cross_out, cross_in, cross_send, cross_recv, job, pair)

    def result(job, offset, size, whose):
        gate, row, column = place(job, whose)
        return total_ref.at[gate, pl.ds(aligned(row + offset), size), pl.ds(column, narrow)]

    def keep_ready(job):
        return tuple(
            pltpu.make_async_copy(
                ready.at[job % SHORT, kind], result(job, row, QUARTER, core), ready_sem.at[kind, job % SHORT]
            )
            for kind, row in enumerate((y_row, own_half))
        )

    def gather(job):
        return tuple(
            remote(
                ready.at[job % SHORT, kind], result(job, row, QUARTER, core), gather_send.at[kind, job % LONG],
                gather_recv.at[kind, job % LONG], {"rows": outward},
            )
            for kind, row in enumerate((y_row, own_half))
        )

    def over(job):
        return remote(
            ready.at[job % SHORT, 1], result(job, own_half, QUARTER, core), over_send.at[job % LONG],
            over_recv.at[job % LONG], {"rows": inward},
        )

    def last_half(job):
        return remote(
            result(job, other_half, QUARTER, core), result(job, other_half, QUARTER, core), last_send.at[job % LONG],
            last_recv.at[job % LONG], {"rows": outward},
        )

    def to_pair(job, first=False):
        source = ready.at[job % SHORT, 0] if first else result(job, y_row, QUARTER, core)
        return remote(
            source, result(job, y_row, QUARTER, core), pair_send.at[job % LONG], pair_recv.at[job % LONG],
            {"rows": pair},
        )

    def to_twin(job):
        return remote(
            result(job, 0, JOB_ROWS, core), result(job, 0, JOB_ROWS, core),
            twin_send.at[job % LONG], twin_recv.at[job % LONG], {"rows": twin},
        )

    def to_partner(block):
        return remote(
            dn_out.at[block % KEPT], dn_in.at[block % RING], dn_send.at[block % KEPT], dn_recv.at[block % RING],
            {"ch": 1 - ch},
        )

    def moments(block):
        return remote(
            moment_out.at[block % 2], moment_in.at[block % RING], moment_send.at[block % 2],
            moment_recv.at[block % RING], {"ch": 1 - ch},
        )

    pieces = NORM_TOKENS // (rows_here * size)

    def first_row(block):
        return aligned(tokens - NORM_TOKENS * (block + 1), NORM_TOKENS)

    def load_norm(block):
        rows = pl.ds(first_row(block), NORM_TOKENS)
        slot = block % KEPT
        return tuple(
            pltpu.make_async_copy(source.at[rows], target.at[slot], norm_sem.at[index, slot])
            for index, (source, target) in enumerate(((pass_ref, pass_in), (mean_ref, mean_in), (scale_ref, scale_in)))
        ) + tuple(
            pltpu.make_async_copy(
                x_ref.at[:, stretches - pieces * (block + 1) + piece], x_in.at[slot, piece],
                norm_sem.at[3 + piece, slot],
            )
            for piece in range(pieces)
        )

    def store_grad(block):
        return tuple(
            pltpu.make_async_copy(
                grad_out.at[block % 2, piece], input_grad_ref.at[:, stretches - pieces * (block + 1) + piece],
                grad_sem.at[piece, block % 2],
            )
            for piece in range(pieces)
        )

    def load_saved(turn):
        slot, stretch, part = turn % AHEAD, stretches - 1 - turn // 2, 1 - turn % 2
        return (
            pltpu.make_async_copy(
                saved_ref.at[stretch, :, :, pl.ds(aligned(part * (HALF // 2), HALF // 2), HALF // 2)],
                saved.at[slot], saved_sem.at[0, slot],
            ),
            pltpu.make_async_copy(
                forget_ref.at[stretch, :, pl.ds(aligned(part * HALF, HALF), HALF)], forgets.at[slot],
                saved_sem.at[1, slot],
            ),
        )

    def small_twin():
        return remote(small_own, small_in.at[0], small_send.at[0], small_recv.at[0], {"rows": twin})

    def small_pair():
        return remote(small_own, small_in.at[1], small_send.at[1], small_recv.at[1], {"rows": pair})

    def small_column(away):
        there = (z + away) % 4
        return remote(
            small_own, small_z.at[z], small_send.at[1 + away], small_recv.at[1 + away],
            {"rows": device + (there - z) * z_stride},
        )

    loads = [
        pltpu.make_async_copy(source, target, vector_sem.at[index])
        for index, (source, target) in enumerate((
            (gain_in, gain_ref), (forget_weight_in, vectors.at[0]), (reset_weight_in, vectors.at[1]), (sums_in, sums_ref),
        ))
    ]
    store_small = pltpu.make_async_copy(small_ref, small_out, vector_sem.at[4])
    load_reset.start()
    for copy in loads:
        copy.start()
    for copy in load_rows(0):
        copy.start()
    for turn in range(AHEAD - 1):
        for copy in load_saved(turn):
            copy.start()

    def is_job(job):
        return jnp.logical_and(job >= 0, job < jobs)

    def is_block(block):
        return jnp.logical_and(block >= 0, block < blocks)

    def when(*conditions):
        return pl.when(functools.reduce(jnp.logical_and, conditions))

    def multiply(t):
        gate, slot, turn = gate_of(t), t % 2, t // SPLIT

        @pl.when(t % SPLIT == 0)
        def _():
            for copy in load_rows(turn):
                copy.wait()

        @when(t % SPLIT == 0, t + SPLIT < jobs)
        def _():
            for copy in load_rows(turn + 1):
                copy.start()

        columns = pl.ds(aligned((t % SPLIT) * narrow, narrow), narrow)
        product = jnp.dot(rows_in[turn % 2], du[gate, :, columns], preferred_element_type=F32)
        mine[t % MINE] = product[:JOB_ROWS]
        core_out[slot] = product[JOB_ROWS:].astype(BF16)

    barrier = pltpu.get_barrier_semaphore()
    for where in [{"rows": twin}, {"rows": pair}, {"ch": 1 - ch}] + [
        {"rows": device + ((z + away) % 4 - z) * z_stride} for away in (1, 2, 3)
    ]:
        pl.semaphore_signal(barrier, inc=1, device_id=where, device_id_type=MESH)
    norm_sums[...] = jnp.zeros_like(norm_sums)
    state_s[...] = jnp.zeros_like(state_s)
    gate_sums[...] = jnp.zeros_like(gate_sums)
    fill_keep(lengths_ref, keep)
    turns = 2 * stretches
    turns_tick = turns // per_gate
    load_reset.wait()
    for copy in loads:
        copy.wait()

    multiply(0)
    pl.semaphore_wait(barrier, 6)

    def tick(t, carry):
        job = t - AT_TWIN - 1

        @when(is_job(job))
        def _():
            to_twin(job).wait_recv()

        job = t - AT_TWIN

        @when(is_job(job), outer)
        def _():
            last_half(job).wait_recv()

        @when(is_job(job))
        def _():
            to_pair(job).wait_recv()
            to_twin(job).start()

        @when(is_job(job - LATE))
        def _():
            to_twin(job - LATE).wait_send()

        job = t - AT_GATHER

        @when(is_job(job), outer)
        def _():
            for copy in gather(job):
                copy.wait_recv()
            to_pair(job).start()

        @when(is_job(job), inner)
        def _():
            over(job).wait_recv()
            last_half(job).start()

        @when(is_job(job - LATE), outer)
        def _():
            to_pair(job - LATE).wait_send()

        @when(is_job(job - LATE), inner)
        def _():
            last_half(job - LATE).wait_send()

        job = t - AT_READY

        @when(is_job(job), inner)
        def _():
            slot = job % SHORT
            to_swap(job).wait_recv()
            ready[slot, 0] = (swap_out[slot].astype(F32) + swap_in[job % RING].astype(F32)).astype(BF16)
            to_cross(job).wait_recv()
            ready[slot, 1] = (cross_out[slot].astype(F32) + cross_in[job % RING].astype(F32)).astype(BF16)
            over(job).start()
            for copy in gather(job):
                copy.start()
            to_pair(job, True).start()
            for copy in keep_ready(job):
                copy.start()

        @when(is_job(job - LATE), inner)
        def _():
            over(job - LATE).wait_send()
            for copy in gather(job - LATE):
                copy.wait_send()
            to_pair(job - LATE, True).wait_send()
            for copy in keep_ready(job - LATE):
                copy.wait()

        job = t - AT_MIDDLE

        @when(is_job(job), inner)
        def _():
            slot = job % MINE
            to_half(job).wait_recv()
            mine[slot, pl.ds(own_half, QUARTER)] += half_in[job % RING].astype(F32)
            cross_out[job % SHORT] = mine[slot, pl.ds(own_half, QUARTER)].astype(BF16)
            to_cross(job).start()
            to_side(job).wait_recv()
            mine[slot, pl.ds(y_row, QUARTER)] += side_in[job % LONG].astype(F32)
            swap_out[job % SHORT] = mine[slot, pl.ds(y_row, QUARTER)].astype(BF16)
            to_swap(job).start()

        @when(is_job(job - LATE), inner)
        def _():
            to_cross(job - LATE).wait_send()
            to_swap(job - LATE).wait_send()

        job = t - AT_Y

        @when(is_job(job))
        def _():
            to_y(job).wait_recv()
            mine[job % MINE, pl.ds(y_row, QUARTER)] += y_in[job % RING].astype(F32)

        @when(is_job(job), outer)
        def _():
            side_out[job % SHORT] = mine[job % MINE, pl.ds(y_row, QUARTER)].astype(BF16)
            to_side(job).start()

        @when(is_job(job), inner)
        def _():
            slot = job % MINE
            to_slab(job).wait_recv()
            mine[slot, QUARTER:3 * QUARTER] += slab_in[job % LONG].astype(F32)
            half_out[job % SHORT] = mine[slot, pl.ds(other_half, QUARTER)].astype(BF16)
            to_half(job).start()

        @when(is_job(job - LATE), outer)
        def _():
            to_side(job - LATE).wait_send()

        @when(is_job(job - LATE), inner)
        def _():
            to_half(job - LATE).wait_send()

        job = t - CORE

        @when(is_job(job))
        def _():
            to_core(job).wait_recv()
            slot = job % MINE
            mine[slot] += core_in[job % SHORT].astype(F32)
            y_out[job % SHORT] = mine[slot, pl.ds(pair_row, QUARTER)].astype(BF16)
            to_y(job).start()

        @when(is_job(job), outer)
        def _():
            slab_out[job % SHORT] = mine[job % MINE, QUARTER:3 * QUARTER].astype(BF16)
            to_slab(job).start()

        @when(is_job(job - LATE))
        def _():
            to_y(job - LATE).wait_send()

        @when(is_job(job - LATE), outer)
        def _():
            to_slab(job - LATE).wait_send()

        @when(is_job(t - 2))
        def _():
            to_core(t - 2).wait_send()

        @when(t > 0, is_job(t))
        def _():
            multiply(t)

        @when(is_job(t))
        def _():
            to_core(t).start()

        @pl.when(t < per_gate)
        def _():
            forget_weight, reset_weight = vectors[0], vectors[1]

            def back_half(turn, carry):
                for copy in load_saved(turn):
                    copy.wait()

                @pl.when(turn + AHEAD - 1 < turns)
                def _():
                    for copy in load_saved(turn + AHEAD - 1):
                        copy.start()

                slot = turn % AHEAD
                stretch, start = stretches - 1 - turn // 2, (1 - turn % 2) * HALF

                def group(back, carry):
                    index = HALF // PIECE - 1 - back
                    running = list(carry[:rows_here])
                    weight_sum, bias_sum = carry[rows_here:]
                    out = [([None] * PIECE, [None] * PIECE) for _ in range(rows_here)]
                    rows = [
                        pl.ds(aligned((stretch * rows_here + row) * size + start + index * PIECE), PIECE)
                        for row in range(rows_here)
                    ]
                    resets = [du[2, rows[row], :].astype(F32).reshape((PIECE,) + TILE) for row in range(rows_here)]
                    pairs = [None] * rows_here
                    for k in range(PIECE - 1, -1, -1):
                        time = index * PIECE + k
                        for row in range(rows_here):
                            if k % 2:
                                pairs[row] = [
                                    saved[slot, kind, row, index * (PIECE // 2) + k // 2].astype(F32)
                                    for kind in range(3)
                                ]
                            lanes = slice(SUBLANES, 2 * SUBLANES) if k % 2 else slice(0, SUBLANES)
                            direct, slope, before = (pair[lanes] for pair in pairs[row])
                            forget = forgets[slot, row, time]
                            kept = keep[row, pl.ds(stretch * size + start + time, 1), :]
                            state_grad = direct + running[row]
                            through = (forget + slope * forget_weight) * kept
                            running[row] = through * state_grad + resets[row][k] * reset_weight * kept
                            forget_grad = state_grad * slope
                            weight_sum = weight_sum + forget_grad * before
                            bias_sum = bias_sum + forget_grad
                            out[row][0][k] = state_grad - state_grad * forget
                            out[row][1][k] = forget_grad
                    for row in range(rows_here):
                        for gate in range(2):
                            du[gate, rows[row], :] = jnp.stack(out[row][gate]).reshape(PIECE, width).astype(BF16)
                    return (*running, weight_sum, bias_sum)

                return lax.fori_loop(0, HALF // PIECE, group, carry)

            carried = lax.fori_loop(
                t * turns_tick, (t + 1) * turns_tick, back_half,
                (*[state_s[row] for row in range(rows_here)], gate_sums[0], gate_sums[1]),
            )
            for row in range(rows_here):
                state_s[row] = carried[row]
            gate_sums[0] = carried[rows_here]
            gate_sums[1] = carried[rows_here + 1]

        for gate in range(3):
            @pl.when(t == gate)
            def _():
                load_weight(gate).start()

        @pl.when(t == OFFSET)
        def _():
            for gate in range(3):
                load_weight(gate).wait()

        block, phase = (t - OFFSET) // PERIOD, (t - OFFSET) % PERIOD

        def split(index):
            each = size // PIECE
            return index // (rows_here * each), (index // each) % rows_here, pl.ds(aligned(index % each * PIECE), PIECE)

        def back(block, whose, part):
            rows = pl.ds(first_row(block), NORM_TOKENS)
            columns = pl.ds(aligned(whose * width + part * narrow, narrow), narrow)
            return sum(
                lax.dot_general(
                    du[gate, rows, :], weights[gate, columns, :], (((1,), (1,)), ((), ())),
                    preferred_element_type=F32,
                )
                for gate in range(3)
            )

        @when(is_block(block), phase < SPLIT)
        def _():
            columns = pl.ds(aligned(phase * narrow, narrow), narrow)
            dn_out[block % KEPT, :, columns] = back(block, 1 - ch, phase).astype(BF16)

        @when(is_block(block), phase == SPLIT - 1)
        def _():
            to_partner(block).start()

        @when(is_block(block - MEET + 1), phase == SPLIT)
        def _():
            for copy in load_norm(block - MEET + 1):
                copy.start()

        @when(is_block(block - MEET), phase >= SPLIT, phase < 2 * SPLIT)
        def _():
            columns = pl.ds(aligned((phase - SPLIT) * narrow, narrow), narrow)
            dn_own[(block - MEET) % KEPT, :, columns] = back(block - MEET, ch, phase - SPLIT)

        @when(is_block(block - MEET), phase == 2 * SPLIT)
        def _():
            now = block - MEET
            slot = now % KEPT
            to_partner(now).wait()
            for copy in load_norm(now):
                copy.wait()

            def part(index, sums):
                gain_sum, shift_sum = sums
                rows = pl.ds(aligned(index * PIECE), PIECE)
                piece, row, inner = split(index)
                dn = dn_own[slot, rows, :] + dn_in[now % RING, rows, :].astype(F32)
                dn_own[slot, rows, :] = dn
                scale = scale_in[slot, rows, 0:1]
                xhat = (x_in[slot, piece, row, inner, :].astype(F32) - mean_in[slot, rows, 0:1]) * scale
                gained = dn * xhat
                dxhat = dn * gain_ref[0:1, :]
                first = jnp.sum(dxhat, axis=1, keepdims=True)
                second = jnp.sum(dxhat * xhat, axis=1, keepdims=True)
                lane = lax.broadcasted_iota(jnp.int32, (PIECE, LANES), 1)
                moment_own[rows, :] = jnp.where(lane == 0, first, second)
                return (
                    gain_sum + gained[:SUBLANES] + gained[SUBLANES:], shift_sum + dn[:SUBLANES] + dn[SUBLANES:],
                )

            gain_sum, shift_sum = lax.fori_loop(
                0, NORM_TOKENS // PIECE, part, (norm_sums[0], norm_sums[1]), unroll=UNROLL
            )
            norm_sums[0] = gain_sum
            norm_sums[1] = shift_sum
            for part in range(NORM_TOKENS // LANES):
                moment_out[now % 2, part] = moment_own[part * LANES:(part + 1) * LANES, :].T[:SUBLANES]
            moments(now).start()

        @when(is_block(block - LEAVE), phase == PERIOD - 1)
        def _():
            now = block - LEAVE
            slot = now % KEPT
            moments(now).wait()
            for part in range(NORM_TOKENS // LANES):
                both = (moment_out[now % 2, part] + moment_in[now % RING, part]) * (1.0 / full)
                moment_own[part * LANES:(part + 1) * LANES, :] = jnp.concatenate([both] * (LANES // SUBLANES), axis=0).T

            @pl.loop(0, NORM_TOKENS // PIECE, unroll=UNROLL)
            def _(index):
                rows = pl.ds(aligned(index * PIECE), PIECE)
                piece, row, inner = split(index)
                first, second = moment_own[rows, 0:1], moment_own[rows, 1:2]
                scale = scale_in[slot, rows, 0:1]
                xhat = (x_in[slot, piece, row, inner, :].astype(F32) - mean_in[slot, rows, 0:1]) * scale
                back = scale * (dn_own[slot, rows, :] * gain_ref[0:1, :] - first - xhat * second)
                grad_out[now % 2, piece, row, inner, :] = (back + pass_in[slot, rows, :].astype(F32)).astype(BF16)

            for copy in store_grad(now):
                copy.start()

        @when(is_block(block - LEAVE - 1), phase == 0)
        def _():
            for copy in store_grad(block - LEAVE - 1):
                copy.wait()

        at = OFFSET + PERIOD * (blocks - 1 + MEET) + 2 * SPLIT + 1

        @pl.when(t == at)
        def _():
            small_own[...] = jnp.zeros_like(small_own)
            small_own[0:1] = gate_sums[0].reshape(1, width)
            small_own[1:2] = sums_ref[0].reshape(1, width)
            small_own[2:3] = gate_sums[1].reshape(1, width)
            small_own[3:4] = sums_ref[1].reshape(1, width)
            small_own[4:5] = jnp.sum(norm_sums[0], axis=0, keepdims=True)
            small_own[5:6] = jnp.sum(norm_sums[1], axis=0, keepdims=True)
            small_twin().start()

        @pl.when(t == at + 1)
        def _():
            small_twin().wait()
            small_own[...] += small_in[0]
            small_pair().start()

        @pl.when(t == at + 1 + HOP)
        def _():
            small_pair().wait()
            small_own[...] += small_in[1]
            for away in (1, 2, 3):
                small_column(away).start()

        @pl.when(t == at + 1 + 2 * HOP)
        def _():
            for away in (1, 2, 3):
                small_column(away).wait()
            small_z[z] = small_own[...]
            small_ref[...] = (small_z[0] + small_z[1]) + (small_z[2] + small_z[3])
            store_small.start()

        return carry

    last = max(
        jobs + AT_TWIN + LATE, OFFSET + PERIOD * (blocks + LEAVE) + 1,
        OFFSET + PERIOD * (blocks - 1 + MEET) + 2 * SPLIT + 3 + 2 * HOP,
    )
    lax.fori_loop(0, last, tick, 0)
    store_small.wait()


def finish(
    lengths, saved, forgets, normed_t, reset, weight, x, mean, scale, passed, gain, forget_weight, reset_weight,
    sums,
):
    full, tokens = normed_t.shape
    rows_here, stretches, size, width = x.shape
    dma = pltpu.SemaphoreType.DMA
    norm = NORM_TOKENS
    narrow = width // SPLIT
    pieces = norm // (rows_here * size)
    return pl.pallas_call(
        finish_kernel,
        out_shape=(
            jax.ShapeDtypeStruct((3, full, width), BF16),
            jax.ShapeDtypeStruct(x.shape, BF16),
            jax.ShapeDtypeStruct((SUBLANES, width), F32),
        ),
        in_specs=[IN_SMEM] + [ANY] * 13,
        out_specs=(ANY, ANY, ANY),
        scratch_shapes=[
            pltpu.VMEM((3, tokens, width), BF16),
            pltpu.VMEM((3, full, width), BF16),
            pltpu.VMEM((2, 2 * JOB_ROWS, tokens), BF16),
            pltpu.VMEM((MINE, JOB_ROWS, narrow), F32),
            pltpu.VMEM((2, JOB_ROWS, narrow), BF16),
            pltpu.VMEM((SHORT, JOB_ROWS, narrow), BF16),
            pltpu.VMEM((SHORT, QUARTER, narrow), BF16),
            pltpu.VMEM((RING, QUARTER, narrow), BF16),
            pltpu.VMEM((SHORT, 2 * QUARTER, narrow), BF16),
            pltpu.VMEM((LONG, 2 * QUARTER, narrow), BF16),
            pltpu.VMEM((SHORT, QUARTER, narrow), BF16),
            pltpu.VMEM((LONG, QUARTER, narrow), BF16),
            pltpu.VMEM((SHORT, QUARTER, narrow), BF16),
            pltpu.VMEM((RING, QUARTER, narrow), BF16),
            pltpu.VMEM((SHORT, QUARTER, narrow), BF16),
            pltpu.VMEM((RING, QUARTER, narrow), BF16),
            pltpu.VMEM((SHORT, QUARTER, narrow), BF16),
            pltpu.VMEM((RING, QUARTER, narrow), BF16),
            pltpu.VMEM((SHORT, 2, QUARTER, narrow), BF16),
            pltpu.VMEM((KEPT, norm, width), F32),
            pltpu.VMEM((KEPT, norm, width), BF16),
            pltpu.VMEM((RING, norm, width), BF16),
            pltpu.VMEM((norm, LANES), F32),
            pltpu.VMEM((2, norm // LANES, SUBLANES, LANES), F32),
            pltpu.VMEM((RING, norm // LANES, SUBLANES, LANES), F32),
            pltpu.VMEM((KEPT, pieces, rows_here, size, width), BF16),
            pltpu.VMEM((KEPT, norm, width), BF16),
            pltpu.VMEM((KEPT, norm, LANES), F32),
            pltpu.VMEM((KEPT, norm, LANES), F32),
            pltpu.VMEM((2, pieces, rows_here, size, width), BF16),
            pltpu.VMEM((2, SUBLANES, width), F32),
            pltpu.VMEM((rows_here, stretches * size, LANES), F32),
            pltpu.VMEM((AHEAD, 3, rows_here, HALF // 2, 2 * SUBLANES, LANES), BF16),
            pltpu.VMEM((AHEAD, rows_here, HALF) + TILE, F32),
            pltpu.VMEM((rows_here,) + TILE, F32),
            pltpu.VMEM((2,) + TILE, F32),
            pltpu.VMEM((SUBLANES, width), F32),
            pltpu.VMEM((2, SUBLANES, width), F32),
            pltpu.VMEM((4, SUBLANES, width), F32),
            pltpu.VMEM((1, width), F32),
            pltpu.VMEM((2,) + TILE, F32),
            pltpu.VMEM((2,) + TILE, F32),
            pltpu.VMEM((SUBLANES, width), F32),
            dma((4,)), dma((2, 2)), dma((2, AHEAD)),
            dma((2,)), dma((SHORT,)), dma((SHORT,)), dma((RING,)), dma((SHORT,)), dma((LONG,)),
            dma((SHORT,)), dma((LONG,)), dma((SHORT,)), dma((RING,)), dma((SHORT,)), dma((RING,)),
            dma((SHORT,)), dma((RING,)), dma((2, SHORT)),
            dma((2, LONG)), dma((2, LONG)), dma((LONG,)), dma((LONG,)), dma((LONG,)), dma((LONG,)),
            dma((LONG,)), dma((LONG,)), dma((LONG,)), dma((LONG,)),
            dma((KEPT,)), dma((RING,)), dma((2,)), dma((RING,)), dma((3 + pieces, KEPT)), dma((pieces, 2)),
            dma((5,)), dma((5,)), dma((5,)),
        ],
        compiler_params=pltpu.CompilerParams(
            collective_id=1, has_side_effects=True, vmem_limit_bytes=VMEM_LIMIT
        ),
        name="finish",
    )(
        lengths, saved, forgets, normed_t, reset, weight, x, mean, scale, passed, gain, forget_weight, reset_weight, sums
    )


COLLECT_PARTS = 4


def collect_kernel(
    total_ref, mixed_ref, input_grad_ref, final_ref, small_ref,
    weight_grad_ref, mixed_to, input_grad_to, final_out, gain_out, shift_out, forget_weight_out, reset_weight_out,
    forget_bias_out, reset_bias_out,
    narrow, wide, mixed, input_grad, final, small, vectors, in_sem, out_sem, pass_sem, small_sem, vector_sem,
):
    gates, full, _ = total_ref.shape
    rows = full // COLLECT_PARTS
    parts = [(gate, part) for gate in range(gates) for part in range(COLLECT_PARTS)]

    def take(index):
        gate, part = parts[index]
        here = pl.ds(part * rows, rows)
        return pltpu.make_async_copy(total_ref.at[gate, here], narrow.at[gate, here], in_sem.at[index])

    def give(index):
        gate, part = parts[index]
        here = pl.ds(part * rows, rows)
        return pltpu.make_async_copy(wide.at[gate, here], weight_grad_ref.at[gate, here], out_sem.at[index])

    passed = [
        (
            pltpu.make_async_copy(source, held, pass_sem.at[0, index]),
            pltpu.make_async_copy(held, target, pass_sem.at[1, index]),
        )
        for index, (source, held, target) in enumerate(
            ((mixed_ref, mixed, mixed_to), (input_grad_ref, input_grad, input_grad_to))
        )
    ]
    take_small = pltpu.make_async_copy(small_ref, small, small_sem.at[0])
    take_final = pltpu.make_async_copy(final_ref, final, small_sem.at[1])
    give_final = pltpu.make_async_copy(final, final_out, small_sem.at[2])
    outs = (forget_weight_out, reset_weight_out, forget_bias_out, reset_bias_out, gain_out, shift_out)
    give_vectors = [
        pltpu.make_async_copy(vectors.at[index], out, vector_sem.at[index]) for index, out in enumerate(outs)
    ]
    take_small.start()
    take_final.start()
    for index in range(len(parts)):
        take(index).start()
        if index == 1:
            passed[0][0].start()
        if index == 3:
            passed[1][0].start()
    take_small.wait()
    for index, copy in enumerate(give_vectors):
        vectors[index] = small[index:index + 1, :].reshape(TILE)
        copy.start()
    take_final.wait()
    give_final.start()
    for index, (gate, part) in enumerate(parts):
        take(index).wait()

        @pl.loop(0, rows // LANES)
        def _(step):
            here = pl.ds(aligned(part * rows + step * LANES, LANES), LANES)
            wide[gate, here, :] = narrow[gate, here, :].astype(F32)

        give(index).start()
        if index in (2, 4):
            copies = passed[index // 2 - 1]
            copies[0].wait()
            copies[1].start()
    for index in range(len(parts)):
        give(index).wait()
    for copies in passed:
        copies[1].wait()
    give_final.wait()
    for copy in give_vectors:
        copy.wait()


def collect(total, mixed, input_grad, final_state, small):
    shape = jax.ShapeDtypeStruct
    dma = pltpu.SemaphoreType.DMA
    parts = total.shape[0] * COLLECT_PARTS
    return pl.pallas_call(
        collect_kernel,
        out_shape=(
            shape(total.shape, F32), shape(mixed.shape, BF16), shape(input_grad.shape, BF16),
            shape(final_state.shape, F32),
        ) + (shape(TILE, F32),) * 6,
        in_specs=[ANY] * 5,
        out_specs=[ANY] * 10,
        scratch_shapes=[
            pltpu.VMEM(total.shape, BF16), pltpu.VMEM(total.shape, F32), pltpu.VMEM(mixed.shape, BF16),
            pltpu.VMEM(input_grad.shape, BF16), pltpu.VMEM(final_state.shape, F32), pltpu.VMEM(small.shape, F32),
            pltpu.VMEM((6,) + TILE, F32), dma((parts,)), dma((parts,)), dma((2, 2)), dma((3,)), dma((6,)),
        ],
        compiler_params=pltpu.CompilerParams(vmem_limit_bytes=VMEM_LIMIT),
        name="collect",
    )(total, mixed, input_grad, final_state, small)


def on_device(
    inputs, doc_lengths, layer_norm_gain, layer_norm_bias, weight, forget_weight, reset_weight, forget_bias,
    reset_bias, out_grad,
):
    rows_here, length, width = inputs.shape
    weights = jnp.transpose(weight, (1, 0, 2))
    stretched = (rows_here, length // STRETCH, STRETCH, width)
    x = inputs.reshape(stretched)
    gain = layer_norm_gain.reshape(1, width)
    vectors = [vector.reshape(TILE) for vector in (forget_weight, reset_weight, forget_bias, reset_bias)]
    saved, forgets, normed_t, mean, scale, mixed, passed, reset_grad, final_state, sums = project(
        doc_lengths, x, gain, layer_norm_bias.reshape(1, width), weights, out_grad.reshape(stretched), *vectors
    )
    weight_grad, input_grad, small = finish(
        doc_lengths, saved, forgets, normed_t, reset_grad, weights, x, mean, scale, passed, gain, vectors[0],
        vectors[1], sums,
    )
    weight_grad, mixed, input_grad, final_state, *vectors = collect(weight_grad, mixed, input_grad, final_state, small)
    devices = lax.axis_size("rows")
    groups = devices // 16
    if groups > 1:
        members = [[] for _ in range(devices // groups)]
        for device in range(devices):
            part, core = device // 2, device % 2
            members[(part // groups) * 2 + core].append(device)
        weight_grad, vectors = lax.psum((weight_grad, vectors), "rows", axis_index_groups=members)
    weight_grad = jnp.transpose(weight_grad, (1, 0, 2))
    return (
        mixed.reshape(inputs.shape), input_grad.reshape(inputs.shape), final_state, weight_grad,
        *[vector.reshape(width) for vector in vectors],
    )


def solution(mesh):
    rows_ch = P("rows", None, "ch")
    ch = P("ch")
    in_specs = (rows_ch, P("rows", None), ch, ch, P(None, None, "ch"), ch, ch, ch, ch, rows_ch)
    out_specs = (rows_ch, rows_ch, P("rows", "ch"), P(None, None, "ch"), ch, ch, ch, ch, ch, ch)
    return jax.shard_map(on_device, mesh=mesh, in_specs=in_specs, out_specs=out_specs, check_vma=False)
```

```python
import functools

import jax
import jax.numpy as jnp
from jax import lax
from jax.experimental import pallas as pl
from jax.experimental.pallas import tpu as pltpu
from jax.sharding import PartitionSpec as P

MESH = pl.DeviceIdType.MESH
F32 = jnp.float32
BF16 = jnp.bfloat16
EPSILON = 1e-05
LANES = 128
SUBLANES = 8
TILE = (SUBLANES, LANES)
STRETCH = 64
GROUP = 16
ANY = pl.BlockSpec(memory_space=pl.ANY)
IN_SMEM = pl.BlockSpec(memory_space=pltpu.SMEM)
VMEM_LIMIT = 60 * 1024 * 1024


def aligned(value, size=GROUP):
    return pl.multiple_of(value, size)


def fill_keep(lengths_ref, keep):
    rows_here, length = keep.shape[0], keep.shape[1]
    for row in range(rows_here):
        starts = [jnp.int32(0)]
        for document in range(lengths_ref.shape[1] - 1):
            starts.append(starts[-1] + lengths_ref[row, document])

        @pl.loop(0, length // LANES)
        def _(part):
            place = lax.broadcasted_iota(jnp.int32, (LANES, LANES), 0) + part * LANES
            value = jnp.ones((LANES, LANES), F32)
            for start in starts:
                value = jnp.where(place == start, 0.0, value)
            keep[row, pl.ds(aligned(part * LANES, LANES), LANES), :] = value


def project_kernel(
    lengths_ref, x_ref, gain_ref, shift_ref, weight_ref, grad_ref,
    forget_weight_in, reset_weight_in, forget_bias_in, reset_bias_in,
    saved_ref, forget_ref, normed_t_ref, mean_ref, scale_ref, mixed_ref, pass_ref, reset_ref, final_out, sums_out,
    both, weights, params, keep, normed, normed_t, mean_out, scale_out, u, grad_in, saved, forget_out, mixed_out, pass_out,
    reset_out, state_s, vectors, final_ref, sums_ref,
    send_sem, recv_sem, own_sem, param_own, param_send, param_recv, weight_sem, grad_sem, out_sem, small_sem,
):
    ch = lax.axis_index("ch")
    other = 1 - ch
    rows_here, stretches, size, width = x_ref.shape
    full = 2 * width
    tokens = rows_here * size
    own_columns = pl.ds(aligned(ch * width, width), width)

    load_weight = pltpu.make_async_copy(weight_ref, weights, weight_sem)

    def params_of(index, source):
        return (
            pltpu.make_async_copy(source, params.at[ch, index], param_own.at[index]),
            pltpu.make_async_remote_copy(
                src_ref=source, dst_ref=params.at[ch, index], send_sem=param_send.at[index],
                recv_sem=param_recv.at[index], device_id={"ch": other}, device_id_type=MESH,
            ),
        )

    def exchange(stretch, row):
        return pltpu.make_async_remote_copy(
            src_ref=x_ref.at[row, stretch], dst_ref=both.at[row, stretch, :, own_columns],
            send_sem=send_sem.at[row, stretch], recv_sem=recv_sem.at[row, stretch],
            device_id={"ch": other}, device_id_type=MESH,
        )

    def keep_own(stretch):
        return pltpu.make_async_copy(x_ref.at[:, stretch], both.at[:, stretch, :, own_columns], own_sem.at[stretch])

    def load_grad(stretch):
        slot = stretch % 2
        return pltpu.make_async_copy(grad_ref.at[:, stretch], grad_in.at[slot], grad_sem.at[slot])

    def outputs(stretch, kinds=slice(None)):
        slot = stretch % 2
        rows = pl.ds(aligned(stretch * tokens, tokens), tokens)
        return tuple(
            pltpu.make_async_copy(source.at[slot], target, out_sem.at[index, slot])
            for index, (source, target) in list(enumerate((
                (normed_t, normed_t_ref.at[:, rows]), (mean_out, mean_ref.at[rows]), (scale_out, scale_ref.at[rows]),
                (saved, saved_ref.at[stretch]), (forget_out, forget_ref.at[stretch]),
                (mixed_out, mixed_ref.at[:, stretch]), (pass_out, pass_ref.at[rows]), (reset_out, reset_ref.at[rows]),
            )))[kinds]
        )

    loads = [
        pltpu.make_async_copy(source, vectors.at[index], small_sem.at[index])
        for index, source in enumerate((forget_weight_in, reset_weight_in, forget_bias_in, reset_bias_in))
    ]
    load_weight.start()
    load_grad(0).start()
    for copy in loads:
        copy.start()
    barrier = pltpu.get_barrier_semaphore()
    pl.semaphore_signal(barrier, inc=1, device_id={"ch": other}, device_id_type=MESH)
    pl.semaphore_wait(barrier, 1)
    for index, source in enumerate((gain_ref, shift_ref)):
        for copy in params_of(index, source):
            copy.start()

    def begin(stretch, carry):
        for row in range(rows_here):
            exchange(stretch, row).start()
        keep_own(stretch).start()
        return carry

    lax.fori_loop(0, stretches, begin, 0)
    fill_keep(lengths_ref, keep)
    state_s[...] = jnp.zeros_like(state_s)
    sums_ref[...] = jnp.zeros_like(sums_ref)
    for index, source in enumerate((gain_ref, shift_ref)):
        for copy in params_of(index, source):
            copy.wait()
    for copy in loads:
        copy.wait()
    load_weight.wait()

    def work(stretch, carry):
        slot = stretch % 2
        keep_own(stretch).wait()
        load_grad(stretch).wait()

        @pl.when(stretch + 1 < stretches)
        def _():
            load_grad(stretch + 1).start()

        @pl.when(stretch >= 2)
        def _():
            for copy in outputs(stretch - 2):
                copy.wait()

        for row in range(rows_here):
            exchange(stretch, row).wait()

            @pl.loop(0, size // GROUP, unroll=4)
            def _(part):
                here = pl.ds(aligned(part * GROUP), GROUP)
                there = pl.ds(aligned(row * size + part * GROUP), GROUP)
                x = both[row, stretch, here, :].astype(F32)
                mean = jnp.sum(x, axis=1, keepdims=True) * (1.0 / full)
                centered = x - mean
                variance = jnp.sum(centered * centered, axis=1, keepdims=True) * (1.0 / full)
                scale = lax.rsqrt(variance + EPSILON)
                gain = jnp.concatenate([params[0, 0], params[1, 0]], axis=1)
                shift = jnp.concatenate([params[0, 1], params[1, 1]], axis=1)
                normed[there, :] = (centered * scale * gain + shift).astype(BF16)
                mean_out[slot, there, :] = jnp.broadcast_to(mean, (GROUP, LANES))
                scale_out[slot, there, :] = jnp.broadcast_to(scale, (GROUP, LANES))

        for gate in range(3):
            u[gate] = jnp.dot(normed[...], weights[gate], preferred_element_type=F32)

        for part in range(full // LANES):
            columns = slice(part * LANES, (part + 1) * LANES)
            normed_t[slot, columns, :] = normed[:, columns].T
        for copy in outputs(stretch, slice(0, 3)):
            copy.start()

        forget_weight, half_reset_weight, forget_bias, reset_bias = (0.5 * vectors[index] for index in range(4))

        def group(index, carry):
            state = list(carry[:rows_here])
            weight_sum, bias_sum = carry[rows_here:]
            here = pl.ds(aligned(index * GROUP), GROUP)
            there = [pl.ds(aligned(row * size + index * GROUP), GROUP) for row in range(rows_here)]
            spread = lambda value: value.astype(F32).reshape((GROUP,) + TILE)
            loaded = [
                (
                    spread(u[0, there[row], :]), spread(u[1, there[row], :]), spread(u[2, there[row], :]),
                    spread(both[row, stretch, here, own_columns]), spread(grad_in[slot, row, here, :]),
                )
                for row in range(rows_here)
            ]
            out = [([], [], []) for _ in range(rows_here)]
            held = [None] * rows_here
            for k in range(GROUP):
                time = index * GROUP + k
                for row in range(rows_here):
                    up_x, up_f, up_r, x, grad = (part[k] for part in loaded[row])
                    before = state[row] * keep[row, pl.ds(stretch * size + time, 1), :]
                    bent = jnp.tanh(0.5 * up_f + forget_bias + forget_weight * before)
                    gap = before - up_x
                    after = 0.5 * (before + up_x) + bent * (0.5 * gap)
                    state[row] = after
                    forget = 0.5 * bent + 0.5
                    reset = 0.5 * jnp.tanh(0.5 * up_r + reset_bias + half_reset_weight * before) + 0.5
                    over = after - x
                    direct = grad * reset
                    reset_grad = direct * over * (1.0 - reset)
                    forget_out[slot, row, time] = forget
                    kinds = (direct, gap * forget * (1.0 - forget), before)
                    if k % 2 == 0:
                        held[row] = kinds
                    else:
                        for kind in range(3):
                            both_steps = jnp.concatenate([held[row][kind], kinds[kind]], axis=0)
                            saved[slot, kind, row, index * (GROUP // 2) + k // 2] = both_steps.astype(BF16)
                    weight_sum = weight_sum + reset_grad * before
                    bias_sum = bias_sum + reset_grad
                    out[row][0].append(x + reset * over)
                    out[row][1].append(grad - direct)
                    out[row][2].append(reset_grad)
            flat = lambda parts: jnp.stack(parts).reshape(GROUP, width).astype(BF16)
            for row in range(rows_here):
                mixed_out[slot, row, here, :] = flat(out[row][0])
                pass_out[slot, there[row], :] = flat(out[row][1])
                reset_out[slot, there[row], :] = flat(out[row][2])
            return (*state, weight_sum, bias_sum)

        carried = lax.fori_loop(
            0, size // GROUP, group, (*[state_s[row] for row in range(rows_here)], sums_ref[0], sums_ref[1])
        )
        for row in range(rows_here):
            state_s[row] = carried[row]
        sums_ref[0] = carried[rows_here]
        sums_ref[1] = carried[rows_here + 1]
        for copy in outputs(stretch, slice(3, None)):
            copy.start()
        return carry

    lax.fori_loop(0, stretches, work, 0)
    for row in range(rows_here):
        final_ref[row:row + 1, :] = state_s[row].reshape(1, width)
    stores = [
        pltpu.make_async_copy(final_ref, final_out, small_sem.at[4]),
        pltpu.make_async_copy(sums_ref, sums_out, small_sem.at[5]),
    ]
    for copy in stores:
        copy.start()
    for stretch in (stretches - 2, stretches - 1):
        for copy in outputs(stretch):
            copy.wait()
    for copy in stores:
        copy.wait()


def project(lengths, x, gain, shift, weight, grad, forget_weight, reset_weight, forget_bias, reset_bias):
    rows_here, stretches, size, width = x.shape
    full = 2 * width
    part = rows_here * size
    tokens = part * stretches
    kept = (3, rows_here, size // 2, 2 * SUBLANES, LANES)
    kept_forget = (rows_here, size) + TILE
    dma = pltpu.SemaphoreType.DMA
    shape = jax.ShapeDtypeStruct
    return pl.pallas_call(
        project_kernel,
        out_shape=(
            shape((stretches,) + kept, BF16),
            shape((stretches,) + kept_forget, F32),
            shape((full, tokens), BF16),
            shape((tokens, LANES), F32),
            shape((tokens, LANES), F32),
            shape(x.shape, BF16),
            shape((tokens, width), BF16),
            shape((tokens, width), BF16),
            shape((rows_here, width), F32),
            shape((2,) + TILE, F32),
        ),
        in_specs=[IN_SMEM] + [ANY] * 9,
        out_specs=[ANY] * 10,
        scratch_shapes=[
            pltpu.VMEM((rows_here, stretches, size, full), BF16),
            pltpu.VMEM((3, full, width), BF16),
            pltpu.VMEM((2, 2, 1, width), F32),
            pltpu.VMEM((rows_here, stretches * size, LANES), F32),
            pltpu.VMEM((part, full), BF16),
            pltpu.VMEM((2, full, part), BF16),
            pltpu.VMEM((2, part, LANES), F32),
            pltpu.VMEM((2, part, LANES), F32),
            pltpu.VMEM((3, part, width), F32),
            pltpu.VMEM((2, rows_here, size, width), BF16),
            pltpu.VMEM((2,) + kept, BF16),
            pltpu.VMEM((2,) + kept_forget, F32),
            pltpu.VMEM((2, rows_here, size, width), BF16),
            pltpu.VMEM((2, part, width), BF16),
            pltpu.VMEM((2, part, width), BF16),
            pltpu.VMEM((rows_here,) + TILE, F32),
            pltpu.VMEM((4,) + TILE, F32),
            pltpu.VMEM((rows_here, width), F32),
            pltpu.VMEM((2,) + TILE, F32),
            dma((rows_here, stretches)), dma((rows_here, stretches)), dma((stretches,)), dma((2,)), dma((2,)), dma((2,)), dma, dma((2,)),
            dma((8, 2)), dma((6,)),
        ],
        compiler_params=pltpu.CompilerParams(
            collective_id=0, has_side_effects=True, vmem_limit_bytes=VMEM_LIMIT
        ),
        name="project",
    )(lengths, x, gain, shift, weight, grad, forget_weight, reset_weight, forget_bias, reset_bias)


JOB_ROWS = 128
PIECE = 16
QUARTER = 32
NORM_TOKENS = 256
HALF = 32
RING = 8
LONG = 12
SHORT = 4
SPLIT = 1
UNROLL = 8
HOP = 2
CORE = 1
AT_Y = CORE + HOP
AT_MIDDLE = AT_Y + HOP
AT_READY = AT_MIDDLE + HOP
AT_GATHER = AT_READY + HOP
AT_TWIN = AT_GATHER + HOP
MINE = AT_MIDDLE + 1
LATE = 3
PERIOD = 3
OFFSET = 3
MEET = 1
LEAVE = 2
KEPT = 3
AHEAD = 6


def finish_kernel(
    lengths_ref, saved_ref, forget_ref, normed_t_ref, reset_ref, weight_ref, x_ref, mean_ref, scale_ref, pass_ref, gain_in,
    forget_weight_in, reset_weight_in, sums_in,
    total_ref, input_grad_ref, small_out,
    du, weights, rows_in, mine, core_out, core_in, y_out, y_in, slab_out, slab_in, side_out, side_in, half_out, half_in,
    swap_out, swap_in, cross_out, cross_in,
    ready, dn_own, dn_out, dn_in, moment_own, moment_out, moment_in, x_in, pass_in, mean_in, scale_in, grad_out,
    norm_sums, keep, saved, forgets, state_s, gate_sums, small_own, small_in, small_z, gain_ref, vectors, sums_ref, small_ref,
    load_sem, rows_sem, saved_sem, core_send, core_recv, y_send, y_recv, slab_send, slab_recv, side_send, side_recv,
    half_send, half_recv, swap_send, swap_recv, cross_send, cross_recv, ready_sem,
    gather_send, gather_recv, over_send, over_recv, last_send, last_recv, pair_send, pair_recv, twin_send, twin_recv,
    dn_send, dn_recv, moment_send, moment_recv, norm_sem, grad_sem,
    small_send, small_recv, vector_sem,
):
    device = lax.axis_index("rows")
    devices = lax.axis_size("rows")
    ch = lax.axis_index("ch")
    z_stride, y_stride = devices // 4, devices // 8
    z = device // z_stride
    y = (device // y_stride) % 2
    core = device % 2
    twin = device + 1 - 2 * core
    pair = device + y_stride * (1 - 2 * y)
    full, tokens = normed_t_ref.shape
    rows_here, stretches, size, width = x_ref.shape
    half = full // 2
    narrow = width // SPLIT
    per_part = half // JOB_ROWS
    per_gate = per_part * SPLIT
    jobs = 3 * per_gate
    blocks = tokens // NORM_TOKENS

    def gate_of(job):
        return (job // per_gate + 2) % 3

    def place(job, whose):
        row = aligned(whose * half + (job // SPLIT % per_part) * JOB_ROWS, JOB_ROWS)
        column = aligned((job % SPLIT) * narrow, narrow)
        return gate_of(job), row, column

    outer = jnp.logical_or(z == 0, z == 3)
    inner = jnp.logical_not(outer)
    inward = device + z_stride * (1 - 2 * (z // 2))
    outward = device - z_stride * (1 - 2 * (z // 2))
    y_row, pair_row = aligned(3 * QUARTER * y, QUARTER), aligned(3 * QUARTER * (1 - y), QUARTER)
    own_half, other_half = aligned(QUARTER * (1 + z // 2), QUARTER), aligned(QUARTER * (2 - z // 2), QUARTER)

    load_reset = pltpu.make_async_copy(reset_ref, du.at[2], load_sem.at[3])

    def load_weight(gate):
        return pltpu.make_async_copy(weight_ref.at[gate], weights.at[gate], load_sem.at[gate])

    def load_rows(turn):
        slot = turn % 2
        own = aligned(core * half + (turn % per_part) * JOB_ROWS, JOB_ROWS)
        other = aligned((1 - core) * half + (turn % per_part) * JOB_ROWS, JOB_ROWS)
        return (
            pltpu.make_async_copy(
                normed_t_ref.at[pl.ds(own, JOB_ROWS)], rows_in.at[slot, pl.ds(0, JOB_ROWS)], rows_sem.at[0, slot]
            ),
            pltpu.make_async_copy(
                normed_t_ref.at[pl.ds(other, JOB_ROWS)], rows_in.at[slot, pl.ds(JOB_ROWS, JOB_ROWS)],
                rows_sem.at[1, slot],
            ),
        )

    def remote(source, target, send, recv, where):
        return pltpu.make_async_remote_copy(
            src_ref=source, dst_ref=target, send_sem=send, recv_sem=recv, device_id=where, device_id_type=MESH
        )

    def to_core(job):
        return remote(
            core_out.at[job % 2], core_in.at[job % SHORT], core_send.at[job % 2], core_recv.at[job % SHORT],
            {"rows": twin},
        )

    def to_y(job):
        return remote(
            y_out.at[job % SHORT], y_in.at[job % RING], y_send.at[job % SHORT], y_recv.at[job % RING], {"rows": pair}
        )

    def ring(source, target, send, recv, job, where, size=RING):
        return remote(
            source.at[job % SHORT], target.at[job % size], send.at[job % SHORT], recv.at[job % size], {"rows": where}
        )

    def to_slab(job):
        return ring(slab_out, slab_in, slab_send, slab_recv, job, inward, LONG)

    def to_side(job):
        return ring(side_out, side_in, side_send, side_recv, job, inward, LONG)

    def to_half(job):
        return ring(half_out, half_in, half_send, half_recv, job, inward)

    def to_swap(job):
        return ring(swap_out, swap_in, swap_send, swap_recv, job, inward)

    def to_cross(job):
        return ring(cross_out, cross_in, cross_send, cross_recv, job, pair)

    def result(job, offset, size, whose):
        gate, row, column = place(job, whose)
        return total_ref.at[gate, pl.ds(aligned(row + offset), size), pl.ds(column, narrow)]

    def keep_ready(job):
        return tuple(
            pltpu.make_async_copy(
                ready.at[job % SHORT, kind], result(job, row, QUARTER, core), ready_sem.at[kind, job % SHORT]
            )
            for kind, row in enumerate((y_row, own_half))
        )

    def gather(job):
        return tuple(
            remote(
                ready.at[job % SHORT, kind], result(job, row, QUARTER, core), gather_send.at[kind, job % LONG],
                gather_recv.at[kind, job % LONG], {"rows": outward},
            )
            for kind, row in enumerate((y_row, own_half))
        )

    def over(job):
        return remote(
            ready.at[job % SHORT, 1], result(job, own_half, QUARTER, core), over_send.at[job % LONG],
            over_recv.at[job % LONG], {"rows": inward},
        )

    def last_half(job):
        return remote(
            result(job, other_half, QUARTER, core), result(job, other_half, QUARTER, core), last_send.at[job % LONG],
            last_recv.at[job % LONG], {"rows": outward},
        )

    def to_pair(job, first=False):
        source = ready.at[job % SHORT, 0] if first else result(job, y_row, QUARTER, core)
        return remote(
            source, result(job, y_row, QUARTER, core), pair_send.at[job % LONG], pair_recv.at[job % LONG],
            {"rows": pair},
        )

    def to_twin(job):
        return remote(
            result(job, 0, JOB_ROWS, core), result(job, 0, JOB_ROWS, core),
            twin_send.at[job % LONG], twin_recv.at[job % LONG], {"rows": twin},
        )

    def to_partner(block):
        return remote(
            dn_out.at[block % KEPT], dn_in.at[block % RING], dn_send.at[block % KEPT], dn_recv.at[block % RING],
            {"ch": 1 - ch},
        )

    def moments(block):
        return remote(
            moment_out.at[block % 2], moment_in.at[block % RING], moment_send.at[block % 2],
            moment_recv.at[block % RING], {"ch": 1 - ch},
        )

    pieces = NORM_TOKENS // (rows_here * size)

    def first_row(block):
        return aligned(tokens - NORM_TOKENS * (block + 1), NORM_TOKENS)

    def load_norm(block):
        rows = pl.ds(first_row(block), NORM_TOKENS)
        slot = block % KEPT
        return tuple(
            pltpu.make_async_copy(source.at[rows], target.at[slot], norm_sem.at[index, slot])
            for index, (source, target) in enumerate(((pass_ref, pass_in), (mean_ref, mean_in), (scale_ref, scale_in)))
        ) + tuple(
            pltpu.make_async_copy(
                x_ref.at[:, stretches - pieces * (block + 1) + piece], x_in.at[slot, piece],
                norm_sem.at[3 + piece, slot],
            )
            for piece in range(pieces)
        )

    def store_grad(block):
        return tuple(
            pltpu.make_async_copy(
                grad_out.at[block % 2, piece], input_grad_ref.at[:, stretches - pieces * (block + 1) + piece],
                grad_sem.at[piece, block % 2],
            )
            for piece in range(pieces)
        )

    def load_saved(turn):
        slot, stretch, part = turn % AHEAD, stretches - 1 - turn // 2, 1 - turn % 2
        return (
            pltpu.make_async_copy(
                saved_ref.at[stretch, :, :, pl.ds(aligned(part * (HALF // 2), HALF // 2), HALF // 2)],
                saved.at[slot], saved_sem.at[0, slot],
            ),
            pltpu.make_async_copy(
                forget_ref.at[stretch, :, pl.ds(aligned(part * HALF, HALF), HALF)], forgets.at[slot],
                saved_sem.at[1, slot],
            ),
        )

    def small_twin():
        return remote(small_own, small_in.at[0], small_send.at[0], small_recv.at[0], {"rows": twin})

    def small_pair():
        return remote(small_own, small_in.at[1], small_send.at[1], small_recv.at[1], {"rows": pair})

    def small_column(away):
        there = (z + away) % 4
        return remote(
            small_own, small_z.at[z], small_send.at[1 + away], small_recv.at[1 + away],
            {"rows": device + (there - z) * z_stride},
        )

    loads = [
        pltpu.make_async_copy(source, target, vector_sem.at[index])
        for index, (source, target) in enumerate((
            (gain_in, gain_ref), (forget_weight_in, vectors.at[0]), (reset_weight_in, vectors.at[1]), (sums_in, sums_ref),
        ))
    ]
    store_small = pltpu.make_async_copy(small_ref, small_out, vector_sem.at[4])
    load_reset.start()
    for copy in loads:
        copy.start()
    for copy in load_rows(0):
        copy.start()
    for turn in range(AHEAD - 1):
        for copy in load_saved(turn):
            copy.start()

    def is_job(job):
        return jnp.logical_and(job >= 0, job < jobs)

    def is_block(block):
        return jnp.logical_and(block >= 0, block < blocks)

    def when(*conditions):
        return pl.when(functools.reduce(jnp.logical_and, conditions))

    def multiply(t):
        gate, slot, turn = gate_of(t), t % 2, t // SPLIT

        @pl.when(t % SPLIT == 0)
        def _():
            for copy in load_rows(turn):
                copy.wait()

        @when(t % SPLIT == 0, t + SPLIT < jobs)
        def _():
            for copy in load_rows(turn + 1):
                copy.start()

        columns = pl.ds(aligned((t % SPLIT) * narrow, narrow), narrow)
        product = jnp.dot(rows_in[turn % 2], du[gate, :, columns], preferred_element_type=F32)
        mine[t % MINE] = product[:JOB_ROWS]
        core_out[slot] = product[JOB_ROWS:].astype(BF16)

    barrier = pltpu.get_barrier_semaphore()
    for where in [{"rows": twin}, {"rows": pair}, {"ch": 1 - ch}] + [
        {"rows": device + ((z + away) % 4 - z) * z_stride} for away in (1, 2, 3)
    ]:
        pl.semaphore_signal(barrier, inc=1, device_id=where, device_id_type=MESH)
    norm_sums[...] = jnp.zeros_like(norm_sums)
    state_s[...] = jnp.zeros_like(state_s)
    gate_sums[...] = jnp.zeros_like(gate_sums)
    fill_keep(lengths_ref, keep)
    turns = 2 * stretches
    turns_tick = turns // per_gate
    load_reset.wait()
    for copy in loads:
        copy.wait()

    multiply(0)
    pl.semaphore_wait(barrier, 6)

    def tick(t, carry):
        job = t - AT_TWIN - 1

        @when(is_job(job))
        def _():
            to_twin(job).wait_recv()

        job = t - AT_TWIN

        @when(is_job(job), outer)
        def _():
            last_half(job).wait_recv()

        @when(is_job(job))
        def _():
            to_pair(job).wait_recv()
            to_twin(job).start()

        @when(is_job(job - LATE))
        def _():
            to_twin(job - LATE).wait_send()

        job = t - AT_GATHER

        @when(is_job(job), outer)
        def _():
            for copy in gather(job):
                copy.wait_recv()
            to_pair(job).start()

        @when(is_job(job), inner)
        def _():
            over(job).wait_recv()
            last_half(job).start()

        @when(is_job(job - LATE), outer)
        def _():
            to_pair(job - LATE).wait_send()

        @when(is_job(job - LATE), inner)
        def _():
            last_half(job - LATE).wait_send()

        job = t - AT_READY

        @when(is_job(job), inner)
        def _():
            slot = job % SHORT
            to_swap(job).wait_recv()
            ready[slot, 0] = (swap_out[slot].astype(F32) + swap_in[job % RING].astype(F32)).astype(BF16)
            to_cross(job).wait_recv()
            ready[slot, 1] = (cross_out[slot].astype(F32) + cross_in[job % RING].astype(F32)).astype(BF16)
            over(job).start()
            for copy in gather(job):
                copy.start()
            to_pair(job, True).start()
            for copy in keep_ready(job):
                copy.start()

        @when(is_job(job - LATE), inner)
        def _():
            over(job - LATE).wait_send()
            for copy in gather(job - LATE):
                copy.wait_send()
            to_pair(job - LATE, True).wait_send()
            for copy in keep_ready(job - LATE):
                copy.wait()

        job = t - AT_MIDDLE

        @when(is_job(job), inner)
        def _():
            slot = job % MINE
            to_half(job).wait_recv()
            mine[slot, pl.ds(own_half, QUARTER)] += half_in[job % RING].astype(F32)
            cross_out[job % SHORT] = mine[slot, pl.ds(own_half, QUARTER)].astype(BF16)
            to_cross(job).start()
            to_side(job).wait_recv()
            mine[slot, pl.ds(y_row, QUARTER)] += side_in[job % LONG].astype(F32)
            swap_out[job % SHORT] = mine[slot, pl.ds(y_row, QUARTER)].astype(BF16)
            to_swap(job).start()

        @when(is_job(job - LATE), inner)
        def _():
            to_cross(job - LATE).wait_send()
            to_swap(job - LATE).wait_send()

        job = t - AT_Y

        @when(is_job(job))
        def _():
            to_y(job).wait_recv()
            mine[job % MINE, pl.ds(y_row, QUARTER)] += y_in[job % RING].astype(F32)

        @when(is_job(job), outer)
        def _():
            side_out[job % SHORT] = mine[job % MINE, pl.ds(y_row, QUARTER)].astype(BF16)
            to_side(job).start()

        @when(is_job(job), inner)
        def _():
            slot = job % MINE
            to_slab(job).wait_recv()
            mine[slot, QUARTER:3 * QUARTER] += slab_in[job % LONG].astype(F32)
            half_out[job % SHORT] = mine[slot, pl.ds(other_half, QUARTER)].astype(BF16)
            to_half(job).start()

        @when(is_job(job - LATE), outer)
        def _():
            to_side(job - LATE).wait_send()

        @when(is_job(job - LATE), inner)
        def _():
            to_half(job - LATE).wait_send()

        job = t - CORE

        @when(is_job(job))
        def _():
            to_core(job).wait_recv()
            slot = job % MINE
            mine[slot] += core_in[job % SHORT].astype(F32)
            y_out[job % SHORT] = mine[slot, pl.ds(pair_row, QUARTER)].astype(BF16)
            to_y(job).start()

        @when(is_job(job), outer)
        def _():
            slab_out[job % SHORT] = mine[job % MINE, QUARTER:3 * QUARTER].astype(BF16)
            to_slab(job).start()

        @when(is_job(job - LATE))
        def _():
            to_y(job - LATE).wait_send()

        @when(is_job(job - LATE), outer)
        def _():
            to_slab(job - LATE).wait_send()

        @when(is_job(t - 2))
        def _():
            to_core(t - 2).wait_send()

        @when(t > 0, is_job(t))
        def _():
            multiply(t)

        @when(is_job(t))
        def _():
            to_core(t).start()

        @pl.when(t < per_gate)
        def _():
            forget_weight, reset_weight = vectors[0], vectors[1]

            def back_half(turn, carry):
                for copy in load_saved(turn):
                    copy.wait()

                @pl.when(turn + AHEAD - 1 < turns)
                def _():
                    for copy in load_saved(turn + AHEAD - 1):
                        copy.start()

                slot = turn % AHEAD
                stretch, start = stretches - 1 - turn // 2, (1 - turn % 2) * HALF

                def group(back, carry):
                    index = HALF // PIECE - 1 - back
                    running = list(carry[:rows_here])
                    weight_sum, bias_sum = carry[rows_here:]
                    out = [([None] * PIECE, [None] * PIECE) for _ in range(rows_here)]
                    rows = [
                        pl.ds(aligned((stretch * rows_here + row) * size + start + index * PIECE), PIECE)
                        for row in range(rows_here)
                    ]
                    resets = [du[2, rows[row], :].astype(F32).reshape((PIECE,) + TILE) for row in range(rows_here)]
                    pairs = [None] * rows_here
                    for k in range(PIECE - 1, -1, -1):
                        time = index * PIECE + k
                        for row in range(rows_here):
                            if k % 2:
                                pairs[row] = [
                                    saved[slot, kind, row, index * (PIECE // 2) + k // 2].astype(F32)
                                    for kind in range(3)
                                ]
                            lanes = slice(SUBLANES, 2 * SUBLANES) if k % 2 else slice(0, SUBLANES)
                            direct, slope, before = (pair[lanes] for pair in pairs[row])
                            forget = forgets[slot, row, time]
                            kept = keep[row, pl.ds(stretch * size + start + time, 1), :]
                            state_grad = direct + running[row]
                            through = (forget + slope * forget_weight) * kept
                            running[row] = through * state_grad + resets[row][k] * reset_weight * kept
                            forget_grad = state_grad * slope
                            weight_sum = weight_sum + forget_grad * before
                            bias_sum = bias_sum + forget_grad
                            out[row][0][k] = state_grad - state_grad * forget
                            out[row][1][k] = forget_grad
                    for row in range(rows_here):
                        for gate in range(2):
                            du[gate, rows[row], :] = jnp.stack(out[row][gate]).reshape(PIECE, width).astype(BF16)
                    return (*running, weight_sum, bias_sum)

                return lax.fori_loop(0, HALF // PIECE, group, carry)

            carried = lax.fori_loop(
                t * turns_tick, (t + 1) * turns_tick, back_half,
                (*[state_s[row] for row in range(rows_here)], gate_sums[0], gate_sums[1]),
            )
            for row in range(rows_here):
                state_s[row] = carried[row]
            gate_sums[0] = carried[rows_here]
            gate_sums[1] = carried[rows_here + 1]

        for gate in range(3):
            @pl.when(t == gate)
            def _():
                load_weight(gate).start()

        @pl.when(t == OFFSET)
        def _():
            for gate in range(3):
                load_weight(gate).wait()

        block, phase = (t - OFFSET) // PERIOD, (t - OFFSET) % PERIOD

        def split(index):
            each = size // PIECE
            return index // (rows_here * each), (index // each) % rows_here, pl.ds(aligned(index % each * PIECE), PIECE)

        def back(block, whose, part):
            rows = pl.ds(first_row(block), NORM_TOKENS)
            columns = pl.ds(aligned(whose * width + part * narrow, narrow), narrow)
            return sum(
                lax.dot_general(
                    du[gate, rows, :], weights[gate, columns, :], (((1,), (1,)), ((), ())),
                    preferred_element_type=F32,
                )
                for gate in range(3)
            )

        @when(is_block(block), phase < SPLIT)
        def _():
            columns = pl.ds(aligned(phase * narrow, narrow), narrow)
            dn_out[block % KEPT, :, columns] = back(block, 1 - ch, phase).astype(BF16)

        @when(is_block(block), phase == SPLIT - 1)
        def _():
            to_partner(block).start()

        @when(is_block(block - MEET + 1), phase == SPLIT)
        def _():
            for copy in load_norm(block - MEET + 1):
                copy.start()

        @when(is_block(block - MEET), phase >= SPLIT, phase < 2 * SPLIT)
        def _():
            columns = pl.ds(aligned((phase - SPLIT) * narrow, narrow), narrow)
            dn_own[(block - MEET) % KEPT, :, columns] = back(block - MEET, ch, phase - SPLIT)

        @when(is_block(block - MEET), phase == 2 * SPLIT)
        def _():
            now = block - MEET
            slot = now % KEPT
            to_partner(now).wait()
            for copy in load_norm(now):
                copy.wait()

            def part(index, sums):
                gain_sum, shift_sum = sums
                rows = pl.ds(aligned(index * PIECE), PIECE)
                piece, row, inner = split(index)
                dn = dn_own[slot, rows, :] + dn_in[now % RING, rows, :].astype(F32)
                dn_own[slot, rows, :] = dn
                scale = scale_in[slot, rows, 0:1]
                xhat = (x_in[slot, piece, row, inner, :].astype(F32) - mean_in[slot, rows, 0:1]) * scale
                gained = dn * xhat
                dxhat = dn * gain_ref[0:1, :]
                first = jnp.sum(dxhat, axis=1, keepdims=True)
                second = jnp.sum(dxhat * xhat, axis=1, keepdims=True)
                lane = lax.broadcasted_iota(jnp.int32, (PIECE, LANES), 1)
                moment_own[rows, :] = jnp.where(lane == 0, first, second)
                return (
                    gain_sum + gained[:SUBLANES] + gained[SUBLANES:], shift_sum + dn[:SUBLANES] + dn[SUBLANES:],
                )

            gain_sum, shift_sum = lax.fori_loop(
                0, NORM_TOKENS // PIECE, part, (norm_sums[0], norm_sums[1]), unroll=UNROLL
            )
            norm_sums[0] = gain_sum
            norm_sums[1] = shift_sum
            for part in range(NORM_TOKENS // LANES):
                moment_out[now % 2, part] = moment_own[part * LANES:(part + 1) * LANES, :].T[:SUBLANES]
            moments(now).start()

        @when(is_block(block - LEAVE), phase == PERIOD - 1)
        def _():
            now = block - LEAVE
            slot = now % KEPT
            moments(now).wait()
            for part in range(NORM_TOKENS // LANES):
                both = (moment_out[now % 2, part] + moment_in[now % RING, part]) * (1.0 / full)
                moment_own[part * LANES:(part + 1) * LANES, :] = jnp.concatenate([both] * (LANES // SUBLANES), axis=0).T

            @pl.loop(0, NORM_TOKENS // PIECE, unroll=UNROLL)
            def _(index):
                rows = pl.ds(aligned(index * PIECE), PIECE)
                piece, row, inner = split(index)
                first, second = moment_own[rows, 0:1], moment_own[rows, 1:2]
                scale = scale_in[slot, rows, 0:1]
                xhat = (x_in[slot, piece, row, inner, :].astype(F32) - mean_in[slot, rows, 0:1]) * scale
                back = scale * (dn_own[slot, rows, :] * gain_ref[0:1, :] - first - xhat * second)
                grad_out[now % 2, piece, row, inner, :] = (back + pass_in[slot, rows, :].astype(F32)).astype(BF16)

            for copy in store_grad(now):
                copy.start()

        @when(is_block(block - LEAVE - 1), phase == 0)
        def _():
            for copy in store_grad(block - LEAVE - 1):
                copy.wait()

        at = OFFSET + PERIOD * (blocks - 1 + MEET) + 2 * SPLIT + 1

        @pl.when(t == at)
        def _():
            small_own[...] = jnp.zeros_like(small_own)
            small_own[0:1] = gate_sums[0].reshape(1, width)
            small_own[1:2] = sums_ref[0].reshape(1, width)
            small_own[2:3] = gate_sums[1].reshape(1, width)
            small_own[3:4] = sums_ref[1].reshape(1, width)
            small_own[4:5] = jnp.sum(norm_sums[0], axis=0, keepdims=True)
            small_own[5:6] = jnp.sum(norm_sums[1], axis=0, keepdims=True)
            small_twin().start()

        @pl.when(t == at + 1)
        def _():
            small_twin().wait()
            small_own[...] += small_in[0]
            small_pair().start()

        @pl.when(t == at + 1 + HOP)
        def _():
            small_pair().wait()
            small_own[...] += small_in[1]
            for away in (1, 2, 3):
                small_column(away).start()

        @pl.when(t == at + 1 + 2 * HOP)
        def _():
            for away in (1, 2, 3):
                small_column(away).wait()
            small_z[z] = small_own[...]
            small_ref[...] = (small_z[0] + small_z[1]) + (small_z[2] + small_z[3])
            store_small.start()

        return carry

    last = max(
        jobs + AT_TWIN + LATE, OFFSET + PERIOD * (blocks + LEAVE) + 1,
        OFFSET + PERIOD * (blocks - 1 + MEET) + 2 * SPLIT + 3 + 2 * HOP,
    )
    lax.fori_loop(0, last, tick, 0)
    store_small.wait()


def finish(
    lengths, saved, forgets, normed_t, reset, weight, x, mean, scale, passed, gain, forget_weight, reset_weight,
    sums,
):
    full, tokens = normed_t.shape
    rows_here, stretches, size, width = x.shape
    dma = pltpu.SemaphoreType.DMA
    norm = NORM_TOKENS
    narrow = width // SPLIT
    pieces = norm // (rows_here * size)
    return pl.pallas_call(
        finish_kernel,
        out_shape=(
            jax.ShapeDtypeStruct((3, full, width), BF16),
            jax.ShapeDtypeStruct(x.shape, BF16),
            jax.ShapeDtypeStruct((SUBLANES, width), F32),
        ),
        in_specs=[IN_SMEM] + [ANY] * 13,
        out_specs=(ANY, ANY, ANY),
        scratch_shapes=[
            pltpu.VMEM((3, tokens, width), BF16),
            pltpu.VMEM((3, full, width), BF16),
            pltpu.VMEM((2, 2 * JOB_ROWS, tokens), BF16),
            pltpu.VMEM((MINE, JOB_ROWS, narrow), F32),
            pltpu.VMEM((2, JOB_ROWS, narrow), BF16),
            pltpu.VMEM((SHORT, JOB_ROWS, narrow), BF16),
            pltpu.VMEM((SHORT, QUARTER, narrow), BF16),
            pltpu.VMEM((RING, QUARTER, narrow), BF16),
            pltpu.VMEM((SHORT, 2 * QUARTER, narrow), BF16),
            pltpu.VMEM((LONG, 2 * QUARTER, narrow), BF16),
            pltpu.VMEM((SHORT, QUARTER, narrow), BF16),
            pltpu.VMEM((LONG, QUARTER, narrow), BF16),
            pltpu.VMEM((SHORT, QUARTER, narrow), BF16),
            pltpu.VMEM((RING, QUARTER, narrow), BF16),
            pltpu.VMEM((SHORT, QUARTER, narrow), BF16),
            pltpu.VMEM((RING, QUARTER, narrow), BF16),
            pltpu.VMEM((SHORT, QUARTER, narrow), BF16),
            pltpu.VMEM((RING, QUARTER, narrow), BF16),
            pltpu.VMEM((SHORT, 2, QUARTER, narrow), BF16),
            pltpu.VMEM((KEPT, norm, width), F32),
            pltpu.VMEM((KEPT, norm, width), BF16),
            pltpu.VMEM((RING, norm, width), BF16),
            pltpu.VMEM((norm, LANES), F32),
            pltpu.VMEM((2, norm // LANES, SUBLANES, LANES), F32),
            pltpu.VMEM((RING, norm // LANES, SUBLANES, LANES), F32),
            pltpu.VMEM((KEPT, pieces, rows_here, size, width), BF16),
            pltpu.VMEM((KEPT, norm, width), BF16),
            pltpu.VMEM((KEPT, norm, LANES), F32),
            pltpu.VMEM((KEPT, norm, LANES), F32),
            pltpu.VMEM((2, pieces, rows_here, size, width), BF16),
            pltpu.VMEM((2, SUBLANES, width), F32),
            pltpu.VMEM((rows_here, stretches * size, LANES), F32),
            pltpu.VMEM((AHEAD, 3, rows_here, HALF // 2, 2 * SUBLANES, LANES), BF16),
            pltpu.VMEM((AHEAD, rows_here, HALF) + TILE, F32),
            pltpu.VMEM((rows_here,) + TILE, F32),
            pltpu.VMEM((2,) + TILE, F32),
            pltpu.VMEM((SUBLANES, width), F32),
            pltpu.VMEM((2, SUBLANES, width), F32),
            pltpu.VMEM((4, SUBLANES, width), F32),
            pltpu.VMEM((1, width), F32),
            pltpu.VMEM((2,) + TILE, F32),
            pltpu.VMEM((2,) + TILE, F32),
            pltpu.VMEM((SUBLANES, width), F32),
            dma((4,)), dma((2, 2)), dma((2, AHEAD)),
            dma((2,)), dma((SHORT,)), dma((SHORT,)), dma((RING,)), dma((SHORT,)), dma((LONG,)),
            dma((SHORT,)), dma((LONG,)), dma((SHORT,)), dma((RING,)), dma((SHORT,)), dma((RING,)),
            dma((SHORT,)), dma((RING,)), dma((2, SHORT)),
            dma((2, LONG)), dma((2, LONG)), dma((LONG,)), dma((LONG,)), dma((LONG,)), dma((LONG,)),
            dma((LONG,)), dma((LONG,)), dma((LONG,)), dma((LONG,)),
            dma((KEPT,)), dma((RING,)), dma((2,)), dma((RING,)), dma((3 + pieces, KEPT)), dma((pieces, 2)),
            dma((5,)), dma((5,)), dma((5,)),
        ],
        compiler_params=pltpu.CompilerParams(
            collective_id=1, has_side_effects=True, vmem_limit_bytes=VMEM_LIMIT
        ),
        name="finish",
    )(
        lengths, saved, forgets, normed_t, reset, weight, x, mean, scale, passed, gain, forget_weight, reset_weight, sums
    )


COLLECT_PARTS = 4


def collect_kernel(
    total_ref, mixed_ref, input_grad_ref, final_ref, small_ref,
    weight_grad_ref, mixed_to, input_grad_to, final_out, gain_out, shift_out, forget_weight_out, reset_weight_out,
    forget_bias_out, reset_bias_out,
    narrow, wide, mixed, input_grad, final, small, vectors, in_sem, out_sem, pass_sem, small_sem, vector_sem,
):
    gates, full, _ = total_ref.shape
    rows = full // COLLECT_PARTS
    parts = [(gate, part) for gate in range(gates) for part in range(COLLECT_PARTS)]

    def take(index):
        gate, part = parts[index]
        here = pl.ds(part * rows, rows)
        return pltpu.make_async_copy(total_ref.at[gate, here], narrow.at[gate, here], in_sem.at[index])

    def give(index):
        gate, part = parts[index]
        here = pl.ds(part * rows, rows)
        return pltpu.make_async_copy(wide.at[gate, here], weight_grad_ref.at[gate, here], out_sem.at[index])

    passed = [
        (
            pltpu.make_async_copy(source, held, pass_sem.at[0, index]),
            pltpu.make_async_copy(held, target, pass_sem.at[1, index]),
        )
        for index, (source, held, target) in enumerate(
            ((mixed_ref, mixed, mixed_to), (input_grad_ref, input_grad, input_grad_to))
        )
    ]
    take_small = pltpu.make_async_copy(small_ref, small, small_sem.at[0])
    take_final = pltpu.make_async_copy(final_ref, final, small_sem.at[1])
    give_final = pltpu.make_async_copy(final, final_out, small_sem.at[2])
    outs = (forget_weight_out, reset_weight_out, forget_bias_out, reset_bias_out, gain_out, shift_out)
    give_vectors = [
        pltpu.make_async_copy(vectors.at[index], out, vector_sem.at[index]) for index, out in enumerate(outs)
    ]
    take_small.start()
    take_final.start()
    for index in range(len(parts)):
        take(index).start()
        if index == 1:
            passed[0][0].start()
        if index == 3:
            passed[1][0].start()
    take_small.wait()
    for index, copy in enumerate(give_vectors):
        vectors[index] = small[index:index + 1, :].reshape(TILE)
        copy.start()
    take_final.wait()
    give_final.start()
    for index, (gate, part) in enumerate(parts):
        take(index).wait()

        @pl.loop(0, rows // LANES)
        def _(step):
            here = pl.ds(aligned(part * rows + step * LANES, LANES), LANES)
            wide[gate, here, :] = narrow[gate, here, :].astype(F32)

        give(index).start()
        if index in (2, 4):
            copies = passed[index // 2 - 1]
            copies[0].wait()
            copies[1].start()
    for index in range(len(parts)):
        give(index).wait()
    for copies in passed:
        copies[1].wait()
    give_final.wait()
    for copy in give_vectors:
        copy.wait()


def collect(total, mixed, input_grad, final_state, small):
    shape = jax.ShapeDtypeStruct
    dma = pltpu.SemaphoreType.DMA
    parts = total.shape[0] * COLLECT_PARTS
    return pl.pallas_call(
        collect_kernel,
        out_shape=(
            shape(total.shape, F32), shape(mixed.shape, BF16), shape(input_grad.shape, BF16),
            shape(final_state.shape, F32),
        ) + (shape(TILE, F32),) * 6,
        in_specs=[ANY] * 5,
        out_specs=[ANY] * 10,
        scratch_shapes=[
            pltpu.VMEM(total.shape, BF16), pltpu.VMEM(total.shape, F32), pltpu.VMEM(mixed.shape, BF16),
            pltpu.VMEM(input_grad.shape, BF16), pltpu.VMEM(final_state.shape, F32), pltpu.VMEM(small.shape, F32),
            pltpu.VMEM((6,) + TILE, F32), dma((parts,)), dma((parts,)), dma((2, 2)), dma((3,)), dma((6,)),
        ],
        compiler_params=pltpu.CompilerParams(vmem_limit_bytes=VMEM_LIMIT),
        name="collect",
    )(total, mixed, input_grad, final_state, small)


def on_device(
    inputs, doc_lengths, layer_norm_gain, layer_norm_bias, weight, forget_weight, reset_weight, forget_bias,
    reset_bias, out_grad,
):
    rows_here, length, width = inputs.shape
    weights = jnp.transpose(weight, (1, 0, 2))
    stretched = (rows_here, length // STRETCH, STRETCH, width)
    x = inputs.reshape(stretched)
    gain = layer_norm_gain.reshape(1, width)
    vectors = [vector.reshape(TILE) for vector in (forget_weight, reset_weight, forget_bias, reset_bias)]
    saved, forgets, normed_t, mean, scale, mixed, passed, reset_grad, final_state, sums = project(
        doc_lengths, x, gain, layer_norm_bias.reshape(1, width), weights, out_grad.reshape(stretched), *vectors
    )
    weight_grad, input_grad, small = finish(
        doc_lengths, saved, forgets, normed_t, reset_grad, weights, x, mean, scale, passed, gain, vectors[0],
        vectors[1], sums,
    )
    weight_grad, mixed, input_grad, final_state, *vectors = collect(weight_grad, mixed, input_grad, final_state, small)
    devices = lax.axis_size("rows")
    groups = devices // 16
    if groups > 1:
        members = [[] for _ in range(devices // groups)]
        for device in range(devices):
            part, core = device // 2, device % 2
            members[(part // groups) * 2 + core].append(device)
        weight_grad, vectors = lax.psum((weight_grad, vectors), "rows", axis_index_groups=members)
    weight_grad = jnp.transpose(weight_grad, (1, 0, 2))
    return (
        mixed.reshape(inputs.shape), input_grad.reshape(inputs.shape), final_state, weight_grad,
        *[vector.reshape(width) for vector in vectors],
    )


def solution(mesh):
    rows_ch = P("rows", None, "ch")
    ch = P("ch")
    in_specs = (rows_ch, P("rows", None), ch, ch, P(None, None, "ch"), ch, ch, ch, ch, rows_ch)
    out_specs = (rows_ch, rows_ch, P("rows", "ch"), P(None, None, "ch"), ch, ch, ch, ch, ch, ch)
    return jax.shard_map(on_device, mesh=mesh, in_specs=in_specs, out_specs=out_specs, check_vma=False)
```
